32 devices in a mesh: grp: 2 (over x), dof: 16 (over z, y, core).
Axes of the slice: x: 2, y: 2, z: 4, core: 2. Of those that a mesh axis runs over, the one named last changes fastest.
Arguments:
- forces: bfloat16 [2, 4096, 12288], P('grp', None, 'dof'), parts along dimension 0, may hold values from -6 to 6
- mode_shapes: bfloat16 [12288, 448], P('dof'), may hold values from -0.1875 to 0.1875
- frf: bfloat16 [512, 2, 448, 448], P('dof'), may hold values from -5 to 5
Outputs:
- displaced: bfloat16 [2, 4096, 12288], P('grp', None, 'dof'), parts along dimension 0
The draws below stay inside these ranges and needn't reach their ends.
There are 2 independent parts, one for each index of `grp`. The reference program is written for one: setup_inputs(seed, part) draws one part's arguments, and reference() takes and returns one part's arrays. A program takes and returns all parts, laid end to end along the dimension named above; an argument that names none is the same for every part. Nothing has to cross between parts.
All inputs are finite; a program needn't handle non-finite values.
Results may differ from the reference program's by a relative error of at most 0.015.
Values may be sent and summed in bfloat16 or wider, within the bound.
No kernel may reach another device: no remote copies, remote signals or barrier semaphores. Data moves between devices by JAX's collectives and lax.ppermute only.
A program may use at most 192 MiB of HBM per device.

```python
import math
import jax
import jax.numpy as jnp
from jax import lax

DOFS = 12288
MODES = 448
STEPS = 4096
FREQS = 512
REALIZATIONS = 1


def draw_frf(key, part):
    key = jax.random.fold_in(key, 11)
    key_mag, key_ang, key_off = jax.random.split(key, 3)
    log_mag = jax.random.uniform(key_mag, (FREQS, MODES), jnp.float32, math.log(0.5), math.log(4.0))
    magnitude = jnp.exp(log_mag)
    phase = jax.random.uniform(key_ang, (FREQS, MODES), jnp.float32, -math.pi, math.pi)
    diag_pair = jnp.stack([magnitude * jnp.cos(phase), magnitude * jnp.sin(phase)], axis=1)
    identity = jnp.eye(MODES, dtype=jnp.float32)
    off_diag = jax.random.normal(key_off, (FREQS, 2, MODES, MODES), jnp.float32) * (0.5 / math.sqrt(MODES))
    whole = off_diag * (1.0 - identity) + diag_pair[:, :, :, None] * identity
    return jnp.clip(whole, -5.0, 5.0).astype(jnp.bfloat16)


def strengthened(entries, stream_key, source, target, shards_of, factor):
    owner, partner = [(jnp.arange(entries.shape[position]) // (entries.shape[position] // shards_of)).reshape([-1 if axis == position else 1 for axis in range(entries.ndim)]) for position in (source, target)]
    chosen = jax.random.permutation(stream_key, shards_of)[partner]
    strong = (owner == chosen) | (owner == (partner + shards_of // 2) % shards_of)
    return jnp.where(strong, factor * entries, entries)


def shard_levels(key, extent, pieces, low, top_value):
    factor_of = 1.0
    for dim, blocks in pieces:
        heights = jax.random.uniform(jax.random.fold_in(jax.random.fold_in(key, 6), dim), (blocks,), jnp.float32, low / len(pieces), top_value / len(pieces))
        factor_of = factor_of * jnp.repeat(jnp.exp(heights), extent[dim] // blocks).reshape((-1,) + (1,) * (len(extent) - 1 - dim))
    return factor_of


def scatter_about(key, extent, deviation, most, cuts=(), kind=jnp.bfloat16):
    gain = shard_levels(key, extent, cuts, -0.22, 0.18) if cuts else 1.0
    array = jax.random.normal(key, extent, jnp.float32) * deviation * gain
    return jnp.minimum(jnp.maximum(array, -most), most).astype(kind)


def gaussian_with(rng, dims, deviation, most, shards, heavy, kind=jnp.bfloat16):
    array = deviation * jax.random.normal(rng, dims, jnp.float32)
    if shards:
        array = array * shard_levels(rng, dims, shards, -0.22, 0.18)
    return jnp.clip(strengthened(array, jax.random.fold_in(rng, 3), *heavy), -most, most).astype(kind)


def setup_inputs(seed: int = 0, part: int = 0) -> dict:
    splits = jax.random.split(jax.random.key(seed), 4)
    part_splits = jax.random.split(jax.random.fold_in(splits[3], part), 4)
    return {
        "forces": scatter_about(part_splits[0], (REALIZATIONS, STEPS, DOFS), 1.0, 6.0, ((2, 16),)),
        "mode_shapes": gaussian_with(splits[1], (DOFS, MODES), 2048 ** -0.5, 0.1875, ((0, 16),), (0, 1, 16, 2.0)),
        "frf": draw_frf(jax.random.fold_in(splits[3], 71), part),
    }


def forward_table(steps, freqs):
    step_ids = jnp.arange(steps, dtype=jnp.int32)
    freq_ids = jnp.arange(freqs, dtype=jnp.int32)
    phase = step_ids[:, None] * freq_ids[None, :] % steps
    angle = phase.astype(jnp.float32) * (2.0 * math.pi / steps)
    table = jnp.stack([jnp.cos(angle), -jnp.sin(angle)], axis=1) * (1.0 / math.sqrt(steps))
    return table.astype(jnp.bfloat16)

def inverse_table(steps, freqs):
    step_ids = jnp.arange(steps, dtype=jnp.int32)
    freq_ids = jnp.arange(freqs, dtype=jnp.int32)
    phase = freq_ids[:, None] * step_ids[None, :] % steps
    angle = phase.astype(jnp.float32) * (2.0 * math.pi / steps)
    weights = jnp.where(freq_ids == 0, 0.5, 1.0).astype(jnp.float32)
    table = jnp.stack([jnp.cos(angle), -jnp.sin(angle)], axis=0) * weights[None, :, None]
    return (table * (2.0 / math.sqrt(steps))).astype(jnp.bfloat16)

def reference(forces, mode_shapes, frf):
    shapes32 = mode_shapes.astype(jnp.float32)
    modal_force = jnp.einsum('rtd,dm->mrt', forces.astype(jnp.float32), shapes32, precision=lax.Precision.HIGHEST)
    fwd = forward_table(STEPS, FREQS).astype(jnp.float32)
    modal_spec = jnp.einsum('mrt,tcf->frcm', modal_force, fwd, precision=lax.Precision.HIGHEST).astype(jnp.bfloat16)
    products = jnp.einsum('fanm,frbm->frabn', frf.astype(jnp.float32), modal_spec.astype(jnp.float32), precision=lax.Precision.HIGHEST)
    real_part = products[:, :, 0, 0] - products[:, :, 1, 1]
    imag_part = products[:, :, 0, 1] + products[:, :, 1, 0]
    response_spec = jnp.stack([real_part, imag_part], axis=2).astype(jnp.bfloat16)
    inv = inverse_table(STEPS, FREQS).astype(jnp.float32)
    modal_resp = jnp.einsum('frcm,cft->mrt', response_spec.astype(jnp.float32), inv, precision=lax.Precision.HIGHEST).astype(jnp.bfloat16)
    displaced = jnp.einsum('mrt,dm->rtd', modal_resp.astype(jnp.float32), shapes32, precision=lax.Precision.HIGHEST)
    return displaced.astype(jnp.bfloat16)
```

```python
import math

import jax
import jax.numpy as jnp
import numpy as np
from jax import lax
from jax.sharding import PartitionSpec as P

FREQS = 512


def half_tables(steps, devices):
    half = steps // 2
    freqs = np.arange(FREQS).reshape(devices, FREQS // devices // 2, 2)
    tables = []
    for parity in range(2):
        ids = freqs[:, :, parity].reshape(-1)
        phase = ids[:, None].astype(np.int64) * np.arange(half)[None, :] % steps
        angle = phase * (2.0 * math.pi / steps)
        table = np.stack([np.cos(angle), -np.sin(angle)], axis=1) / math.sqrt(steps)
        tables.append(table.reshape(FREQS, half))
    return np.stack(tables)


def inverse_scale(devices):
    scale = np.full((devices, 2, FREQS // devices // 2, 2, 1), 2.0, np.float32)
    scale[0, 0, 0] = 1.0
    return scale


def on_device(devices, forces, mode_shapes, frf):
    _, steps, dofs = forces.shape
    modes = mode_shapes.shape[1]
    half = steps // 2
    mine = FREQS // devices // 2
    table = jnp.asarray(half_tables(steps, devices).astype(jnp.bfloat16))
    low = forces[0, :half].astype(jnp.float32)
    high = forces[0, half:].astype(jnp.float32)
    folded = jnp.stack([low + high, low - high]).astype(jnp.bfloat16)
    spec = jnp.einsum("pft,ptd->pfd", table, folded, preferred_element_type=jnp.float32)
    partial = jnp.einsum(
        "pfd,dm->pfm", spec.astype(jnp.bfloat16), mode_shapes, preferred_element_type=jnp.float32
    )
    partial = partial.reshape(2, devices, 2 * mine, modes).transpose(1, 0, 2, 3)
    partial = partial.reshape(devices * 4 * mine, modes).astype(jnp.bfloat16)
    modal_spec = lax.psum_scatter(partial, "dof", scatter_dimension=0, tiled=True)
    modal_spec = modal_spec.reshape(2, mine, 2, modes).transpose(1, 0, 2, 3)
    modal_spec = modal_spec.reshape(2 * mine, 2, modes)
    products = jnp.einsum("fanm,fbm->fabn", frf, modal_spec, preferred_element_type=jnp.float32)
    real_part = products[:, 0, 0] - products[:, 1, 1]
    imag_part = products[:, 0, 1] + products[:, 1, 0]
    response = jnp.stack([real_part, imag_part], axis=1).astype(jnp.bfloat16)
    response = response.reshape(mine, 2, 2, modes).transpose(1, 0, 2, 3)
    response = response.reshape(4 * mine, modes)
    gathered = lax.all_gather(response, "dof", axis=0, tiled=True)
    gathered = gathered.reshape(devices, 2, mine, 2, modes).astype(jnp.float32)
    gathered = (gathered * inverse_scale(devices)).astype(jnp.bfloat16)
    gathered = gathered.transpose(1, 0, 2, 3, 4).reshape(2, FREQS, modes)
    moved = jnp.einsum("pfm,dm->pfd", gathered, mode_shapes, preferred_element_type=jnp.float32)
    waves = jnp.einsum(
        "pft,pfd->ptd", table, moved.astype(jnp.bfloat16), preferred_element_type=jnp.float32
    )
    out = jnp.concatenate([waves[0] + waves[1], waves[0] - waves[1]], axis=0)
    return out.astype(jnp.bfloat16)[None]


def solution(mesh):
    devices = mesh.shape["dof"]

    def run(forces, mode_shapes, frf):
        return on_device(devices, forces, mode_shapes, frf)

    return jax.shard_map(
        run,
        mesh=mesh,
        in_specs=(P("grp", None, "dof"), P("dof", None), P("dof", None, None, None)),
        out_specs=P("grp", None, "dof"),
        check_vma=False,
    )
```

```python
import functools
import math

import jax
import jax.numpy as jnp
import numpy as np
from jax import lax
from jax.experimental import pallas as pl
from jax.experimental.pallas import tpu as pltpu
from jax.sharding import PartitionSpec as P

FREQS = 512
CORES = 2
MIB = 1 << 20


def frequency_order(chips, parity):
    mine = FREQS // (chips * CORES)
    owned = np.arange(FREQS).reshape(chips, CORES, mine // 2, 2)
    return owned[:, :, :, parity].transpose(1, 0, 2).reshape(-1)


def forward_tables(steps, chips):
    times = np.arange(steps // 2, dtype=np.int64)
    tables = []
    for parity in range(2):
        ids = frequency_order(chips, parity)
        angle = (ids[:, None] * times[None, :] % steps) * (2.0 * math.pi / steps)
        table = np.stack([np.cos(angle), -np.sin(angle)], axis=1) / math.sqrt(steps)
        tables.append(table.reshape(FREQS, steps // 2))
    return np.stack(tables)


def inverse_tables(steps, chips):
    tables = forward_tables(steps, chips) * 2.0
    for parity in range(2):
        weights = np.where(frequency_order(chips, parity) == 0, 0.5, 1.0)
        tables[parity] *= np.repeat(weights, 2)[:, None]
    return tables.transpose(0, 2, 1)


def forward_kernel(core_ref, table_ref, forces_ref, shapes_ref, keep_ref, send_ref, acc_ref):
    step = pl.program_id(0)
    chips, _, rows, modes = keep_ref.shape
    low, high = forces_ref[0], forces_ref[1]

    @pl.when(step == 0)
    def _():
        acc_ref[...] = jnp.zeros_like(acc_ref)

    for parity, folded in enumerate((low + high, low - high)):
        acc_ref[parity] += jnp.dot(table_ref[parity], folded, preferred_element_type=jnp.float32)

    @pl.when(step == pl.num_programs(0) - 1)
    def _():
        first = core_ref[0] == 0
        for parity in range(2):
            spec = lax.dot_general(
                acc_ref[parity].astype(jnp.bfloat16),
                shapes_ref[...],
                (((1,), (1,)), ((), ())),
                preferred_element_type=jnp.float32,
            ).reshape(CORES, chips, rows, modes)
            keep_ref[:, parity] = jnp.where(first, spec[0], spec[1]).astype(jnp.bfloat16)
            send_ref[:, parity] = jnp.where(first, spec[1], spec[0]).astype(jnp.bfloat16)


def forward(core, table, forces, shapes_t, chips):
    _, half, dofs = forces.shape
    modes = shapes_t.shape[0]
    block = 512
    rows = FREQS // (chips * CORES)
    out = jax.ShapeDtypeStruct((chips, 2, rows, modes), jnp.bfloat16)
    whole = pl.BlockSpec((chips, 2, rows, modes), lambda i: (0, 0, 0, 0))
    return pl.pallas_call(
        forward_kernel,
        grid=(half // block,),
        in_specs=[
            pl.BlockSpec(memory_space=pltpu.SMEM),
            pl.BlockSpec((2, FREQS, block), lambda i: (0, 0, i)),
            pl.BlockSpec((2, block, dofs), lambda i: (0, i, 0)),
            pl.BlockSpec((modes, dofs), lambda i: (0, 0)),
        ],
        out_specs=[whole, whole],
        out_shape=[out, out],
        scratch_shapes=[pltpu.VMEM((2, FREQS, dofs), jnp.float32)],
        compiler_params=pltpu.CompilerParams(vmem_limit_bytes=32 * MIB),
        cost_estimate=pl.CostEstimate(
            flops=4 * FREQS * dofs * (half + modes), bytes_accessed=12 * MIB, transcendentals=0
        ),
        name="forward",
    )(core, table, forces, shapes_t)


def respond_kernel(pieces_ref, frf_ref, out_ref, direct_ref, turned_ref, acc_ref):
    step = pl.program_id(0)
    _, rows, modes = out_ref.shape
    each = frf_ref.shape[0]

    @pl.when(step == 0)
    def _():
        total = jnp.sum(pieces_ref[...].astype(jnp.float32), axis=0).reshape(2 * rows, modes)
        total = total.astype(jnp.bfloat16).astype(jnp.float32)
        row = lax.broadcasted_iota(jnp.int32, total.shape, 0)
        turned = jnp.where(
            row % 2 == 0, -jnp.roll(total, -1, axis=0), jnp.roll(total, 1, axis=0)
        )
        direct_ref[...] = total.T.astype(jnp.bfloat16)
        turned_ref[...] = turned.T.astype(jnp.bfloat16)
        acc_ref[...] = jnp.zeros_like(acc_ref)

    real = frf_ref[:, 0].reshape(each * modes, modes)
    imag = frf_ref[:, 1].reshape(each * modes, modes)
    products = jnp.dot(real, direct_ref[...], preferred_element_type=jnp.float32)
    products += jnp.dot(imag, turned_ref[...], preferred_element_type=jnp.float32)
    products = products.reshape(each, modes, 2 * rows)
    pair = lax.broadcasted_iota(jnp.int32, (modes, 2 * rows), 1) // 2
    acc = acc_ref[...]
    for i in range(each):
        f = step * each + i
        acc = jnp.where(pair == (f % 2) * (rows // 2) + f // 2, products[i], acc)
    acc_ref[...] = acc

    @pl.when(step == pl.num_programs(0) - 1)
    def _():
        out_ref[...] = acc_ref[...].T.reshape(2, rows, modes).astype(jnp.bfloat16)


def respond(pieces, frf):
    mine, _, modes, _ = frf.shape
    rows = mine
    each = 4
    return pl.pallas_call(
        respond_kernel,
        grid=(mine // each,),
        in_specs=[
            pl.BlockSpec(pieces.shape, lambda i: (0, 0, 0, 0)),
            pl.BlockSpec((each, 2, modes, modes), lambda i: (i, 0, 0, 0)),
        ],
        out_specs=pl.BlockSpec((2, rows, modes), lambda i: (0, 0, 0)),
        out_shape=jax.ShapeDtypeStruct((2, rows, modes), jnp.bfloat16),
        scratch_shapes=[
            pltpu.VMEM((modes, 2 * rows), jnp.bfloat16),
            pltpu.VMEM((modes, 2 * rows), jnp.bfloat16),
            pltpu.VMEM((modes, 2 * rows), jnp.float32),
        ],
        compiler_params=pltpu.CompilerParams(vmem_limit_bytes=24 * MIB),
        cost_estimate=pl.CostEstimate(
            flops=8 * mine * modes * modes, bytes_accessed=frf.size * 2, transcendentals=0
        ),
        name="respond",
    )(pieces, frf)


def inverse_kernel(chips, place_ref, table_ref, shapes_ref, *refs):
    shards, (out_ref, order_ref, moved_ref) = refs[: CORES * chips], refs[CORES * chips :]
    _, rows, modes = shards[0].shape

    @pl.when(pl.program_id(0) == 0)
    def _():
        core, chip = place_ref[0], place_ref[1]
        for far in range(CORES):
            for k in range(chips):
                values = shards[far * chips + k][...]
                for parity in range(2):
                    order_ref[parity, core ^ far, chip ^ k] = values[parity].astype(jnp.float32)
        for parity in range(2):
            moved_ref[parity] = jnp.dot(
                order_ref[parity].reshape(FREQS, modes).astype(jnp.bfloat16),
                shapes_ref[...],
                preferred_element_type=jnp.float32,
            ).astype(jnp.bfloat16)

    even = jnp.dot(table_ref[0], moved_ref[0], preferred_element_type=jnp.float32)
    odd = jnp.dot(table_ref[1], moved_ref[1], preferred_element_type=jnp.float32)
    out_ref[0] = (even + odd).astype(jnp.bfloat16)
    out_ref[1] = (even - odd).astype(jnp.bfloat16)


def inverse(place, table, shapes_t, shards, chips):
    _, half, _ = table.shape
    modes, dofs = shapes_t.shape
    block = 256
    rows = shards[0].shape[1]
    return pl.pallas_call(
        functools.partial(inverse_kernel, chips),
        grid=(half // block,),
        in_specs=[
            pl.BlockSpec(memory_space=pltpu.SMEM),
            pl.BlockSpec((2, block, FREQS), lambda i: (0, i, 0)),
            pl.BlockSpec((modes, dofs), lambda i: (0, 0)),
        ]
        + [pl.BlockSpec((2, rows, modes), lambda i: (0, 0, 0))] * len(shards),
        out_specs=pl.BlockSpec((2, block, dofs), lambda i: (0, i, 0)),
        out_shape=jax.ShapeDtypeStruct((2, half, dofs), jnp.bfloat16),
        scratch_shapes=[
            pltpu.VMEM((2, CORES, chips, rows, modes), jnp.float32),
            pltpu.VMEM((2, FREQS, dofs), jnp.bfloat16),
        ],
        compiler_params=pltpu.CompilerParams(vmem_limit_bytes=32 * MIB),
        cost_estimate=pl.CostEstimate(
            flops=4 * FREQS * dofs * (half + modes), bytes_accessed=12 * MIB, transcendentals=0
        ),
        name="inverse",
    )(place, table, shapes_t, *shards)


def on_device(devices, forces, mode_shapes, frf):
    _, steps, dofs = forces.shape
    half = steps // 2
    chips = devices // CORES
    to_core = [(i, i ^ 1) for i in range(devices)]
    to_chip = [[(i, i ^ (CORES * k)) for i in range(devices)] for k in range(chips)]
    same_core = [[chip * CORES + core for chip in range(chips)] for core in range(CORES)]
    index = lax.axis_index("dof")
    place = jnp.stack([index % CORES, index // CORES]).astype(jnp.int32)
    shapes_t = mode_shapes.T
    fwd = jnp.asarray(forward_tables(steps, chips).astype(jnp.bfloat16))
    inv = jnp.asarray(inverse_tables(steps, chips).astype(jnp.bfloat16))

    keep, send = forward(place, fwd, forces.reshape(2, half, dofs), shapes_t, chips)
    came = lax.ppermute(send, "dof", to_core)
    pair = (keep.astype(jnp.float32) + came.astype(jnp.float32)).astype(jnp.bfloat16)
    pieces = lax.all_to_all(
        pair, "dof", split_axis=0, concat_axis=0, axis_index_groups=same_core, tiled=True
    )
    response = respond(pieces, frf)
    near = [response] + [lax.ppermute(response, "dof", to_chip[k]) for k in range(1, chips)]
    far = [lax.ppermute(shard, "dof", to_core) for shard in near]
    out = inverse(place, inv, shapes_t, near + far, chips)
    return out.reshape(1, steps, dofs)


def solution(mesh):
    devices = mesh.shape["dof"]
    return jax.shard_map(
        functools.partial(on_device, devices),
        mesh=mesh,
        in_specs=(P("grp", None, "dof"), P("dof", None), P("dof", None, None, None)),
        out_specs=P("grp", None, "dof"),
        check_vma=False,
    )
```

```python
import functools
import math

import jax
import jax.numpy as jnp
import numpy as np
from jax import lax
from jax.experimental import pallas as pl
from jax.experimental.pallas import tpu as pltpu
from jax.sharding import PartitionSpec as P

FREQS = 512
CORES = 2
MIB = 1 << 20


def frequency_order(chips, parity):
    mine = FREQS // (chips * CORES)
    owned = np.arange(FREQS).reshape(chips, CORES, mine // 2, 2)
    return owned[:, :, :, parity].transpose(1, 0, 2).reshape(-1)


def forward_tables(steps, chips):
    times = np.arange(steps // 2, dtype=np.int64)
    tables = []
    for parity in range(2):
        ids = frequency_order(chips, parity)
        angle = (ids[:, None] * times[None, :] % steps) * (2.0 * math.pi / steps)
        table = np.stack([np.cos(angle), -np.sin(angle)], axis=1) / math.sqrt(steps)
        tables.append(table.reshape(FREQS, steps // 2))
    return np.stack(tables)


def inverse_tables(steps, chips):
    tables = forward_tables(steps, chips) * 2.0
    for parity in range(2):
        weights = np.where(frequency_order(chips, parity) == 0, 0.5, 1.0)
        tables[parity] *= np.repeat(weights, 2)[:, None]
    return tables.transpose(0, 2, 1)


def chunk_list(half):
    unit = half // 8
    sizes = (unit, unit, 2 * unit, 4 * unit)
    starts = (0, unit, 2 * unit, 4 * unit)
    return tuple(zip(starts, sizes))


def forward_kernel(
    place_ref, table_ref, forces_ref, shapes_ref, frf_ref, keep_ref, send_ref, held_ref,
    table_buf, forces_buf, shapes_buf, acc_ref, table_sem, forces_sem, shapes_sem, held_sem,
):
    _, zs, _, rows, modes = keep_ref.shape
    chips = 2 * zs
    chunks = chunk_list(forces_ref.shape[1])
    copies = []
    for n, (start, size) in enumerate(chunks):
        part = pl.ds(start, size)
        pair = (
            pltpu.make_async_copy(
                forces_ref.at[:, part], forces_buf.at[:, part], forces_sem.at[n]
            ),
            pltpu.make_async_copy(
                table_ref.at[:, :, part], table_buf.at[:, :, part], table_sem.at[n]
            ),
        )
        for copy in pair:
            copy.start()
        copies.append(pair)
    shapes_copy = pltpu.make_async_copy(shapes_ref, shapes_buf, shapes_sem)
    shapes_copy.start()
    held_copy = pltpu.make_async_copy(
        frf_ref.at[pl.ds(0, held_ref.shape[0])], held_ref, held_sem
    )
    held_copy.start()

    for n, (start, size) in enumerate(chunks):
        for copy in copies[n]:
            copy.wait()
        low = forces_buf[0, start : start + size]
        high = forces_buf[1, start : start + size]
        for parity, folded in enumerate((low + high, low - high)):
            part = jnp.dot(
                table_buf[parity, :, start : start + size],
                folded,
                preferred_element_type=jnp.float32,
            )
            if n == 0:
                acc_ref[parity] = part
            else:
                acc_ref[parity] += part

    shapes_copy.wait()
    first, chip = place_ref[0] == 0, place_ref[1]
    for parity in range(2):
        spec = lax.dot_general(
            acc_ref[parity].astype(jnp.bfloat16),
            shapes_buf[...],
            (((1,), (1,)), ((), ())),
            preferred_element_type=jnp.float32,
        ).reshape(CORES, chips, rows, modes)
        keep = jnp.where(first, spec[0], spec[1]).astype(jnp.bfloat16)
        send = jnp.where(first, spec[1], spec[0]).astype(jnp.bfloat16)
        for j in range(chips):
            slot = chip ^ j
            keep_ref[slot % 2, slot // 2, parity] = keep[j]
            send_ref[slot % 2, slot // 2, parity] = send[j]
    held_copy.wait()


def in_hbm(array):
    return pltpu.with_memory_space_constraint(array, pltpu.HBM)


def forward(place, table, forces, shapes_t, frf, held, chips):
    _, half, dofs = forces.shape
    modes = shapes_t.shape[0]
    rows = FREQS // (chips * CORES)
    out = jax.ShapeDtypeStruct((2, chips // 2, 2, rows, modes), jnp.bfloat16)
    vmem, hbm = pl.BlockSpec(memory_space=pltpu.VMEM), pl.BlockSpec(memory_space=pltpu.HBM)
    count = len(chunk_list(half))
    return pl.pallas_call(
        forward_kernel,
        in_specs=[pl.BlockSpec(memory_space=pltpu.SMEM), hbm, hbm, hbm, hbm],
        out_specs=[vmem, vmem, vmem],
        out_shape=[out, out, pltpu.VMEM((held,) + frf.shape[1:], jnp.bfloat16)],
        scratch_shapes=[
            pltpu.VMEM(table.shape, jnp.bfloat16),
            pltpu.VMEM(forces.shape, jnp.bfloat16),
            pltpu.VMEM(shapes_t.shape, jnp.bfloat16),
            pltpu.VMEM((2, FREQS, dofs), jnp.float32),
            pltpu.SemaphoreType.DMA((count,)),
            pltpu.SemaphoreType.DMA((count,)),
            pltpu.SemaphoreType.DMA,
            pltpu.SemaphoreType.DMA,
        ],
        compiler_params=pltpu.CompilerParams(vmem_limit_bytes=24 * MIB),
        cost_estimate=pl.CostEstimate(
            flops=4 * FREQS * dofs * (half + modes), bytes_accessed=20 * MIB, transcendentals=0
        ),
        name="forward",
    )(place, in_hbm(table), in_hbm(forces), in_hbm(shapes_t), in_hbm(frf))


def load_kernel(start, frf_ref, after_ref, held_ref, sem):
    copy = pltpu.make_async_copy(
        frf_ref.at[pl.ds(start, held_ref.shape[0])], held_ref, sem
    )
    copy.start()
    copy.wait()


def load(frf, start, size, after):
    hbm, anywhere = pl.BlockSpec(memory_space=pltpu.HBM), pl.BlockSpec(memory_space=pl.ANY)
    return pl.pallas_call(
        functools.partial(load_kernel, start),
        in_specs=[hbm, anywhere],
        out_specs=pl.BlockSpec(memory_space=pltpu.VMEM),
        out_shape=pltpu.VMEM((size,) + frf.shape[1:], jnp.bfloat16),
        scratch_shapes=[pltpu.SemaphoreType.DMA],
        compiler_params=pltpu.CompilerParams(vmem_limit_bytes=2 * MIB),
        cost_estimate=pl.CostEstimate(
            flops=0, bytes_accessed=4 * size * math.prod(frf.shape[1:]), transcendentals=0
        ),
        name="load",
    )(in_hbm(frf), after)


def respond_kernel(count, *refs):
    pieces, parts = refs[:count], refs[count:-4]
    out_ref, direct_ref, turned_ref, acc_ref = refs[-4:]
    _, rows, modes = out_ref.shape
    total = sum(piece[...].astype(jnp.float32) for piece in pieces).reshape(2 * rows, modes)
    total = total.astype(jnp.bfloat16).astype(jnp.float32)
    row = lax.broadcasted_iota(jnp.int32, total.shape, 0)
    turned = jnp.where(row % 2 == 0, -jnp.roll(total, -1, axis=0), jnp.roll(total, 1, axis=0))
    direct_ref[...] = total.T.astype(jnp.bfloat16)
    turned_ref[...] = turned.T.astype(jnp.bfloat16)
    acc_ref[...] = jnp.zeros_like(acc_ref)
    each = math.gcd(4, *(part.shape[0] for part in parts))
    pair = lax.broadcasted_iota(jnp.int32, (modes, 2 * rows), 1) // 2
    base = 0
    for part in parts:

        @pl.loop(0, part.shape[0] // each)
        def _(step, part=part, base=base):
            block = part.at[pl.ds(step * each, each)]
            real = block[:, 0].reshape(each * modes, modes)
            imag = block[:, 1].reshape(each * modes, modes)
            products = jnp.dot(real, direct_ref[...], preferred_element_type=jnp.float32)
            products += jnp.dot(imag, turned_ref[...], preferred_element_type=jnp.float32)
            products = products.reshape(each, modes, 2 * rows)
            acc = acc_ref[...]
            for i in range(each):
                f = base + step * each + i
                acc = jnp.where(pair == (f % 2) * (rows // 2) + f // 2, products[i], acc)
            acc_ref[...] = acc

        base += part.shape[0]

    out_ref[...] = acc_ref[...].T.reshape(2, rows, modes).astype(jnp.bfloat16)


def respond(pieces, parts):
    rows, modes = pieces[0].shape[1:]
    vmem = pl.BlockSpec(memory_space=pltpu.VMEM)
    size = sum(part.size for part in parts)
    return pl.pallas_call(
        functools.partial(respond_kernel, len(pieces)),
        in_specs=[vmem] * (len(pieces) + len(parts)),
        out_specs=vmem,
        out_shape=jax.ShapeDtypeStruct((2, rows, modes), jnp.bfloat16),
        scratch_shapes=[
            pltpu.VMEM((modes, 2 * rows), jnp.bfloat16),
            pltpu.VMEM((modes, 2 * rows), jnp.bfloat16),
            pltpu.VMEM((modes, 2 * rows), jnp.float32),
        ],
        compiler_params=pltpu.CompilerParams(vmem_limit_bytes=12 * MIB),
        cost_estimate=pl.CostEstimate(flops=4 * size, bytes_accessed=2 * size, transcendentals=0),
        name="respond",
    )(*pieces, *parts)


def inverse_kernel(
    place_ref, table_ref, shapes_ref, own_ref, across_ref, twin_ref, twin_across_ref,
    out_ref, order_ref, moved_ref, out_buf, out_sem,
):
    zs, _, rows, modes = own_ref.shape
    half, block = out_ref.shape[1], out_buf.shape[2]
    core, chip = place_ref[0], place_ref[1]
    for far, near_y in enumerate(((own_ref, across_ref), (twin_ref, twin_across_ref))):
        for rel_y, shard_ref in enumerate(near_y):
            for k in range(zs):
                for parity in range(2):
                    order_ref[parity, core ^ far, chip ^ (2 * k + rel_y)] = shard_ref[
                        k, parity
                    ].astype(jnp.float32)
    for parity in range(2):
        moved_ref[parity] = jnp.dot(
            order_ref[parity].reshape(FREQS, modes).astype(jnp.bfloat16),
            shapes_ref[...],
            preferred_element_type=jnp.float32,
        ).astype(jnp.bfloat16)

    def copy_out(step, slot):
        return pltpu.make_async_copy(
            out_buf.at[slot], out_ref.at[:, pl.ds(step * block, block)], out_sem.at[slot]
        )

    for step in range(half // block):
        slot = step % 2
        part = slice(step * block, (step + 1) * block)
        even = jnp.dot(table_ref[0, part], moved_ref[0], preferred_element_type=jnp.float32)
        odd = jnp.dot(table_ref[1, part], moved_ref[1], preferred_element_type=jnp.float32)
        if step >= 2:
            copy_out(step - 2, slot).wait()
        out_buf[slot, 0] = (even + odd).astype(jnp.bfloat16)
        out_buf[slot, 1] = (even - odd).astype(jnp.bfloat16)
        copy_out(step, slot).start()
    for step in range(half // block - 2, half // block):
        copy_out(step, step % 2).wait()


def inverse(place, table, shapes_t, shards, chips):
    _, half, _ = table.shape
    modes, dofs = shapes_t.shape
    block = 512
    rows = shards[0].shape[2]
    vmem = pl.BlockSpec(memory_space=pltpu.VMEM)
    return pl.pallas_call(
        inverse_kernel,
        in_specs=[pl.BlockSpec(memory_space=pltpu.SMEM)] + [vmem] * 6,
        out_specs=pl.BlockSpec(memory_space=pltpu.HBM),
        out_shape=jax.ShapeDtypeStruct((2, half, dofs), jnp.bfloat16),
        scratch_shapes=[
            pltpu.VMEM((2, CORES, chips, rows, modes), jnp.float32),
            pltpu.VMEM((2, FREQS, dofs), jnp.bfloat16),
            pltpu.VMEM((2, 2, block, dofs), jnp.bfloat16),
            pltpu.SemaphoreType.DMA((2,)),
        ],
        compiler_params=pltpu.CompilerParams(vmem_limit_bytes=24 * MIB),
        cost_estimate=pl.CostEstimate(
            flops=4 * FREQS * dofs * (half + modes), bytes_accessed=12 * MIB, transcendentals=0
        ),
        name="inverse",
    )(place, table, shapes_t, *shards)


def add_kernel(ours_ref, came_ref, after_ref, *out_refs):
    for n, out_ref in enumerate(out_refs):
        total = ours_ref[n].astype(jnp.float32) + came_ref[n].astype(jnp.float32)
        out_ref[...] = total.astype(jnp.bfloat16)


def add(ours, came, after):
    vmem, anywhere = pl.BlockSpec(memory_space=pltpu.VMEM), pl.BlockSpec(memory_space=pl.ANY)
    return pl.pallas_call(
        add_kernel,
        in_specs=[vmem, vmem, anywhere],
        out_specs=[vmem] * ours.shape[0],
        out_shape=[jax.ShapeDtypeStruct(ours.shape[1:], jnp.bfloat16)] * ours.shape[0],
        compiler_params=pltpu.CompilerParams(vmem_limit_bytes=8 * MIB),
        cost_estimate=pl.CostEstimate(
            flops=ours.size, bytes_accessed=6 * ours.size, transcendentals=0
        ),
        name="add",
    )(ours, came, after)


def on_device(devices, forces, mode_shapes, frf):
    _, steps, dofs = forces.shape
    half = steps // 2
    chips = devices // CORES
    zs = chips // 2

    def swap(values, distance):
        pairs = [(i, i ^ distance) for i in range(devices)]
        return lax.ppermute(values, "dof", pairs)

    index = lax.axis_index("dof")
    place = jnp.stack([index % CORES, index // CORES]).astype(jnp.int32)
    shapes_t = mode_shapes.T
    fwd = jnp.asarray(forward_tables(steps, chips).astype(jnp.bfloat16))
    inv = jnp.asarray(inverse_tables(steps, chips).astype(jnp.bfloat16))

    mine = frf.shape[0]
    first, second = mine // 4, 3 * mine // 8
    keep, send, part0 = forward(
        place, fwd, forces.reshape(2, half, dofs), shapes_t, frf, first, chips
    )
    here, there = add(keep, swap(send, 1), send)
    part1 = load(frf, first, second, there)
    pieces = add(here, swap(there, 2), part1)
    part2 = load(frf, first + second, mine - first - second, pieces[0])
    pieces = [pieces[0]] + [swap(pieces[k], 4 * k) for k in range(1, zs)]
    response = respond(pieces, (part0, part1, part2))
    own = jnp.stack([response] + [swap(response, 4 * k) for k in range(1, zs)])
    across = swap(own, 2)
    twin = swap(own, 1)
    twin_across = swap(across, 1)
    out = inverse(place, inv, shapes_t, (own, across, twin, twin_across), chips)
    return out.reshape(1, steps, dofs)


def solution(mesh):
    devices = mesh.shape["dof"]
    return jax.shard_map(
        functools.partial(on_device, devices),
        mesh=mesh,
        in_specs=(P("grp", None, "dof"), P("dof", None), P("dof", None, None, None)),
        out_specs=P("grp", None, "dof"),
        check_vma=False,
    )
```

```python
import functools
import math

import jax
import jax.numpy as jnp
import numpy as np
from jax import lax
from jax.experimental import pallas as pl
from jax.experimental.pallas import tpu as pltpu
from jax.sharding import PartitionSpec as P

FREQS = 512
CORES = 2
MIB = 1 << 20


def frequency_order(chips, parity):
    mine = FREQS // (chips * CORES)
    owned = np.arange(FREQS).reshape(chips // 2, 2, CORES, mine // 2, 2)
    return owned[..., parity].transpose(1, 2, 0, 3).reshape(-1)


def forward_tables(steps, chips):
    times = np.arange(steps // 2, dtype=np.int64)
    tables = []
    for parity in range(2):
        ids = frequency_order(chips, parity)
        angle = (ids[:, None] * times[None, :] % steps) * (2.0 * math.pi / steps)
        table = np.stack([np.cos(angle), -np.sin(angle)], axis=1) / math.sqrt(steps)
        tables.append(table.reshape(FREQS, steps // 2))
    return np.stack(tables)


def inverse_tables(steps, chips):
    tables = forward_tables(steps, chips) * 2.0
    for parity in range(2):
        weights = np.where(frequency_order(chips, parity) == 0, 0.5, 1.0)
        tables[parity] *= np.repeat(weights, 2)[:, None]
    return tables.reshape(2, 2, FREQS // 2, steps // 2).transpose(0, 1, 3, 2)


def chunk_list(half):
    unit = half // 8
    sizes = (unit, unit, 2 * unit, 4 * unit)
    starts = (0, unit, 2 * unit, 4 * unit)
    return tuple(zip(starts, sizes))


def forward_kernel(
    place_ref, table_ref, forces_ref, shapes_ref, frf_ref, keep_ref, send_ref, held_ref,
    table_buf, forces_buf, shapes_buf, acc_ref, table_sem, forces_sem, shapes_sem, held_sem,
):
    _, zs, _, rows, modes = keep_ref.shape
    chunks = chunk_list(forces_ref.shape[1])
    copies = []
    for n, (start, size) in enumerate(chunks):
        part = pl.ds(start, size)
        pair = (
            pltpu.make_async_copy(
                forces_ref.at[:, part], forces_buf.at[:, part], forces_sem.at[n]
            ),
            pltpu.make_async_copy(
                table_ref.at[:, :, part], table_buf.at[:, :, part], table_sem.at[n]
            ),
        )
        for copy in pair:
            copy.start()
        copies.append(pair)
    shapes_copy = pltpu.make_async_copy(shapes_ref, shapes_buf, shapes_sem)
    shapes_copy.start()
    held_copy = pltpu.make_async_copy(
        frf_ref.at[pl.ds(0, held_ref.shape[0])], held_ref, held_sem
    )
    held_copy.start()

    for n, (start, size) in enumerate(chunks):
        for copy in copies[n]:
            copy.wait()
        low = forces_buf[0, start : start + size]
        high = forces_buf[1, start : start + size]
        for parity, folded in enumerate((low + high, low - high)):
            part = jnp.dot(
                table_buf[parity, :, start : start + size],
                folded,
                preferred_element_type=jnp.float32,
            )
            if n == 0:
                acc_ref[parity] = part
            else:
                acc_ref[parity] += part

    shapes_copy.wait()
    first, chip = place_ref[0] == 0, place_ref[1]
    for parity in range(2):
        spec = lax.dot_general(
            acc_ref[parity].astype(jnp.bfloat16),
            shapes_buf[...],
            (((1,), (1,)), ((), ())),
            preferred_element_type=jnp.float32,
        ).reshape(2, CORES, zs, rows, modes)
        for y in range(2):
            keep = jnp.where(first, spec[y, 0], spec[y, 1]).astype(jnp.bfloat16)
            send = jnp.where(first, spec[y, 1], spec[y, 0]).astype(jnp.bfloat16)
            for z in range(zs):
                slot = chip ^ (2 * z + y)
                keep_ref[slot % 2, slot // 2, parity] = keep[z]
                send_ref[slot % 2, slot // 2, parity] = send[z]
    held_copy.wait()


def in_hbm(array):
    return pltpu.with_memory_space_constraint(array, pltpu.HBM)


def forward(place, table, forces, shapes_t, frf, held, chips):
    _, half, dofs = forces.shape
    modes = shapes_t.shape[0]
    rows = FREQS // (chips * CORES)
    out = jax.ShapeDtypeStruct((2, chips // 2, 2, rows, modes), jnp.bfloat16)
    vmem, hbm = pl.BlockSpec(memory_space=pltpu.VMEM), pl.BlockSpec(memory_space=pltpu.HBM)
    count = len(chunk_list(half))
    return pl.pallas_call(
        forward_kernel,
        in_specs=[pl.BlockSpec(memory_space=pltpu.SMEM), hbm, hbm, hbm, hbm],
        out_specs=[vmem, vmem, vmem],
        out_shape=[out, out, pltpu.VMEM((held,) + frf.shape[1:], jnp.bfloat16)],
        scratch_shapes=[
            pltpu.VMEM(table.shape, jnp.bfloat16),
            pltpu.VMEM(forces.shape, jnp.bfloat16),
            pltpu.VMEM(shapes_t.shape, jnp.bfloat16),
            pltpu.VMEM((2, FREQS, dofs), jnp.float32),
            pltpu.SemaphoreType.DMA((count,)),
            pltpu.SemaphoreType.DMA((count,)),
            pltpu.SemaphoreType.DMA,
            pltpu.SemaphoreType.DMA,
        ],
        compiler_params=pltpu.CompilerParams(vmem_limit_bytes=24 * MIB),
        cost_estimate=pl.CostEstimate(
            flops=4 * FREQS * dofs * (half + modes), bytes_accessed=20 * MIB, transcendentals=0
        ),
        name="forward",
    )(place, in_hbm(table), in_hbm(forces), in_hbm(shapes_t), in_hbm(frf))


def load_copies(start, frf_ref, held_ref, sem):
    count = sem.shape[0]
    size = held_ref.shape[0] // count
    return [
        pltpu.make_async_copy(
            frf_ref.at[pl.ds(start + n * size, size)],
            held_ref.at[pl.ds(n * size, size)],
            sem.at[n],
        )
        for n in range(count)
    ]


def load_kernel(start, frf_ref, after_ref, held_ref, sem):
    copies = load_copies(start, frf_ref, held_ref, sem)
    for copy in copies:
        copy.start()
    for copy in copies:
        copy.wait()


def load(frf, start, size, after):
    hbm, anywhere = pl.BlockSpec(memory_space=pltpu.HBM), pl.BlockSpec(memory_space=pl.ANY)
    return pl.pallas_call(
        functools.partial(load_kernel, start),
        in_specs=[hbm, anywhere],
        out_specs=pl.BlockSpec(memory_space=pltpu.VMEM),
        out_shape=pltpu.VMEM((size,) + frf.shape[1:], jnp.bfloat16),
        scratch_shapes=[pltpu.SemaphoreType.DMA((math.gcd(size, 4),))],
        compiler_params=pltpu.CompilerParams(vmem_limit_bytes=2 * MIB),
        cost_estimate=pl.CostEstimate(
            flops=0, bytes_accessed=4 * size * math.prod(frf.shape[1:]), transcendentals=0
        ),
        name="load",
    )(in_hbm(frf), after)


def respond_kernel(count, *refs):
    pieces, parts = refs[:count], refs[count:-4]
    out_ref, direct_ref, turned_ref, result_ref = refs[-4:]
    _, rows, modes = out_ref.shape
    total = sum(piece[0].astype(jnp.float32) for piece in pieces).reshape(2 * rows, modes)
    total = total.astype(jnp.bfloat16).astype(jnp.float32)
    row = lax.broadcasted_iota(jnp.int32, total.shape, 0)
    turned = jnp.where(row % 2 == 0, -jnp.roll(total, -1, axis=0), jnp.roll(total, 1, axis=0))

    def place(f):
        return (f % 2) * rows + f // 2 * 2

    direct_ref[...] = jnp.zeros_like(direct_ref)
    turned_ref[...] = jnp.zeros_like(turned_ref)
    for f in range(rows):
        at = place(f)
        direct_ref[f, 0:2] = total[at : at + 2]
        turned_ref[f, 0:2] = turned[at : at + 2]
    base = 0
    for part in parts:

        @pl.loop(0, part.shape[0], unroll=math.gcd(4, part.shape[0]))
        def _(step, part=part, base=base):
            f = base + step
            products = [
                lax.dot_general(
                    ref[f].astype(jnp.bfloat16),
                    part[step, which],
                    (((1,), (1,)), ((), ())),
                    preferred_element_type=jnp.float32,
                )
                for which, ref in enumerate((direct_ref, turned_ref))
            ]
            result_ref[f] = products[0] + products[1]

        base += part.shape[0]

    for f in range(rows):
        at = place(f)
        direct_ref[at // 8, at % 8 : at % 8 + 2] = result_ref[f, 0:2]
    out_ref[...] = (
        direct_ref[: 2 * rows // 8].reshape(2, rows, modes).astype(jnp.bfloat16)
    )


def respond(pieces, parts):
    rows, modes = pieces[0].shape[2:]
    vmem = pl.BlockSpec(memory_space=pltpu.VMEM)
    size = sum(part.size for part in parts)
    return pl.pallas_call(
        functools.partial(respond_kernel, len(pieces)),
        in_specs=[vmem] * (len(pieces) + len(parts)),
        out_specs=vmem,
        out_shape=jax.ShapeDtypeStruct((2, rows, modes), jnp.bfloat16),
        scratch_shapes=[pltpu.VMEM((rows, 8, modes), jnp.float32)] * 3,
        compiler_params=pltpu.CompilerParams(vmem_limit_bytes=12 * MIB),
        cost_estimate=pl.CostEstimate(flops=4 * size, bytes_accessed=2 * size, transcendentals=0),
        name="respond",
    )(*pieces, *parts)


def project(place_ref, shards, shapes_ref, order_ref, moved_ref):
    _, _, zs, rows, modes = order_ref.shape
    core, z = place_ref[0], place_ref[1] // 2
    start = 0
    for own_ref, twin_ref in zip(shards[::2], shards[1::2]):
        for far, shard_ref in enumerate((own_ref, twin_ref)):
            for k in range(shard_ref.shape[0]):
                for parity in range(2):
                    order_ref[parity, core ^ far, z ^ (start + k)] = shard_ref[
                        k, parity
                    ].astype(jnp.float32)
        start += own_ref.shape[0]
    for parity in range(2):
        moved_ref[parity] = jnp.dot(
            order_ref[parity].reshape(FREQS // 2, modes).astype(jnp.bfloat16),
            shapes_ref[...],
            preferred_element_type=jnp.float32,
        ).astype(jnp.bfloat16)


def early_kernel(place_ref, table_ref, shapes_ref, *refs):
    shards, (waves_ref, order_ref, moved_ref) = refs[:-3], refs[-3:]
    project(place_ref, shards, shapes_ref, order_ref, moved_ref)
    y = place_ref[1] % 2
    block = waves_ref.shape[1] // 4
    for step in range(4):
        part = slice(step * block, (step + 1) * block)
        for parity in range(2):
            waves_ref[parity, part] = jnp.dot(
                table_ref[parity, y, part], moved_ref[parity], preferred_element_type=jnp.float32
            )


def late_kernel(place_ref, table_ref, shapes_ref, *refs):
    shards, (waves_ref, out_ref, order_ref, moved_ref, out_buf, out_sem) = refs[:-6], refs[-6:]
    project(place_ref, shards, shapes_ref, order_ref, moved_ref)
    y = (place_ref[1] % 2) ^ 1
    count = out_sem.shape[0]
    block = out_ref.shape[1] // count

    def copy_out(step):
        part = pl.ds(step * block, block)
        return pltpu.make_async_copy(
            out_buf.at[:, part], out_ref.at[:, part], out_sem.at[step]
        )

    for step in range(count):
        part = slice(step * block, (step + 1) * block)
        even, odd = (
            waves_ref[parity, part]
            + jnp.dot(
                table_ref[parity, y, part], moved_ref[parity], preferred_element_type=jnp.float32
            )
            for parity in range(2)
        )
        out_buf[0, part] = (even + odd).astype(jnp.bfloat16)
        out_buf[1, part] = (even - odd).astype(jnp.bfloat16)
        copy_out(step).start()
    for step in range(count):
        copy_out(step).wait()


def inverse(place, table, shapes_t, shards, waves=None):
    half = table.shape[2]
    modes, dofs = shapes_t.shape
    rows = shards[0].shape[2]
    zs = sum(shard.shape[0] for shard in shards) // 2
    vmem = pl.BlockSpec(memory_space=pltpu.VMEM)
    scratch = [
        pltpu.VMEM((2, CORES, zs, rows, modes), jnp.float32),
        pltpu.VMEM((2, FREQS // 2, dofs), jnp.bfloat16),
    ]
    given = (place, table, shapes_t) + shards
    in_specs = [pl.BlockSpec(memory_space=pltpu.SMEM)] + [vmem] * (len(given) - 1)
    params = pltpu.CompilerParams(vmem_limit_bytes=20 * MIB)
    cost = pl.CostEstimate(
        flops=2 * FREQS * dofs * (half + modes), bytes_accessed=8 * MIB, transcendentals=0
    )
    if waves is None:
        return pl.pallas_call(
            early_kernel,
            in_specs=in_specs,
            out_specs=vmem,
            out_shape=pltpu.VMEM((2, half, dofs), jnp.float32),
            scratch_shapes=scratch,
            compiler_params=params,
            cost_estimate=cost,
            name="early",
        )(*given)
    return pl.pallas_call(
        late_kernel,
        in_specs=in_specs + [vmem],
        out_specs=pl.BlockSpec(memory_space=pltpu.HBM),
        out_shape=jax.ShapeDtypeStruct((2, half, dofs), jnp.bfloat16),
        scratch_shapes=scratch
        + [pltpu.VMEM((2, half, dofs), jnp.bfloat16), pltpu.SemaphoreType.DMA((8,))],
        compiler_params=params,
        cost_estimate=cost,
        name="late",
    )(*given, waves)


def add_kernel(start, splits, ours_ref, came_ref, after_ref, *out_refs):
    at = 0
    for size, out_ref in zip(splits, out_refs):
        for n in range(size):
            total = ours_ref[start + at + n].astype(jnp.float32) + came_ref[at + n].astype(
                jnp.float32
            )
            out_ref[n] = total.astype(jnp.bfloat16)
        at += size


def add(ours, came, start, splits, after):
    vmem, anywhere = pl.BlockSpec(memory_space=pltpu.VMEM), pl.BlockSpec(memory_space=pl.ANY)
    return pl.pallas_call(
        functools.partial(add_kernel, start, splits),
        in_specs=[vmem, vmem, anywhere],
        out_specs=[vmem] * len(splits),
        out_shape=[
            jax.ShapeDtypeStruct((size,) + ours.shape[1:], jnp.bfloat16) for size in splits
        ],
        compiler_params=pltpu.CompilerParams(vmem_limit_bytes=8 * MIB),
        cost_estimate=pl.CostEstimate(
            flops=came.size, bytes_accessed=6 * came.size, transcendentals=0
        ),
        name="add",
    )(ours, came, after)


def on_device(devices, forces, mode_shapes, frf):
    _, steps, dofs = forces.shape
    half = steps // 2
    chips = devices // CORES
    zs = chips // 2

    def swap(values, distance):
        pairs = [(i, i ^ distance) for i in range(devices)]
        return lax.ppermute(values, "dof", pairs)

    index = lax.axis_index("dof")
    place = jnp.stack([index % CORES, index // CORES]).astype(jnp.int32)
    shapes_t = mode_shapes.T
    fwd = jnp.asarray(forward_tables(steps, chips).astype(jnp.bfloat16))
    inv = jnp.asarray(inverse_tables(steps, chips).astype(jnp.bfloat16))

    unit = frf.shape[0] // 8
    keep, send, part0 = forward(
        place, fwd, forces.reshape(2, half, dofs), shapes_t, frf, 2 * unit, chips
    )
    part1 = load(frf, 2 * unit, unit, send)
    slots = (2 * zs,) + keep.shape[2:]
    here, there_near, there_far = add(
        keep.reshape(slots), swap(send, 1).reshape(slots), 0, (zs, 1, zs - 1), part1
    )
    came_far, came_near = swap(there_far, 2), swap(there_near, 2)
    part2 = load(frf, 3 * unit, 3 * unit, there_far)
    pieces = add(here, came_far, 1, (1,) * (zs - 1), part2)
    part3 = load(frf, 6 * unit, 2 * unit, pieces[0])
    came = [swap(piece, 4 * k) for k, piece in enumerate(pieces, 1)]
    response = respond([here[:1], came_near, *came], (part0, part1, part2, part3))

    across = swap(response[None], 2)
    shards = [swap(response, 4 * k) for k in range(1, zs)]
    far, across = lax.optimization_barrier((jnp.stack(shards), across))
    across_far = swap(far, 2)
    own = jnp.concatenate([response[None], far])
    twin, twin_across = swap(own, 1), swap(across, 1)
    waves = inverse(place, inv, shapes_t, (own, twin))
    across_far, waves = lax.optimization_barrier((across_far, waves))
    groups = (across, twin_across, across_far, swap(across_far, 1))
    out = inverse(place, inv, shapes_t, groups, waves)
    return out.reshape(1, steps, dofs)


def solution(mesh):
    devices = mesh.shape["dof"]
    return jax.shard_map(
        functools.partial(on_device, devices),
        mesh=mesh,
        in_specs=(P("grp", None, "dof"), P("dof", None), P("dof", None, None, None)),
        out_specs=P("grp", None, "dof"),
        check_vma=False,
    )
```

```python
import functools
import math

import jax
import jax.numpy as jnp
import numpy as np
from jax import lax
from jax.experimental import pallas as pl
from jax.experimental.pallas import tpu as pltpu
from jax.sharding import PartitionSpec as P

FREQS = 512
CORES = 2
MIB = 1 << 20


def frequency_order(chips, parity):
    mine = FREQS // (chips * CORES)
    owned = np.arange(FREQS).reshape(chips // 2, 2, CORES, mine // 2, 2)
    return owned[..., parity].transpose(1, 2, 0, 3).reshape(-1)


def forward_tables(steps, chips):
    times = np.arange(steps // 2, dtype=np.int64)
    tables = []
    for parity in range(2):
        ids = frequency_order(chips, parity)
        angle = (ids[:, None] * times[None, :] % steps) * (2.0 * math.pi / steps)
        table = np.stack([np.cos(angle), -np.sin(angle)], axis=1) / math.sqrt(steps)
        tables.append(table.reshape(FREQS, steps // 2))
    return np.stack(tables).reshape(2, 2, FREQS // 2, steps // 2)


def inverse_tables(steps, chips):
    tables = forward_tables(steps, chips) * 2.0
    for parity in range(2):
        weights = np.where(frequency_order(chips, parity) == 0, 0.5, 1.0)
        tables[parity] *= np.repeat(weights, 2).reshape(2, FREQS // 2, 1)
    return tables.transpose(0, 1, 3, 2)


def chunk_list(half):
    unit = half // 8
    sizes = (unit, unit, 2 * unit, 4 * unit)
    starts = (0, unit, 2 * unit, 4 * unit)
    return tuple(zip(starts, sizes))


def split_cores(place_ref, spec, shapes_ref, parity, keep_ref, send_ref):
    zs, _, rows, modes = keep_ref.shape
    first, z = place_ref[0] == 0, place_ref[1] // 2
    spec = lax.dot_general(
        spec.astype(jnp.bfloat16),
        shapes_ref[...],
        (((1,), (1,)), ((), ())),
        preferred_element_type=jnp.float32,
    ).reshape(CORES, zs, rows, modes)
    keep = jnp.where(first, spec[0], spec[1]).astype(jnp.bfloat16)
    send = jnp.where(first, spec[1], spec[0]).astype(jnp.bfloat16)
    for k in range(zs):
        keep_ref[z ^ k, parity] = keep[k]
        send_ref[z ^ k, parity] = send[k]


def across_kernel(
    place_ref, table_ref, forces_ref, shapes_ref,
    keep_ref, send_ref, folded_ref, rest_ref, shapes_buf,
    table_buf, forces_buf, acc_ref, table_sem, forces_sem, rest_sem, shapes_sem,
):
    y = place_ref[1] % 2
    chunks = chunk_list(forces_ref.shape[1])
    copies = []
    for n, (start, size) in enumerate(chunks):
        part = pl.ds(start, size)
        pair = (
            pltpu.make_async_copy(
                forces_ref.at[:, part], forces_buf.at[:, part], forces_sem.at[n]
            ),
            pltpu.make_async_copy(
                table_ref.at[:, y ^ 1, :, part], table_buf.at[:, :, part], table_sem.at[n]
            ),
        )
        for copy in pair:
            copy.start()
        copies.append(pair)
    later = (
        pltpu.make_async_copy(shapes_ref, shapes_buf, shapes_sem),
        pltpu.make_async_copy(table_ref.at[:, y], rest_ref, rest_sem),
    )
    for copy in later:
        copy.start()

    for n, (start, size) in enumerate(chunks):
        for copy in copies[n]:
            copy.wait()
        low = forces_buf[0, start : start + size]
        high = forces_buf[1, start : start + size]
        for parity, folded in enumerate((low + high, low - high)):
            folded_ref[parity, start : start + size] = folded
            part = jnp.dot(
                table_buf[parity, :, start : start + size],
                folded,
                preferred_element_type=jnp.float32,
            )
            if n == 0:
                acc_ref[parity] = part
            else:
                acc_ref[parity] += part

    later[0].wait()
    for parity in range(2):
        split_cores(place_ref, acc_ref[parity], shapes_buf, parity, keep_ref, send_ref)
    later[1].wait()


def across(place, table, forces, shapes_t, zs):
    _, half, dofs = forces.shape
    modes = shapes_t.shape[0]
    rows = FREQS // (2 * CORES * zs)
    out = jax.ShapeDtypeStruct((zs, 2, rows, modes), jnp.bfloat16)
    vmem, hbm = pl.BlockSpec(memory_space=pltpu.VMEM), pl.BlockSpec(memory_space=pltpu.HBM)
    count = len(chunk_list(half))
    return pl.pallas_call(
        across_kernel,
        in_specs=[pl.BlockSpec(memory_space=pltpu.SMEM), hbm, hbm, hbm],
        out_specs=[vmem] * 5,
        out_shape=[
            out,
            out,
            pltpu.VMEM(forces.shape, jnp.bfloat16),
            pltpu.VMEM((2, FREQS // 2, half), jnp.bfloat16),
            pltpu.VMEM(shapes_t.shape, jnp.bfloat16),
        ],
        scratch_shapes=[
            pltpu.VMEM((2, FREQS // 2, half), jnp.bfloat16),
            pltpu.VMEM(forces.shape, jnp.bfloat16),
            pltpu.VMEM((2, FREQS // 2, dofs), jnp.float32),
            pltpu.SemaphoreType.DMA((count,)),
            pltpu.SemaphoreType.DMA((count,)),
            pltpu.SemaphoreType.DMA,
            pltpu.SemaphoreType.DMA,
        ],
        compiler_params=pltpu.CompilerParams(vmem_limit_bytes=20 * MIB),
        cost_estimate=pl.CostEstimate(
            flops=2 * FREQS * dofs * (half + modes), bytes_accessed=12 * MIB, transcendentals=0
        ),
        name="across",
    )(place, in_hbm(table), in_hbm(forces), in_hbm(shapes_t))


def within_kernel(
    parity, start, place_ref, table_ref, folded_ref, shapes_ref, frf_ref, after_ref,
    keep_ref, send_ref, held_ref, sem,
):
    copies = load_copies(start, frf_ref, held_ref, sem)
    for copy in copies:
        copy.start()
    spec = jnp.dot(table_ref[parity], folded_ref[parity], preferred_element_type=jnp.float32)
    split_cores(place_ref, spec, shapes_ref, 0, keep_ref, send_ref)
    for copy in copies:
        copy.wait()


def within(parity, place, table, folded, shapes_t, frf, start, held, after, zs):
    _, half, dofs = folded.shape
    modes = shapes_t.shape[0]
    rows = FREQS // (2 * CORES * zs)
    out = jax.ShapeDtypeStruct((zs, 1, rows, modes), jnp.bfloat16)
    vmem, hbm = pl.BlockSpec(memory_space=pltpu.VMEM), pl.BlockSpec(memory_space=pltpu.HBM)
    return pl.pallas_call(
        functools.partial(within_kernel, parity, start),
        in_specs=[pl.BlockSpec(memory_space=pltpu.SMEM), vmem, vmem, vmem, hbm]
        + [pl.BlockSpec(memory_space=pl.ANY)],
        out_specs=[vmem] * 3,
        out_shape=[out, out, pltpu.VMEM((held,) + frf.shape[1:], jnp.bfloat16)],
        scratch_shapes=[pltpu.SemaphoreType.DMA((math.gcd(held, 4),))],
        compiler_params=pltpu.CompilerParams(vmem_limit_bytes=8 * MIB),
        cost_estimate=pl.CostEstimate(
            flops=FREQS * dofs * (half + modes), bytes_accessed=8 * MIB, transcendentals=0
        ),
        name="within",
    )(place, table, folded, shapes_t, in_hbm(frf), after)


def in_hbm(array):
    return pltpu.with_memory_space_constraint(array, pltpu.HBM)


def load_copies(start, frf_ref, held_ref, sem):
    count = sem.shape[0]
    size = held_ref.shape[0] // count
    return [
        pltpu.make_async_copy(
            frf_ref.at[pl.ds(start + n * size, size)],
            held_ref.at[pl.ds(n * size, size)],
            sem.at[n],
        )
        for n in range(count)
    ]


def load_kernel(start, frf_ref, after_ref, held_ref, sem):
    copies = load_copies(start, frf_ref, held_ref, sem)
    for copy in copies:
        copy.start()
    for copy in copies:
        copy.wait()


def load(frf, start, size, after):
    hbm, anywhere = pl.BlockSpec(memory_space=pltpu.HBM), pl.BlockSpec(memory_space=pl.ANY)
    return pl.pallas_call(
        functools.partial(load_kernel, start),
        in_specs=[hbm, anywhere],
        out_specs=pl.BlockSpec(memory_space=pltpu.VMEM),
        out_shape=pltpu.VMEM((size,) + frf.shape[1:], jnp.bfloat16),
        scratch_shapes=[pltpu.SemaphoreType.DMA((math.gcd(size, 4),))],
        compiler_params=pltpu.CompilerParams(vmem_limit_bytes=2 * MIB),
        cost_estimate=pl.CostEstimate(
            flops=0, bytes_accessed=4 * size * math.prod(frf.shape[1:]), transcendentals=0
        ),
        name="load",
    )(in_hbm(frf), after)


def respond_kernel(count, *refs):
    pieces, parts = refs[:count], refs[count:-4]
    out_ref, direct_ref, turned_ref, result_ref = refs[-4:]
    _, rows, modes = out_ref.shape
    total = sum(piece[0].astype(jnp.float32) for piece in pieces).reshape(2 * rows, modes)
    total = total.astype(jnp.bfloat16).astype(jnp.float32)
    row = lax.broadcasted_iota(jnp.int32, total.shape, 0)
    turned = jnp.where(row % 2 == 0, -jnp.roll(total, -1, axis=0), jnp.roll(total, 1, axis=0))

    def place(f):
        return (f % 2) * rows + f // 2 * 2

    direct_ref[...] = jnp.zeros_like(direct_ref)
    turned_ref[...] = jnp.zeros_like(turned_ref)
    for f in range(rows):
        at = place(f)
        direct_ref[f, 0:2] = total[at : at + 2]
        turned_ref[f, 0:2] = turned[at : at + 2]
    base = 0
    for part in parts:

        @pl.loop(0, part.shape[0], unroll=math.gcd(4, part.shape[0]))
        def _(step, part=part, base=base):
            f = base + step
            products = [
                lax.dot_general(
                    ref[f].astype(jnp.bfloat16),
                    part[step, which],
                    (((1,), (1,)), ((), ())),
                    preferred_element_type=jnp.float32,
                )
                for which, ref in enumerate((direct_ref, turned_ref))
            ]
            result_ref[f] = products[0] + products[1]

        base += part.shape[0]

    for f in range(rows):
        at = place(f)
        direct_ref[at // 8, at % 8 : at % 8 + 2] = result_ref[f, 0:2]
    out_ref[...] = (
        direct_ref[: 2 * rows // 8].reshape(2, rows, modes).astype(jnp.bfloat16)
    )


def respond(pieces, parts):
    rows, modes = pieces[0].shape[2:]
    vmem = pl.BlockSpec(memory_space=pltpu.VMEM)
    size = sum(part.size for part in parts)
    return pl.pallas_call(
        functools.partial(respond_kernel, len(pieces)),
        in_specs=[vmem] * (len(pieces) + len(parts)),
        out_specs=vmem,
        out_shape=jax.ShapeDtypeStruct((2, rows, modes), jnp.bfloat16),
        scratch_shapes=[pltpu.VMEM((rows, 8, modes), jnp.float32)] * 3,
        compiler_params=pltpu.CompilerParams(vmem_limit_bytes=12 * MIB),
        cost_estimate=pl.CostEstimate(flops=4 * size, bytes_accessed=2 * size, transcendentals=0),
        name="respond",
    )(*pieces, *parts)


def project(place_ref, shards, shapes_ref, order_ref, moved_ref):
    _, _, zs, rows, modes = order_ref.shape
    core, z = place_ref[0], place_ref[1] // 2
    start = 0
    for own_ref, twin_ref in zip(shards[::2], shards[1::2]):
        for far, shard_ref in enumerate((own_ref, twin_ref)):
            for k in range(shard_ref.shape[0]):
                for parity in range(2):
                    order_ref[parity, core ^ far, z ^ (start + k)] = shard_ref[
                        k, parity
                    ].astype(jnp.float32)
        start += own_ref.shape[0]
    for parity in range(2):
        moved_ref[parity] = jnp.dot(
            order_ref[parity].reshape(FREQS // 2, modes).astype(jnp.bfloat16),
            shapes_ref[...],
            preferred_element_type=jnp.float32,
        ).astype(jnp.bfloat16)


def early_kernel(place_ref, table_ref, shapes_ref, *refs):
    shards, (waves_ref, order_ref, moved_ref) = refs[:-3], refs[-3:]
    project(place_ref, shards, shapes_ref, order_ref, moved_ref)
    y = place_ref[1] % 2
    block = waves_ref.shape[1] // 4
    for step in range(4):
        part = slice(step * block, (step + 1) * block)
        for parity in range(2):
            waves_ref[parity, part] = jnp.dot(
                table_ref[parity, y, part], moved_ref[parity], preferred_element_type=jnp.float32
            )


def late_kernel(place_ref, table_ref, shapes_ref, *refs):
    shards, (waves_ref, out_ref, order_ref, moved_ref, out_buf, out_sem) = refs[:-6], refs[-6:]
    project(place_ref, shards, shapes_ref, order_ref, moved_ref)
    y = (place_ref[1] % 2) ^ 1
    count = out_sem.shape[0]
    block = out_ref.shape[1] // count

    def copy_out(step):
        part = pl.ds(step * block, block)
        return pltpu.make_async_copy(
            out_buf.at[:, part], out_ref.at[:, part], out_sem.at[step]
        )

    for step in range(count):
        part = slice(step * block, (step + 1) * block)
        even, odd = (
            waves_ref[parity, part]
            + jnp.dot(
                table_ref[parity, y, part], moved_ref[parity], preferred_element_type=jnp.float32
            )
            for parity in range(2)
        )
        out_buf[0, part] = (even + odd).astype(jnp.bfloat16)
        out_buf[1, part] = (even - odd).astype(jnp.bfloat16)
        copy_out(step).start()
    for step in range(count):
        copy_out(step).wait()


def inverse(place, table, shapes_t, shards, waves=None):
    half = table.shape[2]
    modes, dofs = shapes_t.shape
    rows = shards[0].shape[2]
    zs = sum(shard.shape[0] for shard in shards) // 2
    vmem = pl.BlockSpec(memory_space=pltpu.VMEM)
    scratch = [
        pltpu.VMEM((2, CORES, zs, rows, modes), jnp.float32),
        pltpu.VMEM((2, FREQS // 2, dofs), jnp.bfloat16),
    ]
    given = (place, table, shapes_t) + shards
    in_specs = [pl.BlockSpec(memory_space=pltpu.SMEM)] + [vmem] * (len(given) - 1)
    params = pltpu.CompilerParams(vmem_limit_bytes=20 * MIB)
    cost = pl.CostEstimate(
        flops=2 * FREQS * dofs * (half + modes), bytes_accessed=8 * MIB, transcendentals=0
    )
    if waves is None:
        return pl.pallas_call(
            early_kernel,
            in_specs=in_specs,
            out_specs=vmem,
            out_shape=pltpu.VMEM((2, half, dofs), jnp.float32),
            scratch_shapes=scratch,
            compiler_params=params,
            cost_estimate=pl.CostEstimate(flops=1000, bytes_accessed=1000, transcendentals=0),
            name="early",
        )(*given)
    return pl.pallas_call(
        late_kernel,
        in_specs=in_specs + [vmem],
        out_specs=pl.BlockSpec(memory_space=pltpu.HBM),
        out_shape=jax.ShapeDtypeStruct((2, half, dofs), jnp.bfloat16),
        scratch_shapes=scratch
        + [pltpu.VMEM((2, half, dofs), jnp.bfloat16), pltpu.SemaphoreType.DMA((8,))],
        compiler_params=params,
        cost_estimate=cost,
        name="late",
    )(*given, waves)


def add_kernel(ours_ref, came_ref, out_ref):
    total = ours_ref[...].astype(jnp.float32) + came_ref[...].astype(jnp.float32)
    out_ref[...] = total.astype(jnp.bfloat16)


def add(ours, came):
    vmem = pl.BlockSpec(memory_space=pltpu.VMEM)
    return pl.pallas_call(
        add_kernel,
        in_specs=[vmem] * 2,
        out_specs=vmem,
        out_shape=jax.ShapeDtypeStruct(ours.shape, jnp.bfloat16),
        compiler_params=pltpu.CompilerParams(vmem_limit_bytes=8 * MIB),
        cost_estimate=pl.CostEstimate(
            flops=came.size, bytes_accessed=6 * came.size, transcendentals=0
        ),
        name="add",
    )(ours, came)


def gather_sum_kernel(came_ref, after_ref, *refs):
    within_refs, out_refs = refs[:4], refs[4:]
    for k, out_ref in enumerate(out_refs):
        for parity in range(2):
            keep_ref, twin_ref = within_refs[2 * parity : 2 * parity + 2]
            total = keep_ref[k, 0].astype(jnp.float32) + twin_ref[k, 0].astype(jnp.float32)
            total = total + came_ref[k, parity].astype(jnp.float32)
            out_ref[0, parity] = total.astype(jnp.bfloat16)


def gather_sum(came, kept, after):
    vmem = pl.BlockSpec(memory_space=pltpu.VMEM)
    zs = came.shape[0]
    return pl.pallas_call(
        gather_sum_kernel,
        in_specs=[vmem, pl.BlockSpec(memory_space=pl.ANY)] + [vmem] * 4,
        out_specs=[vmem] * zs,
        out_shape=[jax.ShapeDtypeStruct((1,) + came.shape[1:], jnp.bfloat16)] * zs,
        compiler_params=pltpu.CompilerParams(vmem_limit_bytes=8 * MIB),
        cost_estimate=pl.CostEstimate(
            flops=2 * came.size, bytes_accessed=8 * came.size, transcendentals=0
        ),
        name="gather_sum",
    )(came, after, *kept)


def on_device(devices, forces, mode_shapes, frf):
    _, steps, dofs = forces.shape
    half = steps // 2
    chips = devices // CORES
    zs = chips // 2

    def swap(values, distance):
        pairs = [(i, i ^ distance) for i in range(devices)]
        return lax.ppermute(values, "dof", pairs)

    index = lax.axis_index("dof")
    place = jnp.stack([index % CORES, index // CORES]).astype(jnp.int32)
    shapes_t = mode_shapes.T
    fwd = jnp.asarray(forward_tables(steps, chips).astype(jnp.bfloat16))
    inv = jnp.asarray(inverse_tables(steps, chips).astype(jnp.bfloat16))

    unit = frf.shape[0] // 8
    keep, send, folded, rest, shapes_v = across(
        place, fwd, forces.reshape(2, half, dofs), shapes_t, zs
    )
    given = (place, rest, folded, shapes_v, frf)
    keep0, send0, part0 = within(0, *given, 0, unit, send, zs)
    pair = add(keep, swap(send, 1))
    came = swap(pair, 2)
    keep1, send1, part1 = within(1, *given, unit, unit, pair, zs)
    part2 = load(frf, 2 * unit, 3 * unit, send1)
    pieces = gather_sum(came, (keep0, swap(send0, 1), keep1, swap(send1, 1)), part2)
    part3 = load(frf, 5 * unit, 3 * unit, pieces[0])
    pieces = [pieces[0]] + [swap(pieces[k], 4 * k) for k in range(1, zs)]
    response = respond(pieces, (part0, part1, part2, part3))

    over = swap(response[None], 2)
    shards = [swap(response, 4 * k) for k in range(1, zs)]
    far, over = lax.optimization_barrier((jnp.stack(shards), over))
    over_far = swap(far, 2)
    own = jnp.concatenate([response[None], far])
    twin, twin_over = swap(own, 1), swap(over, 1)
    waves = inverse(place, inv, shapes_v, (own, twin))
    over_far, waves = lax.optimization_barrier((over_far, waves))
    out = inverse(place, inv, shapes_v, (over, twin_over, over_far, swap(over_far, 1)), waves)
    return out.reshape(1, steps, dofs)


def solution(mesh):
    devices = mesh.shape["dof"]
    return jax.shard_map(
        functools.partial(on_device, devices),
        mesh=mesh,
        in_specs=(P("grp", None, "dof"), P("dof", None), P("dof", None, None, None)),
        out_specs=P("grp", None, "dof"),
        check_vma=False,
    )
```

```python
import functools
import math

import jax
import jax.numpy as jnp
import numpy as np
from jax import lax
from jax.experimental import pallas as pl
from jax.experimental.pallas import tpu as pltpu
from jax.sharding import PartitionSpec as P

FREQS = 512
CORES = 2
CHUNK = 512
MIB = 1 << 20


def frequency_order(chips, parity):
    mine = FREQS // (chips * CORES)
    owned = np.arange(FREQS).reshape(chips // 2, 2, CORES, mine // 2, 2)
    return owned[..., parity].transpose(1, 2, 0, 3).reshape(-1)


def signed_tables(steps, chips):
    times = np.arange(steps // 2, dtype=np.int64)
    tables = []
    for parity in range(2):
        ids = frequency_order(chips, parity)
        angle = (ids[:, None] * times[None, :] % steps) * (2.0 * math.pi / steps)
        table = np.stack([np.cos(angle), -np.sin(angle)], axis=1) / math.sqrt(steps)
        tables.append(table.reshape(2, FREQS // 2, steps // 2))
    return np.stack(tables)


def forward_tables(steps, chips):
    tables = signed_tables(steps, chips).reshape(2, 2, FREQS // 2, -1, CHUNK)
    return tables.transpose(1, 3, 0, 2, 4)


def inverse_tables(steps, chips):
    tables = signed_tables(steps, chips) * 2.0
    for parity in range(2):
        weights = np.where(frequency_order(chips, parity) == 0, 0.5, 1.0)
        tables[parity] *= np.repeat(weights, 2).reshape(2, FREQS // 2, 1)
    return tables.transpose(1, 0, 3, 2)


def split_cores(place_ref, spec, shapes_ref, parity, keep_ref, send_ref):
    zs, _, rows, modes = keep_ref.shape
    first, z = place_ref[0] == 0, place_ref[1] // 2
    spec = lax.dot_general(
        spec.astype(jnp.bfloat16),
        shapes_ref[...],
        (((1,), (1,)), ((), ())),
        preferred_element_type=jnp.float32,
    ).reshape(CORES, zs, rows, modes)
    keep = jnp.where(first, spec[0], spec[1]).astype(jnp.bfloat16)
    send = jnp.where(first, spec[1], spec[0]).astype(jnp.bfloat16)
    for k in range(zs):
        keep_ref[z ^ k, parity] = keep[k]
        send_ref[z ^ k, parity] = send[k]


def across_kernel(
    place_ref, table_ref, forces_ref, shapes_ref,
    keep_ref, send_ref, folded_ref, rest_ref, shapes_buf,
    table_buf, forces_buf, acc_ref, table_sem, forces_sem, rest_sem, shapes_sem,
):
    y = place_ref[1] % 2
    count = folded_ref.shape[0]

    def chunk_copies(n):
        return (
            pltpu.make_async_copy(
                forces_ref.at[:, pl.ds(n * CHUNK, CHUNK)], forces_buf.at[n], forces_sem.at[n]
            ),
            pltpu.make_async_copy(table_ref.at[y ^ 1, n], table_buf.at[n], table_sem.at[n]),
        )

    for n in range(count):
        for copy in chunk_copies(n):
            copy.start()
    later = (
        pltpu.make_async_copy(shapes_ref, shapes_buf, shapes_sem),
        pltpu.make_async_copy(table_ref.at[y], rest_ref, rest_sem),
    )
    for copy in later:
        copy.start()
    acc_ref[...] = jnp.zeros_like(acc_ref)

    @pl.loop(0, count)
    def _(n):
        for copy in chunk_copies(n):
            copy.wait()
        low, high = forces_buf[n, 0], forces_buf[n, 1]
        for parity, folded in enumerate((low + high, low - high)):
            folded_ref[n, parity] = folded
            acc_ref[parity] += jnp.dot(
                table_buf[n, parity], folded, preferred_element_type=jnp.float32
            )

    later[0].wait()

    @pl.loop(0, 2)
    def _(parity):
        split_cores(place_ref, acc_ref[parity], shapes_buf, parity, keep_ref, send_ref)

    later[1].wait()


def across(place, table, forces, shapes_t, zs):
    _, half, dofs = forces.shape
    modes = shapes_t.shape[0]
    rows = FREQS // (2 * CORES * zs)
    out = jax.ShapeDtypeStruct((zs, 2, rows, modes), jnp.bfloat16)
    vmem, hbm = pl.BlockSpec(memory_space=pltpu.VMEM), pl.BlockSpec(memory_space=pltpu.HBM)
    count = half // CHUNK
    return pl.pallas_call(
        across_kernel,
        in_specs=[pl.BlockSpec(memory_space=pltpu.SMEM), hbm, hbm, hbm],
        out_specs=[vmem] * 5,
        out_shape=[
            out,
            out,
            pltpu.VMEM((count, 2, CHUNK, dofs), jnp.bfloat16),
            pltpu.VMEM(table.shape[1:], jnp.bfloat16),
            pltpu.VMEM(shapes_t.shape, jnp.bfloat16),
        ],
        scratch_shapes=[
            pltpu.VMEM(table.shape[1:], jnp.bfloat16),
            pltpu.VMEM((count, 2, CHUNK, dofs), jnp.bfloat16),
            pltpu.VMEM((2, FREQS // 2, dofs), jnp.float32),
            pltpu.SemaphoreType.DMA((count,)),
            pltpu.SemaphoreType.DMA((count,)),
            pltpu.SemaphoreType.DMA,
            pltpu.SemaphoreType.DMA,
        ],
        compiler_params=pltpu.CompilerParams(vmem_limit_bytes=20 * MIB),
        cost_estimate=pl.CostEstimate(
            flops=2 * FREQS * dofs * (half + modes), bytes_accessed=12 * MIB, transcendentals=0
        ),
        name="across",
    )(place, in_hbm(table), in_hbm(forces), in_hbm(shapes_t))


def within_kernel(
    parity, start, place_ref, table_ref, folded_ref, shapes_ref, frf_ref, after_ref,
    keep_ref, send_ref, held_ref, acc_ref, sem,
):
    copies = load_copies(start, frf_ref, held_ref, sem)
    for copy in copies:
        copy.start()
    acc_ref[...] = jnp.zeros_like(acc_ref)

    @pl.loop(0, folded_ref.shape[0])
    def _(n):
        acc_ref[...] += jnp.dot(
            table_ref[n, parity], folded_ref[n, parity], preferred_element_type=jnp.float32
        )

    split_cores(place_ref, acc_ref[...], shapes_ref, 0, keep_ref, send_ref)
    for copy in copies:
        copy.wait()


def within(parity, place, table, folded, shapes_t, frf, start, held, after, zs):
    count, _, chunk, dofs = folded.shape
    modes = shapes_t.shape[0]
    rows = FREQS // (2 * CORES * zs)
    out = jax.ShapeDtypeStruct((zs, 1, rows, modes), jnp.bfloat16)
    vmem, hbm = pl.BlockSpec(memory_space=pltpu.VMEM), pl.BlockSpec(memory_space=pltpu.HBM)
    return pl.pallas_call(
        functools.partial(within_kernel, parity, start),
        in_specs=[pl.BlockSpec(memory_space=pltpu.SMEM), vmem, vmem, vmem, hbm]
        + [pl.BlockSpec(memory_space=pl.ANY)],
        out_specs=[vmem] * 3,
        out_shape=[out, out, pltpu.VMEM((held,) + frf.shape[1:], jnp.bfloat16)],
        scratch_shapes=[
            pltpu.VMEM((FREQS // 2, dofs), jnp.float32),
            pltpu.SemaphoreType.DMA((math.gcd(held, 4),)),
        ],
        compiler_params=pltpu.CompilerParams(vmem_limit_bytes=8 * MIB),
        cost_estimate=pl.CostEstimate(
            flops=FREQS * dofs * (count * chunk + modes),
            bytes_accessed=8 * MIB,
            transcendentals=0,
        ),
        name="within",
    )(place, table, folded, shapes_t, in_hbm(frf), after)


def in_hbm(array):
    return pltpu.with_memory_space_constraint(array, pltpu.HBM)


def load_copies(start, frf_ref, held_ref, sem):
    count = sem.shape[0]
    size = held_ref.shape[0] // count
    return [
        pltpu.make_async_copy(
            frf_ref.at[pl.ds(start + n * size, size)],
            held_ref.at[pl.ds(n * size, size)],
            sem.at[n],
        )
        for n in range(count)
    ]


def load_kernel(start, frf_ref, after_ref, held_ref, sem):
    copies = load_copies(start, frf_ref, held_ref, sem)
    for copy in copies:
        copy.start()
    for copy in copies:
        copy.wait()


def load(frf, start, size, after):
    hbm, anywhere = pl.BlockSpec(memory_space=pltpu.HBM), pl.BlockSpec(memory_space=pl.ANY)
    return pl.pallas_call(
        functools.partial(load_kernel, start),
        in_specs=[hbm, anywhere],
        out_specs=pl.BlockSpec(memory_space=pltpu.VMEM),
        out_shape=pltpu.VMEM((size,) + frf.shape[1:], jnp.bfloat16),
        scratch_shapes=[pltpu.SemaphoreType.DMA((math.gcd(size, 4),))],
        compiler_params=pltpu.CompilerParams(vmem_limit_bytes=2 * MIB),
        cost_estimate=pl.CostEstimate(
            flops=0, bytes_accessed=4 * size * math.prod(frf.shape[1:]), transcendentals=0
        ),
        name="load",
    )(in_hbm(frf), after)


def respond_kernel(count, *refs):
    pieces, parts = refs[:count], refs[count:-4]
    out_ref, direct_ref, turned_ref, result_ref = refs[-4:]
    _, rows, modes = out_ref.shape
    total = sum(piece[0].astype(jnp.float32) for piece in pieces).reshape(2 * rows, modes)
    total = total.astype(jnp.bfloat16).astype(jnp.float32)
    row = lax.broadcasted_iota(jnp.int32, total.shape, 0)
    turned = jnp.where(row % 2 == 0, -jnp.roll(total, -1, axis=0), jnp.roll(total, 1, axis=0))

    def place(f):
        return (f % 2) * rows + f // 2 * 2

    direct_ref[...] = jnp.zeros_like(direct_ref)
    turned_ref[...] = jnp.zeros_like(turned_ref)
    for f in range(rows):
        at = place(f)
        direct_ref[f, 0:2] = total[at : at + 2]
        turned_ref[f, 0:2] = turned[at : at + 2]
    base = 0
    for part in parts:

        @pl.loop(0, part.shape[0], unroll=math.gcd(4, part.shape[0]))
        def _(step, part=part, base=base):
            f = base + step
            products = [
                lax.dot_general(
                    ref[f].astype(jnp.bfloat16),
                    part[step, which],
                    (((1,), (1,)), ((), ())),
                    preferred_element_type=jnp.float32,
                )
                for which, ref in enumerate((direct_ref, turned_ref))
            ]
            result_ref[f] = products[0] + products[1]

        base += part.shape[0]

    for f in range(rows):
        at = place(f)
        direct_ref[at // 8, at % 8 : at % 8 + 2] = result_ref[f, 0:2]
    out_ref[...] = (
        direct_ref[: 2 * rows // 8].reshape(2, rows, modes).astype(jnp.bfloat16)
    )


def respond(pieces, parts):
    rows, modes = pieces[0].shape[2:]
    vmem = pl.BlockSpec(memory_space=pltpu.VMEM)
    size = sum(part.size for part in parts)
    return pl.pallas_call(
        functools.partial(respond_kernel, len(pieces)),
        in_specs=[vmem] * (len(pieces) + len(parts)),
        out_specs=vmem,
        out_shape=jax.ShapeDtypeStruct((2, rows, modes), jnp.bfloat16),
        scratch_shapes=[pltpu.VMEM((rows, 8, modes), jnp.float32)] * 3,
        compiler_params=pltpu.CompilerParams(vmem_limit_bytes=12 * MIB),
        cost_estimate=pl.CostEstimate(flops=4 * size, bytes_accessed=2 * size, transcendentals=0),
        name="respond",
    )(*pieces, *parts)


def project(place_ref, shards, shapes_ref, order_ref, moved_ref):
    _, _, zs, rows, modes = order_ref.shape
    core, z = place_ref[0], place_ref[1] // 2
    start = 0
    for own_ref, twin_ref in zip(shards[::2], shards[1::2]):
        for far, shard_ref in enumerate((own_ref, twin_ref)):
            for k in range(shard_ref.shape[0]):
                for parity in range(2):
                    order_ref[parity, core ^ far, z ^ (start + k)] = shard_ref[
                        k, parity
                    ].astype(jnp.float32)
        start += own_ref.shape[0]

    @pl.loop(0, 2)
    def _(parity):
        moved_ref[parity] = jnp.dot(
            order_ref[parity].reshape(FREQS // 2, modes).astype(jnp.bfloat16),
            shapes_ref[...],
            preferred_element_type=jnp.float32,
        ).astype(jnp.bfloat16)


def early_kernel(place_ref, table_ref, shapes_ref, *refs):
    shards, (waves_ref, order_ref, moved_ref) = refs[:-3], refs[-3:]
    project(place_ref, shards, shapes_ref, order_ref, moved_ref)
    y = place_ref[1] % 2

    @pl.loop(0, waves_ref.shape[1] // CHUNK)
    def _(step):
        part = pl.ds(step * CHUNK, CHUNK)
        for parity in range(2):
            waves_ref[parity, part] = jnp.dot(
                table_ref[y, parity, part], moved_ref[parity], preferred_element_type=jnp.float32
            )


def late_kernel(place_ref, table_ref, shapes_ref, *refs):
    shards, (waves_ref, out_ref, order_ref, moved_ref, out_buf, out_sem) = refs[:-6], refs[-6:]
    project(place_ref, shards, shapes_ref, order_ref, moved_ref)
    y = (place_ref[1] % 2) ^ 1
    count = out_sem.shape[0]
    block = out_ref.shape[1] // count

    def copy_out(step):
        part = pl.ds(step * block, block)
        return pltpu.make_async_copy(
            out_buf.at[:, part], out_ref.at[:, part], out_sem.at[step]
        )

    @pl.loop(0, count)
    def _(step):
        part = pl.ds(step * block, block)
        even, odd = (
            waves_ref[parity, part]
            + jnp.dot(
                table_ref[y, parity, part], moved_ref[parity], preferred_element_type=jnp.float32
            )
            for parity in range(2)
        )
        out_buf[0, part] = (even + odd).astype(jnp.bfloat16)
        out_buf[1, part] = (even - odd).astype(jnp.bfloat16)
        copy_out(step).start()

    for step in range(count):
        copy_out(step).wait()


def inverse(place, table, shapes_t, shards, waves=None):
    half = table.shape[2]
    modes, dofs = shapes_t.shape
    rows = shards[0].shape[2]
    zs = sum(shard.shape[0] for shard in shards) // 2
    vmem = pl.BlockSpec(memory_space=pltpu.VMEM)
    scratch = [
        pltpu.VMEM((2, CORES, zs, rows, modes), jnp.float32),
        pltpu.VMEM((2, FREQS // 2, dofs), jnp.bfloat16),
    ]
    given = (place, table, shapes_t) + shards
    in_specs = [pl.BlockSpec(memory_space=pltpu.SMEM)] + [vmem] * (len(given) - 1)
    params = pltpu.CompilerParams(vmem_limit_bytes=20 * MIB)
    cost = pl.CostEstimate(
        flops=2 * FREQS * dofs * (half + modes), bytes_accessed=8 * MIB, transcendentals=0
    )
    if waves is None:
        return pl.pallas_call(
            early_kernel,
            in_specs=in_specs,
            out_specs=vmem,
            out_shape=pltpu.VMEM((2, half, dofs), jnp.float32),
            scratch_shapes=scratch,
            compiler_params=params,
            cost_estimate=pl.CostEstimate(flops=1000, bytes_accessed=1000, transcendentals=0),
            name="early",
        )(*given)
    return pl.pallas_call(
        late_kernel,
        in_specs=in_specs + [vmem],
        out_specs=pl.BlockSpec(memory_space=pltpu.HBM),
        out_shape=jax.ShapeDtypeStruct((2, half, dofs), jnp.bfloat16),
        scratch_shapes=scratch
        + [pltpu.VMEM((2, half, dofs), jnp.bfloat16), pltpu.SemaphoreType.DMA((8,))],
        compiler_params=params,
        cost_estimate=cost,
        name="late",
    )(*given, waves)


def add_kernel(ours_ref, came_ref, out_ref):
    total = ours_ref[...].astype(jnp.float32) + came_ref[...].astype(jnp.float32)
    out_ref[...] = total.astype(jnp.bfloat16)


def add(ours, came):
    vmem = pl.BlockSpec(memory_space=pltpu.VMEM)
    return pl.pallas_call(
        add_kernel,
        in_specs=[vmem] * 2,
        out_specs=vmem,
        out_shape=jax.ShapeDtypeStruct(ours.shape, jnp.bfloat16),
        compiler_params=pltpu.CompilerParams(vmem_limit_bytes=8 * MIB),
        cost_estimate=pl.CostEstimate(
            flops=came.size, bytes_accessed=6 * came.size, transcendentals=0
        ),
        name="add",
    )(ours, came)


def gather_sum_kernel(came_ref, after_ref, *refs):
    within_refs, out_refs = refs[:4], refs[4:]
    for k, out_ref in enumerate(out_refs):
        for parity in range(2):
            keep_ref, twin_ref = within_refs[2 * parity : 2 * parity + 2]
            total = keep_ref[k, 0].astype(jnp.float32) + twin_ref[k, 0].astype(jnp.float32)
            total = total + came_ref[k, parity].astype(jnp.float32)
            out_ref[0, parity] = total.astype(jnp.bfloat16)


def gather_sum(came, kept, after):
    vmem = pl.BlockSpec(memory_space=pltpu.VMEM)
    zs = came.shape[0]
    return pl.pallas_call(
        gather_sum_kernel,
        in_specs=[vmem, pl.BlockSpec(memory_space=pl.ANY)] + [vmem] * 4,
        out_specs=[vmem] * zs,
        out_shape=[jax.ShapeDtypeStruct((1,) + came.shape[1:], jnp.bfloat16)] * zs,
        compiler_params=pltpu.CompilerParams(vmem_limit_bytes=8 * MIB),
        cost_estimate=pl.CostEstimate(
            flops=2 * came.size, bytes_accessed=8 * came.size, transcendentals=0
        ),
        name="gather_sum",
    )(came, after, *kept)


def on_device(devices, forces, mode_shapes, frf):
    _, steps, dofs = forces.shape
    half = steps // 2
    chips = devices // CORES
    zs = chips // 2

    def swap(values, distance):
        pairs = [(i, i ^ distance) for i in range(devices)]
        return lax.ppermute(values, "dof", pairs)

    index = lax.axis_index("dof")
    place = jnp.stack([index % CORES, index // CORES]).astype(jnp.int32)
    shapes_t = mode_shapes.T
    fwd = jnp.asarray(forward_tables(steps, chips).astype(jnp.bfloat16))
    inv = jnp.asarray(inverse_tables(steps, chips).astype(jnp.bfloat16))

    unit = frf.shape[0] // 8
    keep, send, folded, rest, shapes_v = across(
        place, fwd, forces.reshape(2, half, dofs), shapes_t, zs
    )
    given = (place, rest, folded, shapes_v, frf)
    keep0, send0, part0 = within(0, *given, 0, unit, send, zs)
    pair = add(keep, swap(send, 1))
    came = swap(pair, 2)
    keep1, send1, part1 = within(1, *given, unit, unit, pair, zs)
    part2 = load(frf, 2 * unit, 3 * unit, send1)
    pieces = gather_sum(came, (keep0, swap(send0, 1), keep1, swap(send1, 1)), part2)
    part3 = load(frf, 5 * unit, 3 * unit, pieces[0])
    pieces = [pieces[0]] + [swap(pieces[k], 4 * k) for k in range(1, zs)]
    response = respond(pieces, (part0, part1, part2, part3))

    over = swap(response[None], 2)
    shards = [swap(response, 4 * k) for k in range(1, zs)]
    far, over = lax.optimization_barrier((jnp.stack(shards), over))
    over_far = swap(far, 2)
    own = jnp.concatenate([response[None], far])
    twin, twin_over = swap(own, 1), swap(over, 1)
    waves = inverse(place, inv, shapes_v, (own, twin))
    over_far, waves = lax.optimization_barrier((over_far, waves))
    out = inverse(place, inv, shapes_v, (over, twin_over, over_far, swap(over_far, 1)), waves)
    return out.reshape(1, steps, dofs)


def solution(mesh):
    devices = mesh.shape["dof"]
    return jax.shard_map(
        functools.partial(on_device, devices),
        mesh=mesh,
        in_specs=(P("grp", None, "dof"), P("dof", None), P("dof", None, None, None)),
        out_specs=P("grp", None, "dof"),
        check_vma=False,
    )
```

```python
import functools
import math

import jax
import jax.numpy as jnp
import numpy as np
from jax import lax
from jax.experimental import pallas as pl
from jax.experimental.pallas import tpu as pltpu
from jax.sharding import PartitionSpec as P

FREQS = 512
CORES = 2
CHUNK = 512
MIB = 1 << 20


def frequency_order(chips, parity):
    mine = FREQS // (chips * CORES)
    owned = np.arange(FREQS).reshape(chips // 2, 2, CORES, mine // 2, 2)
    return owned[..., parity].transpose(1, 2, 0, 3).reshape(-1)


def signed_tables(steps, chips):
    times = np.arange(steps // 2, dtype=np.int64)
    tables = []
    for parity in range(2):
        ids = frequency_order(chips, parity)
        angle = (ids[:, None] * times[None, :] % steps) * (2.0 * math.pi / steps)
        table = np.stack([np.cos(angle), -np.sin(angle)], axis=1) / math.sqrt(steps)
        tables.append(table.reshape(2, FREQS // 2, steps // 2))
    return np.stack(tables)


def forward_tables(steps, chips):
    return signed_tables(steps, chips).reshape(2, FREQS, steps // 2)


def inverse_tables(steps, chips):
    tables = signed_tables(steps, chips) * 2.0
    for parity in range(2):
        weights = np.where(frequency_order(chips, parity) == 0, 0.5, 1.0)
        tables[parity] *= np.repeat(weights, 2).reshape(2, FREQS // 2, 1)
    return tables.transpose(1, 0, 3, 2)


def chunk_list(half):
    unit = half // 8
    sizes = (unit, unit, 2 * unit, 2 * unit, 2 * unit)
    return tuple((sum(sizes[:n]), size) for n, size in enumerate(sizes))


def split_cores(place_ref, spec_ref, shapes_ref, keep_ref, send_ref):
    _, zs, rows, modes = keep_ref.shape
    first, y, z = place_ref[0] == 0, place_ref[1] % 2, place_ref[1] // 2
    spec = lax.dot_general(
        spec_ref[...].astype(jnp.bfloat16),
        shapes_ref[...],
        (((1,), (1,)), ((), ())),
        preferred_element_type=jnp.float32,
    ).reshape(2, CORES, zs, rows, modes)
    for j in range(2):
        keep = jnp.where(first, spec[j, 0], spec[j, 1]).astype(jnp.bfloat16)
        send = jnp.where(first, spec[j, 1], spec[j, 0]).astype(jnp.bfloat16)
        for k in range(zs):
            keep_ref[y ^ j, z ^ k] = keep[k]
            send_ref[y ^ j, z ^ k] = send[k]


def add_product(acc_ref, first, table, steps):
    part = jnp.dot(table, steps, preferred_element_type=jnp.float32)
    if first:
        acc_ref[...] = part
    else:
        acc_ref[...] += part


def even_kernel(
    place_ref, table_ref, forces_ref, shapes_ref,
    keep_ref, send_ref, odd_ref, rest_ref, shapes_buf,
    table_buf, forces_buf, acc_ref, table_sem, forces_sem, rest_sem, shapes_sem,
):
    chunks = chunk_list(forces_ref.shape[1])
    copies = []
    for n, (start, size) in enumerate(chunks):
        part = pl.ds(start, size)
        pair = (
            pltpu.make_async_copy(
                forces_ref.at[:, part], forces_buf.at[:, part], forces_sem.at[n]
            ),
            pltpu.make_async_copy(
                table_ref.at[0, :, part], table_buf.at[:, part], table_sem.at[n]
            ),
        )
        for copy in pair:
            copy.start()
        copies.append(pair)
    later = (
        pltpu.make_async_copy(shapes_ref, shapes_buf, shapes_sem),
        pltpu.make_async_copy(table_ref.at[1], rest_ref, rest_sem),
    )
    for copy in later:
        copy.start()

    for n, (start, size) in enumerate(chunks):
        part = slice(start, start + size)
        for copy in copies[n]:
            copy.wait()
        low, high = forces_buf[0, part], forces_buf[1, part]
        odd_ref[part] = low - high
        add_product(acc_ref, n == 0, table_buf[:, part], low + high)

    later[0].wait()
    split_cores(place_ref, acc_ref, shapes_buf, keep_ref, send_ref)
    later[1].wait()


def even_spectra(place, table, forces, shapes_t, zs):
    _, half, dofs = forces.shape
    modes = shapes_t.shape[0]
    rows = FREQS // (2 * CORES * zs)
    out = jax.ShapeDtypeStruct((2, zs, rows, modes), jnp.bfloat16)
    vmem, hbm = pl.BlockSpec(memory_space=pltpu.VMEM), pl.BlockSpec(memory_space=pltpu.HBM)
    count = len(chunk_list(half))
    return pl.pallas_call(
        even_kernel,
        in_specs=[pl.BlockSpec(memory_space=pltpu.SMEM), hbm, hbm, hbm],
        out_specs=[vmem] * 5,
        out_shape=[
            out,
            out,
            pltpu.VMEM((half, dofs), jnp.bfloat16),
            pltpu.VMEM((FREQS, half), jnp.bfloat16),
            pltpu.VMEM(shapes_t.shape, jnp.bfloat16),
        ],
        scratch_shapes=[
            pltpu.VMEM((FREQS, half), jnp.bfloat16),
            pltpu.VMEM(forces.shape, jnp.bfloat16),
            pltpu.VMEM((FREQS, dofs), jnp.float32),
            pltpu.SemaphoreType.DMA((count,)),
            pltpu.SemaphoreType.DMA((count,)),
            pltpu.SemaphoreType.DMA,
            pltpu.SemaphoreType.DMA,
        ],
        compiler_params=pltpu.CompilerParams(vmem_limit_bytes=20 * MIB),
        cost_estimate=pl.CostEstimate(
            flops=2 * FREQS * dofs * (half + modes), bytes_accessed=12 * MIB, transcendentals=0
        ),
        name="even_spectra",
    )(place, in_hbm(table), in_hbm(forces), in_hbm(shapes_t))


def odd_sum_kernel(begin, end, start, table_ref, odd_ref, frf_ref, before_ref, after_ref,
                   acc_ref, held_ref, sem):
    copies = load_copies(start, frf_ref, held_ref, sem)
    for copy in copies:
        copy.start()
    for first in range(begin, end, CHUNK):
        part = slice(first, first + CHUNK)
        add_product(acc_ref, first == begin, table_ref[:, part], odd_ref[part])
    if begin > 0:
        acc_ref[...] += before_ref[...]
    for copy in copies:
        copy.wait()


def odd_sum(table, odd, frf, begin, end, start, held, before, after):
    dofs = odd.shape[1]
    vmem, hbm = pl.BlockSpec(memory_space=pltpu.VMEM), pl.BlockSpec(memory_space=pltpu.HBM)
    anywhere = pl.BlockSpec(memory_space=pl.ANY)
    return pl.pallas_call(
        functools.partial(odd_sum_kernel, begin, end, start),
        in_specs=[vmem, vmem, hbm, vmem if begin > 0 else anywhere, anywhere],
        out_specs=[vmem] * 2,
        out_shape=[
            pltpu.VMEM((FREQS, dofs), jnp.float32),
            pltpu.VMEM((held,) + frf.shape[1:], jnp.bfloat16),
        ],
        scratch_shapes=[pltpu.SemaphoreType.DMA((math.gcd(held, 4),))],
        compiler_params=pltpu.CompilerParams(vmem_limit_bytes=8 * MIB),
        cost_estimate=pl.CostEstimate(
            flops=2 * FREQS * dofs * (end - begin), bytes_accessed=8 * MIB, transcendentals=0
        ),
        name="odd_sum",
    )(table, odd, in_hbm(frf), before, after)


def odd_modes_kernel(place_ref, acc_ref, shapes_ref, after_ref, keep_ref, send_ref):
    split_cores(place_ref, acc_ref, shapes_ref, keep_ref, send_ref)


def odd_modes(place, sums, shapes_t, zs, after):
    modes, dofs = shapes_t.shape
    rows = FREQS // (2 * CORES * zs)
    vmem = pl.BlockSpec(memory_space=pltpu.VMEM)
    out = jax.ShapeDtypeStruct((2, zs, rows, modes), jnp.bfloat16)
    return pl.pallas_call(
        odd_modes_kernel,
        in_specs=[pl.BlockSpec(memory_space=pltpu.SMEM), vmem, vmem]
        + [pl.BlockSpec(memory_space=pl.ANY)],
        out_specs=[vmem] * 2,
        out_shape=[out, out],
        compiler_params=pltpu.CompilerParams(vmem_limit_bytes=8 * MIB),
        cost_estimate=pl.CostEstimate(
            flops=2 * FREQS * dofs * modes, bytes_accessed=3 * MIB, transcendentals=0
        ),
        name="odd_modes",
    )(place, sums, shapes_t, after)


def in_hbm(array):
    return pltpu.with_memory_space_constraint(array, pltpu.HBM)


def load_copies(start, frf_ref, held_ref, sem):
    count = sem.shape[0]
    size = held_ref.shape[0] // count
    return [
        pltpu.make_async_copy(
            frf_ref.at[pl.ds(start + n * size, size)],
            held_ref.at[pl.ds(n * size, size)],
            sem.at[n],
        )
        for n in range(count)
    ]


def load_kernel(start, frf_ref, after_ref, held_ref, sem):
    copies = load_copies(start, frf_ref, held_ref, sem)
    for copy in copies:
        copy.start()
    for copy in copies:
        copy.wait()


def load(frf, start, size, after, weight=4):
    hbm, anywhere = pl.BlockSpec(memory_space=pltpu.HBM), pl.BlockSpec(memory_space=pl.ANY)
    return pl.pallas_call(
        functools.partial(load_kernel, start),
        in_specs=[hbm, anywhere],
        out_specs=pl.BlockSpec(memory_space=pltpu.VMEM),
        out_shape=pltpu.VMEM((size,) + frf.shape[1:], jnp.bfloat16),
        scratch_shapes=[pltpu.SemaphoreType.DMA((math.gcd(size, 4),))],
        compiler_params=pltpu.CompilerParams(vmem_limit_bytes=2 * MIB),
        cost_estimate=pl.CostEstimate(
            flops=0, bytes_accessed=weight * size * math.prod(frf.shape[1:]), transcendentals=0
        ),
        name="load",
    )(in_hbm(frf), after)


def respond_kernel(count, *refs):
    pieces, parts = refs[:count], refs[count:-4]
    out_ref, direct_ref, turned_ref, result_ref = refs[-4:]
    _, rows, modes = out_ref.shape
    total = sum(piece[...].astype(jnp.float32) for piece in pieces).reshape(2 * rows, modes)
    total = total.astype(jnp.bfloat16).astype(jnp.float32)
    row = lax.broadcasted_iota(jnp.int32, total.shape, 0)
    turned = jnp.where(row % 2 == 0, -jnp.roll(total, -1, axis=0), jnp.roll(total, 1, axis=0))

    def place(f):
        return (f % 2) * rows + f // 2 * 2

    direct_ref[...] = jnp.zeros_like(direct_ref)
    turned_ref[...] = jnp.zeros_like(turned_ref)
    for f in range(rows):
        at = place(f)
        direct_ref[f, 0:2] = total[at : at + 2]
        turned_ref[f, 0:2] = turned[at : at + 2]
    base = 0
    for part in parts:

        @pl.loop(0, part.shape[0], unroll=math.gcd(4, part.shape[0]))
        def _(step, part=part, base=base):
            f = base + step
            products = [
                lax.dot_general(
                    ref[f].astype(jnp.bfloat16),
                    part[step, which],
                    (((1,), (1,)), ((), ())),
                    preferred_element_type=jnp.float32,
                )
                for which, ref in enumerate((direct_ref, turned_ref))
            ]
            result_ref[f] = products[0] + products[1]

        base += part.shape[0]

    for f in range(rows):
        at = place(f)
        direct_ref[at // 8, at % 8 : at % 8 + 2] = result_ref[f, 0:2]
    out_ref[...] = (
        direct_ref[: 2 * rows // 8].reshape(2, rows, modes).astype(jnp.bfloat16)
    )


def respond(pieces, parts):
    rows, modes = pieces[0].shape[1:]
    vmem = pl.BlockSpec(memory_space=pltpu.VMEM)
    size = sum(part.size for part in parts)
    return pl.pallas_call(
        functools.partial(respond_kernel, len(pieces)),
        in_specs=[vmem] * (len(pieces) + len(parts)),
        out_specs=vmem,
        out_shape=jax.ShapeDtypeStruct((2, rows, modes), jnp.bfloat16),
        scratch_shapes=[pltpu.VMEM((rows, 8, modes), jnp.float32)] * 3,
        compiler_params=pltpu.CompilerParams(vmem_limit_bytes=12 * MIB),
        cost_estimate=pl.CostEstimate(flops=4 * size, bytes_accessed=2 * size, transcendentals=0),
        name="respond",
    )(*pieces, *parts)


def project(place_ref, shards, shapes_ref, order_ref, moved_ref):
    _, _, zs, rows, modes = order_ref.shape
    core, z = place_ref[0], place_ref[1] // 2
    start = 0
    for own_ref, twin_ref in zip(shards[::2], shards[1::2]):
        for far, shard_ref in enumerate((own_ref, twin_ref)):
            for k in range(shard_ref.shape[0]):
                for parity in range(2):
                    order_ref[parity, core ^ far, z ^ (start + k)] = shard_ref[
                        k, parity
                    ].astype(jnp.float32)
        start += own_ref.shape[0]
    for parity in range(2):
        moved_ref[parity] = jnp.dot(
            order_ref[parity].reshape(FREQS // 2, modes).astype(jnp.bfloat16),
            shapes_ref[...],
            preferred_element_type=jnp.float32,
        ).astype(jnp.bfloat16)


def early_kernel(place_ref, table_ref, shapes_ref, *refs):
    shards, (waves_ref, order_ref, moved_ref) = refs[:-3], refs[-3:]
    project(place_ref, shards, shapes_ref, order_ref, moved_ref)
    y = place_ref[1] % 2
    block = 2 * CHUNK
    for start in range(0, waves_ref.shape[1], block):
        part = slice(start, start + block)
        for parity in range(2):
            waves_ref[parity, part] = jnp.dot(
                table_ref[y, parity, part], moved_ref[parity], preferred_element_type=jnp.float32
            )


def late_kernel(place_ref, table_ref, shapes_ref, *refs):
    shards, (waves_ref, out_ref, order_ref, moved_ref, out_buf, out_sem) = refs[:-6], refs[-6:]
    project(place_ref, shards, shapes_ref, order_ref, moved_ref)
    y = (place_ref[1] % 2) ^ 1
    count = out_sem.shape[0]
    block = out_ref.shape[1] // count

    def copy_out(step):
        part = pl.ds(step * block, block)
        return pltpu.make_async_copy(
            out_buf.at[:, part], out_ref.at[:, part], out_sem.at[step]
        )

    for step in range(count):
        part = slice(step * block, (step + 1) * block)
        even, odd = (
            waves_ref[parity, part]
            + jnp.dot(
                table_ref[y, parity, part], moved_ref[parity], preferred_element_type=jnp.float32
            )
            for parity in range(2)
        )
        out_buf[0, part] = (even + odd).astype(jnp.bfloat16)
        out_buf[1, part] = (even - odd).astype(jnp.bfloat16)
        copy_out(step).start()

    for step in range(count):
        copy_out(step).wait()


def inverse(place, table, shapes_t, shards, waves=None):
    half = table.shape[2]
    modes, dofs = shapes_t.shape
    rows = shards[0].shape[2]
    zs = sum(shard.shape[0] for shard in shards) // 2
    vmem = pl.BlockSpec(memory_space=pltpu.VMEM)
    scratch = [
        pltpu.VMEM((2, CORES, zs, rows, modes), jnp.float32),
        pltpu.VMEM((2, FREQS // 2, dofs), jnp.bfloat16),
    ]
    given = (place, table, shapes_t) + shards
    in_specs = [pl.BlockSpec(memory_space=pltpu.SMEM)] + [vmem] * (len(given) - 1)
    params = pltpu.CompilerParams(vmem_limit_bytes=20 * MIB)
    cost = pl.CostEstimate(
        flops=2 * FREQS * dofs * (half + modes), bytes_accessed=8 * MIB, transcendentals=0
    )
    if waves is None:
        return pl.pallas_call(
            early_kernel,
            in_specs=in_specs,
            out_specs=vmem,
            out_shape=pltpu.VMEM((2, half, dofs), jnp.float32),
            scratch_shapes=scratch,
            compiler_params=params,
            cost_estimate=pl.CostEstimate(flops=1000, bytes_accessed=1000, transcendentals=0),
            name="early",
        )(*given)
    return pl.pallas_call(
        late_kernel,
        in_specs=in_specs + [vmem],
        out_specs=pl.BlockSpec(memory_space=pltpu.HBM),
        out_shape=jax.ShapeDtypeStruct((2, half, dofs), jnp.bfloat16),
        scratch_shapes=scratch
        + [pltpu.VMEM((2, half, dofs), jnp.bfloat16), pltpu.SemaphoreType.DMA((half // CHUNK,))],
        compiler_params=params,
        cost_estimate=cost,
        name="late",
    )(*given, waves)


def add_kernel(count, ours_ref, came_ref, *refs):
    out_refs = refs[count:]
    for n, out_ref in enumerate(out_refs):
        total = ours_ref[n].astype(jnp.float32) + came_ref[n].astype(jnp.float32)
        out_ref[...] = total.astype(jnp.bfloat16)


def add(ours, came, *after):
    vmem = pl.BlockSpec(memory_space=pltpu.VMEM)
    return pl.pallas_call(
        functools.partial(add_kernel, len(after)),
        in_specs=[vmem] * 2 + [pl.BlockSpec(memory_space=pl.ANY)] * len(after),
        out_specs=[vmem] * ours.shape[0],
        out_shape=[jax.ShapeDtypeStruct(ours.shape[1:], jnp.bfloat16)] * ours.shape[0],
        compiler_params=pltpu.CompilerParams(vmem_limit_bytes=8 * MIB),
        cost_estimate=pl.CostEstimate(
            flops=came.size, bytes_accessed=6 * came.size, transcendentals=0
        ),
        name="add",
    )(ours, came, *after)


def gather_sum_kernel(after_ref, *refs):
    pairs, out_refs = refs[:4], refs[4:]
    for k, out_ref in enumerate(out_refs):
        for parity in range(2):
            ours_ref, came_ref = pairs[2 * parity : 2 * parity + 2]
            total = ours_ref[k].astype(jnp.float32) + came_ref[k].astype(jnp.float32)
            out_ref[parity] = total.astype(jnp.bfloat16)


def gather_sum(pairs, after):
    vmem = pl.BlockSpec(memory_space=pltpu.VMEM)
    zs, rows, modes = pairs[0].shape
    return pl.pallas_call(
        gather_sum_kernel,
        in_specs=[pl.BlockSpec(memory_space=pl.ANY)] + [vmem] * 4,
        out_specs=[vmem] * zs,
        out_shape=[jax.ShapeDtypeStruct((2, rows, modes), jnp.bfloat16)] * zs,
        compiler_params=pltpu.CompilerParams(vmem_limit_bytes=8 * MIB),
        cost_estimate=pl.CostEstimate(
            flops=pairs[0].size, bytes_accessed=12 * pairs[0].size, transcendentals=0
        ),
        name="gather_sum",
    )(after, *pairs)


def on_device(devices, forces, mode_shapes, frf):
    _, steps, dofs = forces.shape
    half = steps // 2
    chips = devices // CORES
    zs = chips // 2

    def swap(values, distance):
        pairs = [(i, i ^ distance) for i in range(devices)]
        return lax.ppermute(values, "dof", pairs)

    index = lax.axis_index("dof")
    place = jnp.stack([index % CORES, index // CORES]).astype(jnp.int32)
    shapes_t = mode_shapes.T
    fwd = jnp.asarray(forward_tables(steps, chips).astype(jnp.bfloat16))
    inv = jnp.asarray(inverse_tables(steps, chips).astype(jnp.bfloat16))

    unit = frf.shape[0] // 8
    keep, send, odd, rest, shapes_v = even_spectra(
        place, fwd, forces.reshape(2, half, dofs), shapes_t, zs
    )
    sums, part0 = odd_sum(rest, odd, frf, 0, CHUNK, 0, unit, shapes_v, keep)
    here, there = add(keep, swap(send, 1), part0)
    came = swap(there, 2)
    sums, part1 = odd_sum(rest, odd, frf, CHUNK, half, unit, unit, sums, there)
    odd_keep, odd_send = odd_modes(place, sums, shapes_v, zs, came)
    part2 = load(frf, 2 * unit, unit, odd_send)
    odd_here, odd_there = add(odd_keep, swap(odd_send, 1), part2)
    part3 = load(frf, 3 * unit, 2 * unit, odd_there)
    pieces = gather_sum((here, came, odd_here, swap(odd_there, 2)), part3)
    part4 = load(frf, 5 * unit, 3 * unit, pieces[0])
    pieces = [pieces[0]] + [swap(pieces[k], 4 * k) for k in range(1, zs)]
    response = respond(pieces, (part0, part1, part2, part3, part4))

    over = swap(response[None], 2)
    shards = [swap(response, 4 * k) for k in range(1, zs)]
    far, over = lax.optimization_barrier((jnp.stack(shards), over))
    over_far = swap(far, 2)
    own = jnp.concatenate([response[None], far])
    twin, twin_over = swap(own, 1), swap(over, 1)
    waves = inverse(place, inv, shapes_v, (own, twin))
    over_far, waves = lax.optimization_barrier((over_far, waves))
    out = inverse(place, inv, shapes_v, (over, twin_over, over_far, swap(over_far, 1)), waves)
    return out.reshape(1, steps, dofs)


def solution(mesh):
    devices = mesh.shape["dof"]
    return jax.shard_map(
        functools.partial(on_device, devices),
        mesh=mesh,
        in_specs=(P("grp", None, "dof"), P("dof", None), P("dof", None, None, None)),
        out_specs=P("grp", None, "dof"),
        check_vma=False,
    )
```

```python
import functools
import math

import jax
import jax.numpy as jnp
import numpy as np
from jax import lax
from jax.experimental import pallas as pl
from jax.experimental.pallas import tpu as pltpu
from jax.sharding import PartitionSpec as P

FREQS = 512
CORES = 2
CHUNK = 512
MIB = 1 << 20


def frequency_order(chips, parity):
    mine = FREQS // (chips * CORES)
    owned = np.arange(FREQS).reshape(chips // 2, 2, CORES, mine // 2, 2)
    return owned[..., parity].transpose(1, 2, 0, 3).reshape(-1)


def forward_tables(steps, chips):
    times = np.arange(steps // 2, dtype=np.int64)
    tables = []
    for parity in range(2):
        ids = frequency_order(chips, parity)
        angle = (ids[:, None] * times[None, :] % steps) * (2.0 * math.pi / steps)
        table = np.stack([np.cos(angle), -np.sin(angle)], axis=1) / math.sqrt(steps)
        tables.append(table.reshape(FREQS, steps // 2))
    return np.stack(tables).reshape(2, 2, FREQS // 2, steps // 2)


def inverse_tables(steps, chips):
    tables = forward_tables(steps, chips) * 2.0
    for parity in range(2):
        weights = np.where(frequency_order(chips, parity) == 0, 0.5, 1.0)
        tables[parity] *= np.repeat(weights, 2).reshape(2, FREQS // 2, 1)
    return tables.transpose(0, 1, 3, 2)


def chunk_list(half):
    unit = half // 8
    sizes = (unit, unit, 2 * unit, 2 * unit, 2 * unit)
    return tuple((sum(sizes[:n]), size) for n, size in enumerate(sizes))


def split_cores(place_ref, spec, shapes_ref, parity, keep_ref, send_ref):
    zs, _, rows, modes = keep_ref.shape
    first, z = place_ref[0] == 0, place_ref[1] // 2
    spec = lax.dot_general(
        spec.astype(jnp.bfloat16),
        shapes_ref[...],
        (((1,), (1,)), ((), ())),
        preferred_element_type=jnp.float32,
    ).reshape(CORES, zs, rows, modes)
    keep = jnp.where(first, spec[0], spec[1]).astype(jnp.bfloat16)
    send = jnp.where(first, spec[1], spec[0]).astype(jnp.bfloat16)
    for k in range(zs):
        keep_ref[z ^ k, parity] = keep[k]
        if len(send_ref.shape) == 3:
            send_ref[z ^ k] = send[k]
        else:
            send_ref[z ^ k, parity] = send[k]


def across_kernel(
    place_ref, table_ref, forces_ref, shapes_ref,
    keep_ref, send_ref, folded_ref, rest_ref, shapes_buf,
    table_buf, forces_buf, acc_ref, table_sem, forces_sem, rest_sem, shapes_sem,
):
    y = place_ref[1] % 2
    chunks = chunk_list(forces_ref.shape[1])
    copies = []
    for n, (start, size) in enumerate(chunks):
        part = pl.ds(start, size)
        pair = (
            pltpu.make_async_copy(
                forces_ref.at[:, part], forces_buf.at[:, part], forces_sem.at[n]
            ),
            pltpu.make_async_copy(
                table_ref.at[:, y ^ 1, :, part], table_buf.at[:, :, part], table_sem.at[n]
            ),
        )
        for copy in pair:
            copy.start()
        copies.append(pair)
    later = (
        pltpu.make_async_copy(shapes_ref, shapes_buf, shapes_sem),
        pltpu.make_async_copy(table_ref.at[:, y], rest_ref, rest_sem),
    )
    for copy in later:
        copy.start()

    for n, (start, size) in enumerate(chunks):
        for copy in copies[n]:
            copy.wait()
        low = forces_buf[0, start : start + size]
        high = forces_buf[1, start : start + size]
        for parity, folded in enumerate((low + high, low - high)):
            folded_ref[parity, start : start + size] = folded
            part = jnp.dot(
                table_buf[parity, :, start : start + size],
                folded,
                preferred_element_type=jnp.float32,
            )
            if n == 0:
                acc_ref[parity] = part
            else:
                acc_ref[parity] += part

    later[0].wait()
    for parity in range(2):
        split_cores(place_ref, acc_ref[parity], shapes_buf, parity, keep_ref, send_ref)
    later[1].wait()


def across(place, table, forces, shapes_t, zs):
    _, half, dofs = forces.shape
    modes = shapes_t.shape[0]
    rows = FREQS // (2 * CORES * zs)
    out = jax.ShapeDtypeStruct((zs, 2, rows, modes), jnp.bfloat16)
    vmem, hbm = pl.BlockSpec(memory_space=pltpu.VMEM), pl.BlockSpec(memory_space=pltpu.HBM)
    count = len(chunk_list(half))
    return pl.pallas_call(
        across_kernel,
        in_specs=[pl.BlockSpec(memory_space=pltpu.SMEM), hbm, hbm, hbm],
        out_specs=[vmem] * 5,
        out_shape=[
            out,
            out,
            pltpu.VMEM(forces.shape, jnp.bfloat16),
            pltpu.VMEM((2, FREQS // 2, half), jnp.bfloat16),
            pltpu.VMEM(shapes_t.shape, jnp.bfloat16),
        ],
        scratch_shapes=[
            pltpu.VMEM((2, FREQS // 2, half), jnp.bfloat16),
            pltpu.VMEM(forces.shape, jnp.bfloat16),
            pltpu.VMEM((2, FREQS // 2, dofs), jnp.float32),
            pltpu.SemaphoreType.DMA((count,)),
            pltpu.SemaphoreType.DMA((count,)),
            pltpu.SemaphoreType.DMA,
            pltpu.SemaphoreType.DMA,
        ],
        compiler_params=pltpu.CompilerParams(vmem_limit_bytes=20 * MIB),
        cost_estimate=pl.CostEstimate(
            flops=2 * FREQS * dofs * (half + modes), bytes_accessed=12 * MIB, transcendentals=0
        ),
        name="across",
    )(place, in_hbm(table), in_hbm(forces), in_hbm(shapes_t))


def within_kernel(
    place_ref, table_ref, folded_ref, shapes_ref, frf_ref, after_ref,
    keep_ref, send0_ref, send1_ref, held_ref, acc_ref, sem,
):
    copies = load_copies(0, frf_ref, held_ref, sem)
    for copy in copies:
        copy.start()
    for parity in range(2):
        for first in range(0, folded_ref.shape[1], CHUNK):
            part = slice(first, first + CHUNK)
            product = jnp.dot(
                table_ref[parity, :, part],
                folded_ref[parity, part],
                preferred_element_type=jnp.float32,
            )
            if first == 0:
                acc_ref[parity] = product
            else:
                acc_ref[parity] += product
    for parity, send_ref in enumerate((send0_ref, send1_ref)):
        split_cores(place_ref, acc_ref[parity], shapes_ref, parity, keep_ref, send_ref)
    for copy in copies:
        copy.wait()


def within(place, table, folded, shapes_t, frf, held, after, zs):
    _, half, dofs = folded.shape
    modes = shapes_t.shape[0]
    rows = FREQS // (2 * CORES * zs)
    out = jax.ShapeDtypeStruct((zs, 2, rows, modes), jnp.bfloat16)
    send = jax.ShapeDtypeStruct((zs, rows, modes), jnp.bfloat16)
    vmem, hbm = pl.BlockSpec(memory_space=pltpu.VMEM), pl.BlockSpec(memory_space=pltpu.HBM)
    return pl.pallas_call(
        within_kernel,
        in_specs=[pl.BlockSpec(memory_space=pltpu.SMEM), vmem, vmem, vmem, hbm]
        + [pl.BlockSpec(memory_space=pl.ANY)],
        out_specs=[vmem] * 4,
        out_shape=[out, send, send, pltpu.VMEM((held,) + frf.shape[1:], jnp.bfloat16)],
        scratch_shapes=[
            pltpu.VMEM((2, FREQS // 2, dofs), jnp.float32),
            pltpu.SemaphoreType.DMA((math.gcd(held, 4),)),
        ],
        compiler_params=pltpu.CompilerParams(vmem_limit_bytes=10 * MIB),
        cost_estimate=pl.CostEstimate(
            flops=2 * FREQS * dofs * (half + modes), bytes_accessed=12 * MIB, transcendentals=0
        ),
        name="within",
    )(place, table, folded, shapes_t, in_hbm(frf), after)


def in_hbm(array):
    return pltpu.with_memory_space_constraint(array, pltpu.HBM)


def load_copies(start, frf_ref, held_ref, sem):
    count = sem.shape[0]
    size = held_ref.shape[0] // count
    return [
        pltpu.make_async_copy(
            frf_ref.at[pl.ds(start + n * size, size)],
            held_ref.at[pl.ds(n * size, size)],
            sem.at[n],
        )
        for n in range(count)
    ]


def load_kernel(start, frf_ref, after_ref, held_ref, sem):
    copies = load_copies(start, frf_ref, held_ref, sem)
    for copy in copies:
        copy.start()
    for copy in copies:
        copy.wait()


def load(frf, start, size, after, weight=4):
    hbm, anywhere = pl.BlockSpec(memory_space=pltpu.HBM), pl.BlockSpec(memory_space=pl.ANY)
    return pl.pallas_call(
        functools.partial(load_kernel, start),
        in_specs=[hbm, anywhere],
        out_specs=pl.BlockSpec(memory_space=pltpu.VMEM),
        out_shape=pltpu.VMEM((size,) + frf.shape[1:], jnp.bfloat16),
        scratch_shapes=[pltpu.SemaphoreType.DMA((math.gcd(size, 4),))],
        compiler_params=pltpu.CompilerParams(vmem_limit_bytes=2 * MIB),
        cost_estimate=pl.CostEstimate(
            flops=0, bytes_accessed=weight * size * math.prod(frf.shape[1:]), transcendentals=0
        ),
        name="load",
    )(in_hbm(frf), after)


def respond_kernel(count, *refs):
    pieces, parts = refs[:count], refs[count:-7]
    frf_ref, out_ref, direct_ref, turned_ref, result_ref, rest_ref, sem = refs[-7:]
    held = sum(part.shape[0] for part in parts)
    copies = load_copies(held, frf_ref, rest_ref, sem)
    for copy in copies:
        copy.start()
    _, rows, modes = out_ref.shape
    total = sum(piece[...].astype(jnp.float32) for piece in pieces).reshape(2 * rows, modes)
    total = total.astype(jnp.bfloat16).astype(jnp.float32)
    row = lax.broadcasted_iota(jnp.int32, total.shape, 0)
    turned = jnp.where(row % 2 == 0, -jnp.roll(total, -1, axis=0), jnp.roll(total, 1, axis=0))

    def place(f):
        return (f % 2) * rows + f // 2 * 2

    direct_ref[...] = jnp.zeros_like(direct_ref)
    turned_ref[...] = jnp.zeros_like(turned_ref)
    for f in range(rows):
        at = place(f)
        direct_ref[f, 0:2] = total[at : at + 2]
        turned_ref[f, 0:2] = turned[at : at + 2]

    def multiply(matrix_ref, step, f):
        products = [
            lax.dot_general(
                ref[f].astype(jnp.bfloat16),
                matrix_ref[step, which],
                (((1,), (1,)), ((), ())),
                preferred_element_type=jnp.float32,
            )
            for which, ref in enumerate((direct_ref, turned_ref))
        ]
        result_ref[f] = products[0] + products[1]

    base = 0
    for part in parts:

        @pl.loop(0, part.shape[0], unroll=math.gcd(4, part.shape[0]))
        def _(step, part=part, base=base):
            multiply(part, step, base + step)

        base += part.shape[0]

    each = rest_ref.shape[0] // len(copies)
    for n, copy in enumerate(copies):
        copy.wait()

        @pl.loop(n * each, (n + 1) * each, unroll=each)
        def _(step):
            multiply(rest_ref, step, held + step)

    for f in range(rows):
        at = place(f)
        direct_ref[at // 8, at % 8 : at % 8 + 2] = result_ref[f, 0:2]
    out_ref[...] = (
        direct_ref[: 2 * rows // 8].reshape(2, rows, modes).astype(jnp.bfloat16)
    )


def respond(pieces, parts, frf):
    rows, modes = pieces[0].shape[1:]
    vmem, hbm = pl.BlockSpec(memory_space=pltpu.VMEM), pl.BlockSpec(memory_space=pltpu.HBM)
    rest = frf.shape[0] - sum(part.shape[0] for part in parts)
    return pl.pallas_call(
        functools.partial(respond_kernel, len(pieces)),
        in_specs=[vmem] * (len(pieces) + len(parts)) + [hbm],
        out_specs=vmem,
        out_shape=jax.ShapeDtypeStruct((2, rows, modes), jnp.bfloat16),
        scratch_shapes=[pltpu.VMEM((rows, 8, modes), jnp.float32)] * 3
        + [
            pltpu.VMEM((rest,) + frf.shape[1:], jnp.bfloat16),
            pltpu.SemaphoreType.DMA((rest // math.gcd(rest, 4),)),
        ],
        compiler_params=pltpu.CompilerParams(vmem_limit_bytes=36 * MIB),
        cost_estimate=pl.CostEstimate(
            flops=4 * frf.size, bytes_accessed=2 * frf.size, transcendentals=0
        ),
        name="respond",
    )(*pieces, *parts, in_hbm(frf))


def project(place_ref, shards, shapes_ref, order_ref, moved_ref):
    _, _, zs, rows, modes = order_ref.shape
    core, z = place_ref[0], place_ref[1] // 2
    start = 0
    for own_ref, twin_ref in zip(shards[::2], shards[1::2]):
        for far, shard_ref in enumerate((own_ref, twin_ref)):
            for k in range(shard_ref.shape[0]):
                for parity in range(2):
                    order_ref[parity, core ^ far, z ^ (start + k)] = shard_ref[
                        k, parity
                    ].astype(jnp.float32)
        start += own_ref.shape[0]
    for parity in range(2):
        moved_ref[parity] = jnp.dot(
            order_ref[parity].reshape(FREQS // 2, modes).astype(jnp.bfloat16),
            shapes_ref[...],
            preferred_element_type=jnp.float32,
        ).astype(jnp.bfloat16)


def early_kernel(place_ref, table_ref, shapes_ref, *refs):
    shards, (waves_ref, order_ref, moved_ref) = refs[:-3], refs[-3:]
    project(place_ref, shards, shapes_ref, order_ref, moved_ref)
    y = place_ref[1] % 2
    block = waves_ref.shape[1] // 4
    for step in range(4):
        part = slice(step * block, (step + 1) * block)
        for parity in range(2):
            waves_ref[parity, part] = jnp.dot(
                table_ref[parity, y, part], moved_ref[parity], preferred_element_type=jnp.float32
            )


def late_kernel(place_ref, table_ref, shapes_ref, *refs):
    shards, (waves_ref, out_ref, order_ref, moved_ref, out_buf, out_sem) = refs[:-6], refs[-6:]
    project(place_ref, shards, shapes_ref, order_ref, moved_ref)
    y = (place_ref[1] % 2) ^ 1
    count = out_sem.shape[0]
    block = out_ref.shape[1] // count

    def copy_out(step):
        part = pl.ds(step * block, block)
        return pltpu.make_async_copy(
            out_buf.at[:, part], out_ref.at[:, part], out_sem.at[step]
        )

    for step in range(count):
        part = slice(step * block, (step + 1) * block)
        even, odd = (
            waves_ref[parity, part]
            + jnp.dot(
                table_ref[parity, y, part], moved_ref[parity], preferred_element_type=jnp.float32
            )
            for parity in range(2)
        )
        out_buf[0, part] = (even + odd).astype(jnp.bfloat16)
        out_buf[1, part] = (even - odd).astype(jnp.bfloat16)
        copy_out(step).start()
    for step in range(count):
        copy_out(step).wait()


def inverse(place, table, shapes_t, shards, waves=None):
    half = table.shape[2]
    modes, dofs = shapes_t.shape
    rows = shards[0].shape[2]
    zs = sum(shard.shape[0] for shard in shards) // 2
    vmem = pl.BlockSpec(memory_space=pltpu.VMEM)
    scratch = [
        pltpu.VMEM((2, CORES, zs, rows, modes), jnp.float32),
        pltpu.VMEM((2, FREQS // 2, dofs), jnp.bfloat16),
    ]
    given = (place, table, shapes_t) + shards
    in_specs = [pl.BlockSpec(memory_space=pltpu.SMEM)] + [vmem] * (len(given) - 1)
    params = pltpu.CompilerParams(vmem_limit_bytes=20 * MIB)
    cost = pl.CostEstimate(
        flops=2 * FREQS * dofs * (half + modes), bytes_accessed=8 * MIB, transcendentals=0
    )
    if waves is None:
        return pl.pallas_call(
            early_kernel,
            in_specs=in_specs,
            out_specs=vmem,
            out_shape=pltpu.VMEM((2, half, dofs), jnp.float32),
            scratch_shapes=scratch,
            compiler_params=params,
            cost_estimate=pl.CostEstimate(flops=1000, bytes_accessed=1000, transcendentals=0),
            name="early",
        )(*given)
    return pl.pallas_call(
        late_kernel,
        in_specs=in_specs + [vmem],
        out_specs=pl.BlockSpec(memory_space=pltpu.HBM),
        out_shape=jax.ShapeDtypeStruct((2, half, dofs), jnp.bfloat16),
        scratch_shapes=scratch
        + [pltpu.VMEM((2, half, dofs), jnp.bfloat16), pltpu.SemaphoreType.DMA((8,))],
        compiler_params=params,
        cost_estimate=cost,
        name="late",
    )(*given, waves)


def add_kernel(ours_ref, came_ref, out_ref):
    total = ours_ref[...].astype(jnp.float32) + came_ref[...].astype(jnp.float32)
    out_ref[...] = total.astype(jnp.bfloat16)


def add(ours, came):
    vmem = pl.BlockSpec(memory_space=pltpu.VMEM)
    return pl.pallas_call(
        add_kernel,
        in_specs=[vmem] * 2,
        out_specs=vmem,
        out_shape=jax.ShapeDtypeStruct(ours.shape, jnp.bfloat16),
        compiler_params=pltpu.CompilerParams(vmem_limit_bytes=8 * MIB),
        cost_estimate=pl.CostEstimate(
            flops=came.size, bytes_accessed=6 * came.size, transcendentals=0
        ),
        name="add",
    )(ours, came)


def gather_sum_kernel(came_ref, keep_ref, twin0_ref, twin1_ref, after_ref, *out_refs):
    for k, out_ref in enumerate(out_refs):
        for parity, twin_ref in enumerate((twin0_ref, twin1_ref)):
            total = keep_ref[k, parity].astype(jnp.float32) + twin_ref[k].astype(jnp.float32)
            total = total + came_ref[k, parity].astype(jnp.float32)
            out_ref[parity] = total.astype(jnp.bfloat16)


def gather_sum(came, keep, twin0, twin1, after):
    vmem = pl.BlockSpec(memory_space=pltpu.VMEM)
    zs = came.shape[0]
    return pl.pallas_call(
        gather_sum_kernel,
        in_specs=[vmem] * 4 + [pl.BlockSpec(memory_space=pl.ANY)],
        out_specs=[vmem] * zs,
        out_shape=[jax.ShapeDtypeStruct(came.shape[1:], jnp.bfloat16)] * zs,
        compiler_params=pltpu.CompilerParams(vmem_limit_bytes=8 * MIB),
        cost_estimate=pl.CostEstimate(
            flops=2 * came.size, bytes_accessed=8 * came.size, transcendentals=0
        ),
        name="gather_sum",
    )(came, keep, twin0, twin1, after)


def on_device(devices, forces, mode_shapes, frf):
    _, steps, dofs = forces.shape
    half = steps // 2
    chips = devices // CORES
    zs = chips // 2

    def swap(values, distance):
        pairs = [(i, i ^ distance) for i in range(devices)]
        return lax.ppermute(values, "dof", pairs)

    index = lax.axis_index("dof")
    place = jnp.stack([index % CORES, index // CORES]).astype(jnp.int32)
    shapes_t = mode_shapes.T
    fwd = jnp.asarray(forward_tables(steps, chips).astype(jnp.bfloat16))
    inv = jnp.asarray(inverse_tables(steps, chips).astype(jnp.bfloat16))

    keep, send, folded, rest, shapes_v = across(
        place, fwd, forces.reshape(2, half, dofs), shapes_t, zs
    )
    pair = add(keep, swap(send, 1))
    came = swap(pair, 2)
    unit = frf.shape[0] // 8
    keep, send0, send1, part0 = within(place, rest, folded, shapes_v, frf, 2 * unit, pair, zs)
    part1 = load(frf, 2 * unit, unit, send1)
    pieces = gather_sum(came, keep, swap(send0, 1), swap(send1, 1), part1)
    pieces = [pieces[0]] + [swap(pieces[k], 4 * k) for k in range(1, zs)]
    response = respond(pieces, (part0, part1), frf)

    over = swap(response[None], 2)
    shards = [swap(response, 4 * k) for k in range(1, zs)]
    far, over = lax.optimization_barrier((jnp.stack(shards), over))
    over_far = swap(far, 2)
    own = jnp.concatenate([response[None], far])
    twin, twin_over = swap(own, 1), swap(over, 1)
    waves = inverse(place, inv, shapes_v, (own, twin))
    over_far, waves = lax.optimization_barrier((over_far, waves))
    out = inverse(place, inv, shapes_v, (over, twin_over, over_far, swap(over_far, 1)), waves)
    return out.reshape(1, steps, dofs)


def solution(mesh):
    devices = mesh.shape["dof"]
    return jax.shard_map(
        functools.partial(on_device, devices),
        mesh=mesh,
        in_specs=(P("grp", None, "dof"), P("dof", None), P("dof", None, None, None)),
        out_specs=P("grp", None, "dof"),
        check_vma=False,
    )
```

```python
import functools
import math

import jax
import jax.numpy as jnp
import numpy as np
from jax import lax
from jax.experimental import pallas as pl
from jax.experimental.pallas import tpu as pltpu
from jax.sharding import PartitionSpec as P

FREQS = 512
CORES = 2
MIB = 1 << 20


def frequency_order(chips, parity):
    mine = FREQS // (chips * CORES)
    owned = np.arange(FREQS).reshape(chips // 2, 2, CORES, mine // 2, 2)
    return owned[..., parity].transpose(1, 2, 0, 3).reshape(-1)


def forward_tables(steps, chips):
    times = np.arange(steps // 2, dtype=np.int64)
    tables = []
    for parity in range(2):
        ids = frequency_order(chips, parity)
        angle = (ids[:, None] * times[None, :] % steps) * (2.0 * math.pi / steps)
        table = np.stack([np.cos(angle), -np.sin(angle)], axis=1) / math.sqrt(steps)
        tables.append(table.reshape(FREQS, steps // 2))
    return np.stack(tables)


def inverse_tables(steps, chips):
    tables = forward_tables(steps, chips) * 2.0
    for parity in range(2):
        weights = np.where(frequency_order(chips, parity) == 0, 0.5, 1.0)
        tables[parity] *= np.repeat(weights, 2)[:, None]
    return tables.reshape(2, 2, FREQS // 2, steps // 2).transpose(0, 1, 3, 2)


def chunk_list(half):
    unit = half // 8
    sizes = (unit, unit, 2 * unit, 2 * unit, 2 * unit)
    return tuple((sum(sizes[:n]), size) for n, size in enumerate(sizes))


def forward_kernel(
    place_ref, table_ref, forces_ref, shapes_ref, keep_ref, send_ref,
    table_buf, forces_buf, shapes_buf, acc_ref, table_sem, forces_sem, shapes_sem,
):
    _, zs, _, rows, modes = keep_ref.shape
    chunks = chunk_list(forces_ref.shape[1])
    copies = []
    for n, (start, size) in enumerate(chunks):
        part = pl.ds(start, size)
        pair = (
            pltpu.make_async_copy(
                forces_ref.at[:, part], forces_buf.at[:, part], forces_sem.at[n]
            ),
            pltpu.make_async_copy(
                table_ref.at[:, :, part], table_buf.at[:, :, part], table_sem.at[n]
            ),
        )
        for copy in pair:
            copy.start()
        copies.append(pair)
    shapes_copy = pltpu.make_async_copy(shapes_ref, shapes_buf, shapes_sem)
    shapes_copy.start()

    for n, (start, size) in enumerate(chunks):
        for copy in copies[n]:
            copy.wait()
        low = forces_buf[0, start : start + size]
        high = forces_buf[1, start : start + size]
        for parity, folded in enumerate((low + high, low - high)):
            part = jnp.dot(
                table_buf[parity, :, start : start + size],
                folded,
                preferred_element_type=jnp.float32,
            )
            if n == 0:
                acc_ref[parity] = part
            else:
                acc_ref[parity] += part

    shapes_copy.wait()
    first, chip = place_ref[0] == 0, place_ref[1]
    for parity in range(2):
        spec = lax.dot_general(
            acc_ref[parity].astype(jnp.bfloat16),
            shapes_buf[...],
            (((1,), (1,)), ((), ())),
            preferred_element_type=jnp.float32,
        ).reshape(2, CORES, zs, rows, modes)
        for y in range(2):
            keep = jnp.where(first, spec[y, 0], spec[y, 1]).astype(jnp.bfloat16)
            send = jnp.where(first, spec[y, 1], spec[y, 0]).astype(jnp.bfloat16)
            for z in range(zs):
                slot = chip ^ (2 * z + y)
                keep_ref[slot % 2, slot // 2, parity] = keep[z]
                send_ref[slot % 2, slot // 2, parity] = send[z]


def in_hbm(array):
    return pltpu.with_memory_space_constraint(array, pltpu.HBM)


def forward(place, table, forces, shapes_t, chips):
    _, half, dofs = forces.shape
    modes = shapes_t.shape[0]
    rows = FREQS // (chips * CORES)
    out = jax.ShapeDtypeStruct((2, chips // 2, 2, rows, modes), jnp.bfloat16)
    vmem, hbm = pl.BlockSpec(memory_space=pltpu.VMEM), pl.BlockSpec(memory_space=pltpu.HBM)
    count = len(chunk_list(half))
    return pl.pallas_call(
        forward_kernel,
        in_specs=[pl.BlockSpec(memory_space=pltpu.SMEM), hbm, hbm, hbm],
        out_specs=[vmem, vmem],
        out_shape=[out, out],
        scratch_shapes=[
            pltpu.VMEM(table.shape, jnp.bfloat16),
            pltpu.VMEM(forces.shape, jnp.bfloat16),
            pltpu.VMEM(shapes_t.shape, jnp.bfloat16),
            pltpu.VMEM((2, FREQS, dofs), jnp.float32),
            pltpu.SemaphoreType.DMA((count,)),
            pltpu.SemaphoreType.DMA((count,)),
            pltpu.SemaphoreType.DMA,
        ],
        compiler_params=pltpu.CompilerParams(vmem_limit_bytes=24 * MIB),
        cost_estimate=pl.CostEstimate(
            flops=4 * FREQS * dofs * (half + modes), bytes_accessed=12 * MIB, transcendentals=0
        ),
        name="forward",
    )(place, in_hbm(table), in_hbm(forces), in_hbm(shapes_t))


def load_copies(start, frf_ref, held_ref, sem):
    count = sem.shape[0]
    size = held_ref.shape[0] // count
    return [
        pltpu.make_async_copy(
            frf_ref.at[pl.ds(start + n * size, size)],
            held_ref.at[pl.ds(n * size, size)],
            sem.at[n],
        )
        for n in range(count)
    ]


def load_kernel(start, frf_ref, after_ref, held_ref, sem):
    copies = load_copies(start, frf_ref, held_ref, sem)
    for copy in copies:
        copy.start()
    for copy in copies:
        copy.wait()


def load(frf, start, size, after):
    hbm, anywhere = pl.BlockSpec(memory_space=pltpu.HBM), pl.BlockSpec(memory_space=pl.ANY)
    return pl.pallas_call(
        functools.partial(load_kernel, start),
        in_specs=[hbm, anywhere],
        out_specs=pl.BlockSpec(memory_space=pltpu.VMEM),
        out_shape=pltpu.VMEM((size,) + frf.shape[1:], jnp.bfloat16),
        scratch_shapes=[pltpu.SemaphoreType.DMA((math.gcd(size, 4),))],
        compiler_params=pltpu.CompilerParams(vmem_limit_bytes=2 * MIB),
        cost_estimate=pl.CostEstimate(
            flops=0, bytes_accessed=4 * size * math.prod(frf.shape[1:]), transcendentals=0
        ),
        name="load",
    )(in_hbm(frf), after)


def respond_kernel(count, *refs):
    pieces, parts = refs[:count], refs[count:-7]
    frf_ref, out_ref, direct_ref, turned_ref, result_ref, rest_ref, sem = refs[-7:]
    held = sum(part.shape[0] for part in parts)
    copies = load_copies(held, frf_ref, rest_ref, sem)
    for copy in copies:
        copy.start()
    _, rows, modes = out_ref.shape
    total = sum(piece[0].astype(jnp.float32) for piece in pieces).reshape(2 * rows, modes)
    total = total.astype(jnp.bfloat16).astype(jnp.float32)
    row = lax.broadcasted_iota(jnp.int32, total.shape, 0)
    turned = jnp.where(row % 2 == 0, -jnp.roll(total, -1, axis=0), jnp.roll(total, 1, axis=0))

    def place(f):
        return (f % 2) * rows + f // 2 * 2

    direct_ref[...] = jnp.zeros_like(direct_ref)
    turned_ref[...] = jnp.zeros_like(turned_ref)
    for f in range(rows):
        at = place(f)
        direct_ref[f, 0:2] = total[at : at + 2]
        turned_ref[f, 0:2] = turned[at : at + 2]

    def multiply(matrix_ref, step, f):
        products = [
            lax.dot_general(
                ref[f].astype(jnp.bfloat16),
                matrix_ref[step, which],
                (((1,), (1,)), ((), ())),
                preferred_element_type=jnp.float32,
            )
            for which, ref in enumerate((direct_ref, turned_ref))
        ]
        result_ref[f] = products[0] + products[1]

    base = 0
    for part in parts:

        @pl.loop(0, part.shape[0], unroll=math.gcd(4, part.shape[0]))
        def _(step, part=part, base=base):
            multiply(part, step, base + step)

        base += part.shape[0]

    each = rest_ref.shape[0] // len(copies)
    for n, copy in enumerate(copies):
        copy.wait()

        @pl.loop(n * each, (n + 1) * each, unroll=each)
        def _(step):
            multiply(rest_ref, step, held + step)

    for f in range(rows):
        at = place(f)
        direct_ref[at // 8, at % 8 : at % 8 + 2] = result_ref[f, 0:2]
    out_ref[...] = (
        direct_ref[: 2 * rows // 8].reshape(2, rows, modes).astype(jnp.bfloat16)
    )


def respond(pieces, parts, frf):
    rows, modes = pieces[0].shape[2:]
    vmem, hbm = pl.BlockSpec(memory_space=pltpu.VMEM), pl.BlockSpec(memory_space=pltpu.HBM)
    rest = frf.shape[0] - sum(part.shape[0] for part in parts)
    return pl.pallas_call(
        functools.partial(respond_kernel, len(pieces)),
        in_specs=[vmem] * (len(pieces) + len(parts)) + [hbm],
        out_specs=vmem,
        out_shape=jax.ShapeDtypeStruct((2, rows, modes), jnp.bfloat16),
        scratch_shapes=[pltpu.VMEM((rows, 8, modes), jnp.float32)] * 3
        + [
            pltpu.VMEM((rest,) + frf.shape[1:], jnp.bfloat16),
            pltpu.SemaphoreType.DMA((rest // math.gcd(rest, 4),)),
        ],
        compiler_params=pltpu.CompilerParams(vmem_limit_bytes=36 * MIB),
        cost_estimate=pl.CostEstimate(
            flops=4 * frf.size, bytes_accessed=2 * frf.size, transcendentals=0
        ),
        name="respond",
    )(*pieces, *parts, in_hbm(frf))


def project(place_ref, slots, shapes_ref, order_ref, moved_ref):
    _, _, zs, rows, modes = order_ref.shape
    core, z = place_ref[0], place_ref[1] // 2
    for shard_ref, n, far, k in slots:
        for parity in range(2):
            order_ref[parity, core ^ far, z ^ k] = shard_ref[n, parity].astype(jnp.float32)
    for parity in range(2):
        moved_ref[parity] = jnp.dot(
            order_ref[parity].reshape(FREQS // 2, modes).astype(jnp.bfloat16),
            shapes_ref[...],
            preferred_element_type=jnp.float32,
        ).astype(jnp.bfloat16)


def named_slots(plan, shards):
    return [(shards[which], n, far, k) for which, n, far, k in plan]


def early_kernel(plan, place_ref, table_ref, shapes_ref, *refs):
    shards, (waves_ref, order_ref, moved_ref) = refs[:-3], refs[-3:]
    project(place_ref, named_slots(plan, shards), shapes_ref, order_ref, moved_ref)
    y = place_ref[1] % 2
    block = waves_ref.shape[1] // 4
    for step in range(4):
        part = slice(step * block, (step + 1) * block)
        for parity in range(2):
            waves_ref[parity, part] = jnp.dot(
                table_ref[parity, y, part], moved_ref[parity], preferred_element_type=jnp.float32
            )


def late_kernel(plan, place_ref, table_ref, shapes_ref, *refs):
    shards, (waves_ref, out_ref, order_ref, moved_ref, out_buf, out_sem) = refs[:-6], refs[-6:]
    project(place_ref, named_slots(plan, shards), shapes_ref, order_ref, moved_ref)
    y = (place_ref[1] % 2) ^ 1
    count = out_sem.shape[0]
    block = out_ref.shape[1] // count

    def copy_out(step):
        part = pl.ds(step * block, block)
        return pltpu.make_async_copy(
            out_buf.at[:, part], out_ref.at[:, part], out_sem.at[step]
        )

    for step in range(count):
        part = slice(step * block, (step + 1) * block)
        even, odd = (
            waves_ref[parity, part]
            + jnp.dot(
                table_ref[parity, y, part], moved_ref[parity], preferred_element_type=jnp.float32
            )
            for parity in range(2)
        )
        out_buf[0, part] = (even + odd).astype(jnp.bfloat16)
        out_buf[1, part] = (even - odd).astype(jnp.bfloat16)
        copy_out(step).start()
    for step in range(count):
        copy_out(step).wait()


def inverse(place, table, shapes_t, shards, plan, waves=None):
    half = table.shape[2]
    modes, dofs = shapes_t.shape
    rows = shards[0].shape[2]
    zs = len(plan) // 2
    vmem = pl.BlockSpec(memory_space=pltpu.VMEM)
    scratch = [
        pltpu.VMEM((2, CORES, zs, rows, modes), jnp.float32),
        pltpu.VMEM((2, FREQS // 2, dofs), jnp.bfloat16),
    ]
    given = (place, table, shapes_t) + shards
    in_specs = [pl.BlockSpec(memory_space=pltpu.SMEM)] + [vmem] * (len(given) - 1)
    params = pltpu.CompilerParams(vmem_limit_bytes=20 * MIB)
    cost = pl.CostEstimate(
        flops=2 * FREQS * dofs * (half + modes), bytes_accessed=8 * MIB, transcendentals=0
    )
    if waves is None:
        return pl.pallas_call(
            functools.partial(early_kernel, plan),
            in_specs=in_specs,
            out_specs=vmem,
            out_shape=pltpu.VMEM((2, half, dofs), jnp.float32),
            scratch_shapes=scratch,
            compiler_params=params,
            cost_estimate=pl.CostEstimate(flops=1000, bytes_accessed=1000, transcendentals=0),
            name="early",
        )(*given)
    return pl.pallas_call(
        functools.partial(late_kernel, plan),
        in_specs=in_specs + [vmem],
        out_specs=pl.BlockSpec(memory_space=pltpu.HBM),
        out_shape=jax.ShapeDtypeStruct((2, half, dofs), jnp.bfloat16),
        scratch_shapes=scratch
        + [pltpu.VMEM((2, half, dofs), jnp.bfloat16), pltpu.SemaphoreType.DMA((8,))],
        compiler_params=params,
        cost_estimate=cost,
        name="late",
    )(*given, waves)


def add_kernel(start, splits, ours_ref, came_ref, after_ref, *out_refs):
    at = 0
    for size, out_ref in zip(splits, out_refs):
        for n in range(size):
            total = ours_ref[start + at + n].astype(jnp.float32) + came_ref[at + n].astype(
                jnp.float32
            )
            out_ref[n] = total.astype(jnp.bfloat16)
        at += size


def add(ours, came, start, splits, after):
    vmem, anywhere = pl.BlockSpec(memory_space=pltpu.VMEM), pl.BlockSpec(memory_space=pl.ANY)
    return pl.pallas_call(
        functools.partial(add_kernel, start, splits),
        in_specs=[vmem, vmem, anywhere],
        out_specs=[vmem] * len(splits),
        out_shape=[
            jax.ShapeDtypeStruct((size,) + ours.shape[1:], jnp.bfloat16) for size in splits
        ],
        compiler_params=pltpu.CompilerParams(vmem_limit_bytes=8 * MIB),
        cost_estimate=pl.CostEstimate(
            flops=came.size, bytes_accessed=6 * came.size, transcendentals=0
        ),
        name="add",
    )(ours, came, after)


def on_device(devices, forces, mode_shapes, frf):
    _, steps, dofs = forces.shape
    half = steps // 2
    chips = devices // CORES
    zs = chips // 2

    def swap(values, distance):
        pairs = [(i, i ^ distance) for i in range(devices)]
        return lax.ppermute(values, "dof", pairs)

    index = lax.axis_index("dof")
    place = jnp.stack([index % CORES, index // CORES]).astype(jnp.int32)
    shapes_t = mode_shapes.T
    fwd = jnp.asarray(forward_tables(steps, chips).astype(jnp.bfloat16))
    inv = jnp.asarray(inverse_tables(steps, chips).astype(jnp.bfloat16))

    unit = frf.shape[0] // 8
    keep, send = forward(place, fwd, forces.reshape(2, half, dofs), shapes_t, chips)
    slots = (2 * zs,) + keep.shape[2:]
    here, there_near, there_far = add(
        keep.reshape(slots), swap(send, 1).reshape(slots), 0, (zs, 1, zs - 1), send
    )
    came_far, came_near = swap(there_far, 2), swap(there_near, 2)
    part0 = load(frf, 0, 3 * unit, there_far)
    pieces = add(here, came_far, 1, (1,) * (zs - 1), part0)
    part1 = load(frf, 3 * unit, 3 * unit, pieces[0])
    came = [swap(piece, 4 * k) for k, piece in enumerate(pieces, 1)]
    response = respond([here[:1], came_near, *came], (part0, part1), frf)

    own = response[None]
    over = swap(own, 2)
    shards = [swap(response, 4 * k) for k in range(1, zs)]
    far, over = lax.optimization_barrier((jnp.stack(shards), over))
    over_far = swap(far, 2)
    cut = (zs - 1) // 2
    twin = swap(jnp.concatenate([own, over]), 1)
    twin_far = [swap(jnp.stack(shards[:-cut]), 1), swap(jnp.stack(shards[-cut:]), 1)]
    plan = [(0, 0, 0, 0), (2, 0, 1, 0)]
    for k in range(1, zs):
        at = k - 1
        plan += [(1, at, 0, k)]
        plan += [(3, at, 1, k) if at < zs - 1 - cut else (4, at - (zs - 1 - cut), 1, k)]
    waves = inverse(place, inv, shapes_t, (own, far, twin, *twin_far), plan)
    over_far, waves = lax.optimization_barrier((over_far, waves))
    plan = [(0, 0, 0, 0), (2, 1, 1, 0)]
    for k in range(1, zs):
        plan += [(1, k - 1, 0, k), (3, k - 1, 1, k)]
    out = inverse(place, inv, shapes_t, (over, over_far, twin, swap(over_far, 1)), plan, waves)
    return out.reshape(1, steps, dofs)


def solution(mesh):
    devices = mesh.shape["dof"]
    return jax.shard_map(
        functools.partial(on_device, devices),
        mesh=mesh,
        in_specs=(P("grp", None, "dof"), P("dof", None), P("dof", None, None, None)),
        out_specs=P("grp", None, "dof"),
        check_vma=False,
    )
```

```python
import functools
import math

import jax
import jax.numpy as jnp
import numpy as np
from jax import lax
from jax.experimental import pallas as pl
from jax.experimental.pallas import tpu as pltpu
from jax.sharding import PartitionSpec as P

FREQS = 512
CORES = 2
MIB = 1 << 20


def frequency_order(chips, parity):
    mine = FREQS // (chips * CORES)
    owned = np.arange(FREQS).reshape(chips // 2, 2, CORES, mine // 2, 2)
    return owned[..., parity].transpose(1, 2, 0, 3).reshape(-1)


def forward_tables(steps, chips):
    times = np.arange(steps // 2, dtype=np.int64)
    tables = []
    for parity in range(2):
        ids = frequency_order(chips, parity)
        angle = (ids[:, None] * times[None, :] % steps) * (2.0 * math.pi / steps)
        table = np.stack([np.cos(angle), -np.sin(angle)], axis=1) / math.sqrt(steps)
        tables.append(table.reshape(FREQS, steps // 2))
    return np.stack(tables)


def inverse_tables(steps, chips):
    tables = forward_tables(steps, chips) * 2.0
    for parity in range(2):
        weights = np.where(frequency_order(chips, parity) == 0, 0.5, 1.0)
        tables[parity] *= np.repeat(weights, 2)[:, None]
    return tables.reshape(2, 2, FREQS // 2, steps // 2).transpose(0, 1, 3, 2)


def chunk_list(half):
    unit = half // 8
    sizes = (unit, unit, 2 * unit, 2 * unit, 2 * unit)
    return tuple((sum(sizes[:n]), size) for n, size in enumerate(sizes))


def forward_kernel(
    place_ref, table_ref, forces_ref, shapes_ref, keep_ref, send_ref,
    table_buf, forces_buf, shapes_buf, acc_ref, table_sem, forces_sem, shapes_sem,
):
    _, zs, _, rows, modes = keep_ref.shape
    chunks = chunk_list(forces_ref.shape[1])
    copies = []
    for n, (start, size) in enumerate(chunks):
        part = pl.ds(start, size)
        pair = (
            pltpu.make_async_copy(
                forces_ref.at[:, part], forces_buf.at[:, part], forces_sem.at[n]
            ),
            pltpu.make_async_copy(
                table_ref.at[:, :, part], table_buf.at[:, :, part], table_sem.at[n]
            ),
        )
        for copy in pair:
            copy.start()
        copies.append(pair)
    shapes_copy = pltpu.make_async_copy(shapes_ref, shapes_buf, shapes_sem)
    shapes_copy.start()

    for n, (start, size) in enumerate(chunks):
        for copy in copies[n]:
            copy.wait()
        low = forces_buf[0, start : start + size]
        high = forces_buf[1, start : start + size]
        for parity, folded in enumerate((low + high, low - high)):
            part = jnp.dot(
                table_buf[parity, :, start : start + size],
                folded,
                preferred_element_type=jnp.float32,
            )
            if n == 0:
                acc_ref[parity] = part
            else:
                acc_ref[parity] += part

    shapes_copy.wait()
    first, chip = place_ref[0] == 0, place_ref[1]
    for parity in range(2):
        spec = lax.dot_general(
            acc_ref[parity].astype(jnp.bfloat16),
            shapes_buf[...],
            (((1,), (1,)), ((), ())),
            preferred_element_type=jnp.float32,
        ).reshape(2, CORES, zs, rows, modes)
        for y in range(2):
            keep = jnp.where(first, spec[y, 0], spec[y, 1]).astype(jnp.bfloat16)
            send = jnp.where(first, spec[y, 1], spec[y, 0]).astype(jnp.bfloat16)
            for z in range(zs):
                slot = chip ^ (2 * z + y)
                keep_ref[slot % 2, slot // 2, parity] = keep[z]
                send_ref[slot % 2, slot // 2, parity] = send[z]


def in_hbm(array):
    return pltpu.with_memory_space_constraint(array, pltpu.HBM)


def forward(place, table, forces, shapes_t, chips):
    _, half, dofs = forces.shape
    modes = shapes_t.shape[0]
    rows = FREQS // (chips * CORES)
    out = jax.ShapeDtypeStruct((2, chips // 2, 2, rows, modes), jnp.bfloat16)
    vmem, hbm = pl.BlockSpec(memory_space=pltpu.VMEM), pl.BlockSpec(memory_space=pltpu.HBM)
    count = len(chunk_list(half))
    return pl.pallas_call(
        forward_kernel,
        in_specs=[pl.BlockSpec(memory_space=pltpu.SMEM), hbm, hbm, hbm],
        out_specs=[vmem, vmem],
        out_shape=[out, out],
        scratch_shapes=[
            pltpu.VMEM(table.shape, jnp.bfloat16),
            pltpu.VMEM(forces.shape, jnp.bfloat16),
            pltpu.VMEM(shapes_t.shape, jnp.bfloat16),
            pltpu.VMEM((2, FREQS, dofs), jnp.float32),
            pltpu.SemaphoreType.DMA((count,)),
            pltpu.SemaphoreType.DMA((count,)),
            pltpu.SemaphoreType.DMA,
        ],
        compiler_params=pltpu.CompilerParams(vmem_limit_bytes=24 * MIB),
        cost_estimate=pl.CostEstimate(
            flops=4 * FREQS * dofs * (half + modes), bytes_accessed=12 * MIB, transcendentals=0
        ),
        name="forward",
    )(place, in_hbm(table), in_hbm(forces), in_hbm(shapes_t))


def load_copies(start, frf_ref, held_ref, sem):
    count = sem.shape[0]
    size = held_ref.shape[0] // count
    return [
        pltpu.make_async_copy(
            frf_ref.at[pl.ds(start + n * size, size)],
            held_ref.at[pl.ds(n * size, size)],
            sem.at[n],
        )
        for n in range(count)
    ]


def load_kernel(start, frf_ref, after_ref, held_ref, sem):
    copies = load_copies(start, frf_ref, held_ref, sem)
    for copy in copies:
        copy.start()
    for copy in copies:
        copy.wait()


def load(frf, start, size, after):
    hbm, anywhere = pl.BlockSpec(memory_space=pltpu.HBM), pl.BlockSpec(memory_space=pl.ANY)
    return pl.pallas_call(
        functools.partial(load_kernel, start),
        in_specs=[hbm, anywhere],
        out_specs=pl.BlockSpec(memory_space=pltpu.VMEM),
        out_shape=pltpu.VMEM((size,) + frf.shape[1:], jnp.bfloat16),
        scratch_shapes=[pltpu.SemaphoreType.DMA((math.gcd(size, 4),))],
        compiler_params=pltpu.CompilerParams(vmem_limit_bytes=2 * MIB),
        cost_estimate=pl.CostEstimate(
            flops=0, bytes_accessed=4 * size * math.prod(frf.shape[1:]), transcendentals=0
        ),
        name="load",
    )(in_hbm(frf), after)


def respond_kernel(count, *refs):
    pieces, parts = refs[:count], refs[count:-7]
    frf_ref, out_ref, direct_ref, turned_ref, result_ref, rest_ref, sem = refs[-7:]
    held = sum(part.shape[0] for part in parts)
    copies = load_copies(held, frf_ref, rest_ref, sem)
    for copy in copies:
        copy.start()
    _, rows, modes = out_ref.shape
    total = sum(piece[0].astype(jnp.float32) for piece in pieces).reshape(2 * rows, modes)
    total = total.astype(jnp.bfloat16).astype(jnp.float32)
    row = lax.broadcasted_iota(jnp.int32, total.shape, 0)
    turned = jnp.where(row % 2 == 0, -jnp.roll(total, -1, axis=0), jnp.roll(total, 1, axis=0))

    def place(f):
        return (f % 2) * rows + f // 2 * 2

    direct_ref[...] = jnp.zeros_like(direct_ref)
    turned_ref[...] = jnp.zeros_like(turned_ref)
    for f in range(rows):
        at = place(f)
        direct_ref[f, 0:2] = total[at : at + 2]
        turned_ref[f, 0:2] = turned[at : at + 2]

    def multiply(matrix_ref, step, f):
        products = [
            lax.dot_general(
                ref[f].astype(jnp.bfloat16),
                matrix_ref[step, which],
                (((1,), (1,)), ((), ())),
                preferred_element_type=jnp.float32,
            )
            for which, ref in enumerate((direct_ref, turned_ref))
        ]
        result_ref[f] = products[0] + products[1]

    base = 0
    for part in parts:

        @pl.loop(0, part.shape[0], unroll=math.gcd(4, part.shape[0]))
        def _(step, part=part, base=base):
            multiply(part, step, base + step)

        base += part.shape[0]

    each = rest_ref.shape[0] // len(copies)
    for n, copy in enumerate(copies):
        copy.wait()

        @pl.loop(n * each, (n + 1) * each, unroll=each)
        def _(step):
            multiply(rest_ref, step, held + step)

    for f in range(rows):
        at = place(f)
        direct_ref[at // 8, at % 8 : at % 8 + 2] = result_ref[f, 0:2]
    out_ref[...] = (
        direct_ref[: 2 * rows // 8].reshape(2, rows, modes).astype(jnp.bfloat16)
    )


def respond(pieces, parts, frf):
    rows, modes = pieces[0].shape[2:]
    vmem, hbm = pl.BlockSpec(memory_space=pltpu.VMEM), pl.BlockSpec(memory_space=pltpu.HBM)
    rest = frf.shape[0] - sum(part.shape[0] for part in parts)
    return pl.pallas_call(
        functools.partial(respond_kernel, len(pieces)),
        in_specs=[vmem] * (len(pieces) + len(parts)) + [hbm],
        out_specs=vmem,
        out_shape=jax.ShapeDtypeStruct((2, rows, modes), jnp.bfloat16),
        scratch_shapes=[pltpu.VMEM((rows, 8, modes), jnp.float32)] * 3
        + [
            pltpu.VMEM((rest,) + frf.shape[1:], jnp.bfloat16),
            pltpu.SemaphoreType.DMA((rest // math.gcd(rest, 4),)),
        ],
        compiler_params=pltpu.CompilerParams(vmem_limit_bytes=16 * MIB),
        cost_estimate=pl.CostEstimate(
            flops=4 * frf.size, bytes_accessed=2 * frf.size, transcendentals=0
        ),
        name="respond",
    )(*pieces, *parts, in_hbm(frf))


def project(place_ref, slots, shapes_ref, order_ref, moved_ref):
    _, _, zs, rows, modes = order_ref.shape
    core, z = place_ref[0], place_ref[1] // 2
    for shard_ref, n, far, k in slots:
        for parity in range(2):
            order_ref[parity, core ^ far, z ^ k] = shard_ref[n, parity].astype(jnp.float32)
    for parity in range(2):
        moved_ref[parity] = jnp.dot(
            order_ref[parity].reshape(FREQS // 2, modes).astype(jnp.bfloat16),
            shapes_ref[...],
            preferred_element_type=jnp.float32,
        ).astype(jnp.bfloat16)


def named_slots(plan, shards):
    return [(shards[which], n, far, k) for which, n, far, k in plan]


def early_kernel(plan, place_ref, table_ref, shapes_ref, *refs):
    shards, (waves_ref, order_ref, moved_ref) = refs[:-3], refs[-3:]
    project(place_ref, named_slots(plan, shards), shapes_ref, order_ref, moved_ref)
    y = place_ref[1] % 2
    block = waves_ref.shape[1] // 4
    for step in range(4):
        part = slice(step * block, (step + 1) * block)
        for parity in range(2):
            waves_ref[parity, part] = jnp.dot(
                table_ref[parity, y, part], moved_ref[parity], preferred_element_type=jnp.float32
            )


def late_kernel(plan, place_ref, table_ref, shapes_ref, *refs):
    shards, (waves_ref, out_ref, order_ref, moved_ref, out_buf, out_sem) = refs[:-6], refs[-6:]
    project(place_ref, named_slots(plan, shards), shapes_ref, order_ref, moved_ref)
    y = (place_ref[1] % 2) ^ 1
    count = out_sem.shape[0]
    block = out_ref.shape[1] // count

    def copy_out(step):
        part = pl.ds(step * block, block)
        return pltpu.make_async_copy(
            out_buf.at[:, part], out_ref.at[:, part], out_sem.at[step]
        )

    for step in range(count):
        part = slice(step * block, (step + 1) * block)
        even, odd = (
            waves_ref[parity, part]
            + jnp.dot(
                table_ref[parity, y, part], moved_ref[parity], preferred_element_type=jnp.float32
            )
            for parity in range(2)
        )
        out_buf[0, part] = (even + odd).astype(jnp.bfloat16)
        out_buf[1, part] = (even - odd).astype(jnp.bfloat16)
        copy_out(step).start()
    for step in range(count):
        copy_out(step).wait()


def inverse(place, table, shapes_t, shards, plan, waves=None):
    half = table.shape[2]
    modes, dofs = shapes_t.shape
    rows = shards[0].shape[2]
    zs = len(plan) // 2
    vmem = pl.BlockSpec(memory_space=pltpu.VMEM)
    scratch = [
        pltpu.VMEM((2, CORES, zs, rows, modes), jnp.float32),
        pltpu.VMEM((2, FREQS // 2, dofs), jnp.bfloat16),
    ]
    given = (place, table, shapes_t) + shards
    in_specs = [pl.BlockSpec(memory_space=pltpu.SMEM)] + [vmem] * (len(given) - 1)
    params = pltpu.CompilerParams(vmem_limit_bytes=20 * MIB)
    cost = pl.CostEstimate(
        flops=2 * FREQS * dofs * (half + modes), bytes_accessed=8 * MIB, transcendentals=0
    )
    if waves is None:
        return pl.pallas_call(
            functools.partial(early_kernel, plan),
            in_specs=in_specs,
            out_specs=vmem,
            out_shape=pltpu.VMEM((2, half, dofs), jnp.float32),
            scratch_shapes=scratch,
            compiler_params=params,
            cost_estimate=pl.CostEstimate(flops=1000, bytes_accessed=1000, transcendentals=0),
            name="early",
        )(*given)
    return pl.pallas_call(
        functools.partial(late_kernel, plan),
        in_specs=in_specs + [vmem],
        out_specs=pl.BlockSpec(memory_space=pltpu.HBM),
        out_shape=jax.ShapeDtypeStruct((2, half, dofs), jnp.bfloat16),
        scratch_shapes=scratch
        + [pltpu.VMEM((2, half, dofs), jnp.bfloat16), pltpu.SemaphoreType.DMA((8,))],
        compiler_params=params,
        cost_estimate=cost,
        name="late",
    )(*given, waves)


def add_kernel(start, splits, ours_ref, came_ref, after_ref, *out_refs):
    at = 0
    for size, out_ref in zip(splits, out_refs):
        for n in range(size):
            total = ours_ref[start + at + n].astype(jnp.float32) + came_ref[at + n].astype(
                jnp.float32
            )
            out_ref[n] = total.astype(jnp.bfloat16)
        at += size


def add(ours, came, start, splits, after):
    vmem, anywhere = pl.BlockSpec(memory_space=pltpu.VMEM), pl.BlockSpec(memory_space=pl.ANY)
    return pl.pallas_call(
        functools.partial(add_kernel, start, splits),
        in_specs=[vmem, vmem, anywhere],
        out_specs=[vmem] * len(splits),
        out_shape=[
            jax.ShapeDtypeStruct((size,) + ours.shape[1:], jnp.bfloat16) for size in splits
        ],
        compiler_params=pltpu.CompilerParams(vmem_limit_bytes=8 * MIB),
        cost_estimate=pl.CostEstimate(
            flops=came.size, bytes_accessed=6 * came.size, transcendentals=0
        ),
        name="add",
    )(ours, came, after)


def on_device(devices, forces, mode_shapes, frf):
    _, steps, dofs = forces.shape
    half = steps // 2
    chips = devices // CORES
    zs = chips // 2

    def swap(values, distance):
        pairs = [(i, i ^ distance) for i in range(devices)]
        return lax.ppermute(values, "dof", pairs)

    index = lax.axis_index("dof")
    place = jnp.stack([index % CORES, index // CORES]).astype(jnp.int32)
    shapes_t = mode_shapes.T
    fwd = jnp.asarray(forward_tables(steps, chips).astype(jnp.bfloat16))
    inv = jnp.asarray(inverse_tables(steps, chips).astype(jnp.bfloat16))

    unit = frf.shape[0] // 8
    keep, send = forward(place, fwd, forces.reshape(2, half, dofs), shapes_t, chips)
    slots = (2 * zs,) + keep.shape[2:]
    here, there_near, there_far = add(
        keep.reshape(slots), swap(send, 1).reshape(slots), 0, (zs, 1, zs - 1), send
    )
    came_far, came_near = swap(there_far, 2), swap(there_near, 2)
    part0 = load(frf, 0, 3 * unit, there_far)
    pieces = add(here, came_far, 1, (1,) * (zs - 1), part0)
    part1 = load(frf, 3 * unit, 3 * unit, pieces[0])
    came = [swap(piece, 4 * k) for k, piece in enumerate(pieces, 1)]
    response = respond([here[:1], came_near, *came], (part0, part1), frf)

    own = response[None]
    over = swap(own, 2)
    shards = [swap(response, 4 * k) for k in range(1, zs)]
    far, over = lax.optimization_barrier((jnp.stack(shards), over))
    over_far = swap(far, 2)
    cut = (zs - 1) // 2
    twin = swap(jnp.concatenate([own, over]), 1)
    twin_far = [swap(jnp.stack(shards[:-cut]), 1), swap(jnp.stack(shards[-cut:]), 1)]
    plan = [(0, 0, 0, 0), (2, 0, 1, 0)]
    for k in range(1, zs):
        at = k - 1
        plan += [(1, at, 0, k)]
        plan += [(3, at, 1, k) if at < zs - 1 - cut else (4, at - (zs - 1 - cut), 1, k)]
    waves = inverse(place, inv, shapes_t, (own, far, twin, *twin_far), plan)
    over_far, waves = lax.optimization_barrier((over_far, waves))
    plan = [(0, 0, 0, 0), (2, 1, 1, 0)]
    for k in range(1, zs):
        plan += [(1, k - 1, 0, k), (3, k - 1, 1, k)]
    out = inverse(place, inv, shapes_t, (over, over_far, twin, swap(over_far, 1)), plan, waves)
    return out.reshape(1, steps, dofs)


def solution(mesh):
    devices = mesh.shape["dof"]
    return jax.shard_map(
        functools.partial(on_device, devices),
        mesh=mesh,
        in_specs=(P("grp", None, "dof"), P("dof", None), P("dof", None, None, None)),
        out_specs=P("grp", None, "dof"),
        check_vma=False,
    )
```

```python
import functools
import math

import jax
import jax.numpy as jnp
import numpy as np
from jax import lax
from jax.experimental import pallas as pl
from jax.experimental.pallas import tpu as pltpu
from jax.sharding import PartitionSpec as P

FREQS = 512
CORES = 2
MIB = 1 << 20


def frequency_order(chips, parity):
    mine = FREQS // (chips * CORES)
    owned = np.arange(FREQS).reshape(chips // 2, 2, CORES, mine // 2, 2)
    return owned[..., parity].transpose(1, 2, 0, 3).reshape(-1)


def forward_tables(steps, chips):
    times = np.arange(steps // 2, dtype=np.int64)
    tables = []
    for parity in range(2):
        ids = frequency_order(chips, parity)
        angle = (ids[:, None] * times[None, :] % steps) * (2.0 * math.pi / steps)
        table = np.stack([np.cos(angle), -np.sin(angle)], axis=1) / math.sqrt(steps)
        tables.append(table.reshape(FREQS, steps // 2))
    return np.stack(tables)


def inverse_tables(steps, chips):
    tables = forward_tables(steps, chips) * 2.0
    for parity in range(2):
        weights = np.where(frequency_order(chips, parity) == 0, 0.5, 1.0)
        tables[parity] *= np.repeat(weights, 2)[:, None]
    return tables.reshape(2, 2, FREQS // 2, steps // 2).transpose(0, 1, 3, 2)


def chunk_list(half):
    unit = half // 8
    sizes = (unit, unit, 2 * unit, 2 * unit, 2 * unit)
    return tuple((sum(sizes[:n]), size) for n, size in enumerate(sizes))


def forward_kernel(
    place_ref, table_ref, forces_ref, shapes_ref, keep_ref, send_ref,
    table_buf, forces_buf, shapes_buf, acc_ref, table_sem, forces_sem, shapes_sem,
):
    _, zs, _, rows, modes = keep_ref.shape
    chunks = chunk_list(forces_ref.shape[1])
    copies = []
    for n, (start, size) in enumerate(chunks):
        part = pl.ds(start, size)
        pair = (
            pltpu.make_async_copy(
                forces_ref.at[:, part], forces_buf.at[:, part], forces_sem.at[n]
            ),
            pltpu.make_async_copy(
                table_ref.at[:, :, part], table_buf.at[:, :, part], table_sem.at[n]
            ),
        )
        for copy in pair:
            copy.start()
        copies.append(pair)
    shapes_copy = pltpu.make_async_copy(shapes_ref, shapes_buf, shapes_sem)
    shapes_copy.start()

    for n, (start, size) in enumerate(chunks):
        for copy in copies[n]:
            copy.wait()
        low = forces_buf[0, start : start + size]
        high = forces_buf[1, start : start + size]
        for parity, folded in enumerate((low + high, low - high)):
            part = jnp.dot(
                table_buf[parity, :, start : start + size],
                folded,
                preferred_element_type=jnp.float32,
            )
            if n == 0:
                acc_ref[parity] = part
            else:
                acc_ref[parity] += part

    shapes_copy.wait()
    first, chip = place_ref[0] == 0, place_ref[1]
    for parity in range(2):
        spec = lax.dot_general(
            acc_ref[parity].astype(jnp.bfloat16),
            shapes_buf[...],
            (((1,), (1,)), ((), ())),
            preferred_element_type=jnp.float32,
        ).reshape(2, CORES, zs, rows, modes)
        for y in range(2):
            keep = jnp.where(first, spec[y, 0], spec[y, 1]).astype(jnp.bfloat16)
            send = jnp.where(first, spec[y, 1], spec[y, 0]).astype(jnp.bfloat16)
            for z in range(zs):
                slot = chip ^ (2 * z + y)
                keep_ref[slot % 2, slot // 2, parity] = keep[z]
                send_ref[slot % 2, slot // 2, parity] = send[z]


def in_hbm(array):
    return pltpu.with_memory_space_constraint(array, pltpu.HBM)


def forward(place, table, forces, shapes_t, chips):
    _, half, dofs = forces.shape
    modes = shapes_t.shape[0]
    rows = FREQS // (chips * CORES)
    out = jax.ShapeDtypeStruct((2, chips // 2, 2, rows, modes), jnp.bfloat16)
    vmem, hbm = pl.BlockSpec(memory_space=pltpu.VMEM), pl.BlockSpec(memory_space=pltpu.HBM)
    count = len(chunk_list(half))
    return pl.pallas_call(
        forward_kernel,
        in_specs=[pl.BlockSpec(memory_space=pltpu.SMEM), hbm, hbm, hbm],
        out_specs=[vmem, vmem],
        out_shape=[out, out],
        scratch_shapes=[
            pltpu.VMEM(table.shape, jnp.bfloat16),
            pltpu.VMEM(forces.shape, jnp.bfloat16),
            pltpu.VMEM(shapes_t.shape, jnp.bfloat16),
            pltpu.VMEM((2, FREQS, dofs), jnp.float32),
            pltpu.SemaphoreType.DMA((count,)),
            pltpu.SemaphoreType.DMA((count,)),
            pltpu.SemaphoreType.DMA,
        ],
        compiler_params=pltpu.CompilerParams(vmem_limit_bytes=24 * MIB),
        cost_estimate=pl.CostEstimate(
            flops=4 * FREQS * dofs * (half + modes), bytes_accessed=12 * MIB, transcendentals=0
        ),
        name="forward",
    )(place, in_hbm(table), in_hbm(forces), in_hbm(shapes_t))


def load_copies(start, frf_ref, held_ref, sem):
    count = sem.shape[0]
    size = held_ref.shape[0] // count
    return [
        pltpu.make_async_copy(
            frf_ref.at[pl.ds(start + n * size, size)],
            held_ref.at[pl.ds(n * size, size)],
            sem.at[n],
        )
        for n in range(count)
    ]


def load_kernel(start, frf_ref, after_ref, held_ref, sem):
    copies = load_copies(start, frf_ref, held_ref, sem)
    for copy in copies:
        copy.start()
    for copy in copies:
        copy.wait()


def load(frf, start, size, after):
    hbm, anywhere = pl.BlockSpec(memory_space=pltpu.HBM), pl.BlockSpec(memory_space=pl.ANY)
    return pl.pallas_call(
        functools.partial(load_kernel, start),
        in_specs=[hbm, anywhere],
        out_specs=pl.BlockSpec(memory_space=pltpu.VMEM),
        out_shape=pltpu.VMEM((size,) + frf.shape[1:], jnp.bfloat16),
        scratch_shapes=[pltpu.SemaphoreType.DMA((math.gcd(size, 4),))],
        compiler_params=pltpu.CompilerParams(vmem_limit_bytes=2 * MIB),
        cost_estimate=pl.CostEstimate(
            flops=0, bytes_accessed=4 * size * math.prod(frf.shape[1:]), transcendentals=0
        ),
        name="load",
    )(in_hbm(frf), after)


def respond_kernel(count, *refs):
    pieces, parts = refs[:count], refs[count:-7]
    frf_ref, out_ref, direct_ref, turned_ref, result_ref, rest_ref, sem = refs[-7:]
    held = sum(part.shape[0] for part in parts)
    copies = load_copies(held, frf_ref, rest_ref, sem)
    for copy in copies:
        copy.start()
    _, rows, modes = out_ref.shape
    total = sum(piece[0].astype(jnp.float32) for piece in pieces).reshape(2 * rows, modes)
    total = total.astype(jnp.bfloat16).astype(jnp.float32)
    row = lax.broadcasted_iota(jnp.int32, total.shape, 0)
    turned = jnp.where(row % 2 == 0, -jnp.roll(total, -1, axis=0), jnp.roll(total, 1, axis=0))

    def place(f):
        return (f % 2) * rows + f // 2 * 2

    direct_ref[...] = jnp.zeros_like(direct_ref)
    turned_ref[...] = jnp.zeros_like(turned_ref)
    for f in range(rows):
        at = place(f)
        direct_ref[f, 0:2] = total[at : at + 2]
        turned_ref[f, 0:2] = turned[at : at + 2]

    def multiply(matrix_ref, step, f):
        products = [
            lax.dot_general(
                ref[f].astype(jnp.bfloat16),
                matrix_ref[step, which],
                (((1,), (1,)), ((), ())),
                preferred_element_type=jnp.float32,
            )
            for which, ref in enumerate((direct_ref, turned_ref))
        ]
        result_ref[f] = products[0] + products[1]

    base = 0
    for part in parts:

        @pl.loop(0, part.shape[0], unroll=math.gcd(4, part.shape[0]))
        def _(step, part=part, base=base):
            multiply(part, step, base + step)

        base += part.shape[0]

    each = rest_ref.shape[0] // len(copies)
    for n, copy in enumerate(copies):
        copy.wait()

        @pl.loop(n * each, (n + 1) * each, unroll=each)
        def _(step):
            multiply(rest_ref, step, held + step)

    for f in range(rows):
        at = place(f)
        direct_ref[at // 8, at % 8 : at % 8 + 2] = result_ref[f, 0:2]
    out_ref[...] = (
        direct_ref[: 2 * rows // 8].reshape(2, rows, modes).astype(jnp.bfloat16)
    )


def respond(pieces, parts, frf):
    rows, modes = pieces[0].shape[2:]
    vmem, hbm = pl.BlockSpec(memory_space=pltpu.VMEM), pl.BlockSpec(memory_space=pltpu.HBM)
    rest = frf.shape[0] - sum(part.shape[0] for part in parts)
    return pl.pallas_call(
        functools.partial(respond_kernel, len(pieces)),
        in_specs=[vmem] * (len(pieces) + len(parts)) + [hbm],
        out_specs=vmem,
        out_shape=jax.ShapeDtypeStruct((2, rows, modes), jnp.bfloat16),
        scratch_shapes=[pltpu.VMEM((rows, 8, modes), jnp.float32)] * 3
        + [
            pltpu.VMEM((rest,) + frf.shape[1:], jnp.bfloat16),
            pltpu.SemaphoreType.DMA((rest // math.gcd(rest, 4),)),
        ],
        compiler_params=pltpu.CompilerParams(vmem_limit_bytes=16 * MIB),
        cost_estimate=pl.CostEstimate(
            flops=4 * frf.size, bytes_accessed=2 * frf.size, transcendentals=0
        ),
        name="respond",
    )(*pieces, *parts, in_hbm(frf))


def project(place_ref, slots, shapes_ref, order_ref, moved_ref):
    _, _, zs, rows, modes = order_ref.shape
    core, z = place_ref[0], place_ref[1] // 2
    for shard_ref, n, far, k in slots:
        for parity in range(2):
            order_ref[parity, core ^ far, z ^ k] = shard_ref[n, parity].astype(jnp.float32)
    for parity in range(2):
        moved_ref[parity] = jnp.dot(
            order_ref[parity].reshape(FREQS // 2, modes).astype(jnp.bfloat16),
            shapes_ref[...],
            preferred_element_type=jnp.float32,
        ).astype(jnp.bfloat16)


def named_slots(plan, shards):
    return [(shards[which], n, far, k) for which, n, far, k in plan]


def early_kernel(plan, place_ref, table_ref, shapes_ref, *refs):
    shards, (waves_ref, order_ref, moved_ref) = refs[:-3], refs[-3:]
    project(place_ref, named_slots(plan, shards), shapes_ref, order_ref, moved_ref)
    y = place_ref[1] % 2
    block = waves_ref.shape[1] // 4
    for step in range(4):
        part = slice(step * block, (step + 1) * block)
        for parity in range(2):
            waves_ref[parity, part] = jnp.dot(
                table_ref[parity, y, part], moved_ref[parity], preferred_element_type=jnp.float32
            )


def late_kernel(plan, place_ref, table_ref, shapes_ref, *refs):
    shards, (waves_ref, out_ref, order_ref, moved_ref, out_buf, out_sem) = refs[:-6], refs[-6:]
    project(place_ref, named_slots(plan, shards), shapes_ref, order_ref, moved_ref)
    y = (place_ref[1] % 2) ^ 1
    count = out_sem.shape[0]
    block = out_ref.shape[1] // count

    def copy_out(step):
        part = pl.ds(step * block, block)
        return pltpu.make_async_copy(
            out_buf.at[:, part], out_ref.at[:, part], out_sem.at[step]
        )

    for step in range(count):
        part = slice(step * block, (step + 1) * block)
        even, odd = (
            waves_ref[parity, part]
            + jnp.dot(
                table_ref[parity, y, part], moved_ref[parity], preferred_element_type=jnp.float32
            )
            for parity in range(2)
        )
        out_buf[0, part] = (even + odd).astype(jnp.bfloat16)
        out_buf[1, part] = (even - odd).astype(jnp.bfloat16)
        copy_out(step).start()
    for step in range(count):
        copy_out(step).wait()


def inverse(place, table, shapes_t, shards, plan, waves=None):
    half = table.shape[2]
    modes, dofs = shapes_t.shape
    rows = shards[0].shape[2]
    zs = len(plan) // 2
    vmem = pl.BlockSpec(memory_space=pltpu.VMEM)
    scratch = [
        pltpu.VMEM((2, CORES, zs, rows, modes), jnp.float32),
        pltpu.VMEM((2, FREQS // 2, dofs), jnp.bfloat16),
    ]
    given = (place, table, shapes_t) + shards
    in_specs = [pl.BlockSpec(memory_space=pltpu.SMEM)] + [vmem] * (len(given) - 1)
    params = pltpu.CompilerParams(vmem_limit_bytes=20 * MIB)
    cost = pl.CostEstimate(
        flops=2 * FREQS * dofs * (half + modes), bytes_accessed=8 * MIB, transcendentals=0
    )
    if waves is None:
        return pl.pallas_call(
            functools.partial(early_kernel, plan),
            in_specs=in_specs,
            out_specs=vmem,
            out_shape=pltpu.VMEM((2, half, dofs), jnp.float32),
            scratch_shapes=scratch,
            compiler_params=params,
            cost_estimate=pl.CostEstimate(flops=1000, bytes_accessed=1000, transcendentals=0),
            name="early",
        )(*given)
    return pl.pallas_call(
        functools.partial(late_kernel, plan),
        in_specs=in_specs + [vmem],
        out_specs=pl.BlockSpec(memory_space=pltpu.HBM),
        out_shape=jax.ShapeDtypeStruct((2, half, dofs), jnp.bfloat16),
        scratch_shapes=scratch
        + [pltpu.VMEM((2, half, dofs), jnp.bfloat16), pltpu.SemaphoreType.DMA((8,))],
        compiler_params=params,
        cost_estimate=cost,
        name="late",
    )(*given, waves)


def add_kernel(start, splits, ours_ref, came_ref, after_ref, *out_refs):
    at = 0
    for size, out_ref in zip(splits, out_refs):
        for n in range(size):
            total = ours_ref[start + at + n].astype(jnp.float32) + came_ref[at + n].astype(
                jnp.float32
            )
            out_ref[n] = total.astype(jnp.bfloat16)
        at += size


def add(ours, came, start, splits, after):
    vmem, anywhere = pl.BlockSpec(memory_space=pltpu.VMEM), pl.BlockSpec(memory_space=pl.ANY)
    return pl.pallas_call(
        functools.partial(add_kernel, start, splits),
        in_specs=[vmem, vmem, anywhere],
        out_specs=[vmem] * len(splits),
        out_shape=[
            jax.ShapeDtypeStruct((size,) + ours.shape[1:], jnp.bfloat16) for size in splits
        ],
        compiler_params=pltpu.CompilerParams(vmem_limit_bytes=8 * MIB),
        cost_estimate=pl.CostEstimate(
            flops=came.size, bytes_accessed=6 * came.size, transcendentals=0
        ),
        name="add",
    )(ours, came, after)


def on_device(devices, forces, mode_shapes, frf):
    _, steps, dofs = forces.shape
    half = steps // 2
    chips = devices // CORES
    zs = chips // 2

    def swap(values, distance):
        pairs = [(i, i ^ distance) for i in range(devices)]
        return lax.ppermute(values, "dof", pairs)

    index = lax.axis_index("dof")
    place = jnp.stack([index % CORES, index // CORES]).astype(jnp.int32)
    shapes_t = mode_shapes.T
    fwd = jnp.asarray(forward_tables(steps, chips).astype(jnp.bfloat16))
    inv = jnp.asarray(inverse_tables(steps, chips).astype(jnp.bfloat16))

    unit = frf.shape[0] // 8
    keep, send = forward(place, fwd, forces.reshape(2, half, dofs), shapes_t, chips)
    slots = (2 * zs,) + keep.shape[2:]
    here, there_near, there_far = add(
        keep.reshape(slots), swap(send, 1).reshape(slots), 0, (zs, 1, zs - 1), send
    )
    came_far, came_near = swap(there_far, 2), swap(there_near, 2)
    part0 = load(frf, 0, 3 * unit, there_far)
    pieces = add(here, came_far, 1, (1,) * (zs - 1), part0)
    part1 = load(frf, 3 * unit, 2 * unit, pieces[0])
    came = [swap(piece, 4 * k) for k, piece in enumerate(pieces, 1)]
    response = respond([here[:1], came_near, *came], (part0, part1), frf)

    shards = [response] + [swap(response, 4 * k) for k in range(1, zs)]
    own = jnp.stack(shards)
    over = swap(own, 2)
    cut = zs // 2
    twin = [swap(jnp.stack(half_shards), 1) for half_shards in (shards[:cut], shards[cut:])]
    plan = [(0, k, 0, k) for k in range(zs)]
    plan += [(1 + k // cut, k % cut, 1, k) for k in range(zs)]
    waves = inverse(place, inv, shapes_t, (own, *twin), plan)
    over, waves = lax.optimization_barrier((over, waves))
    plan = [(far, k, far, k) for far in range(CORES) for k in range(zs)]
    out = inverse(place, inv, shapes_t, (over, swap(over, 1)), plan, waves)
    return out.reshape(1, steps, dofs)


def solution(mesh):
    devices = mesh.shape["dof"]
    return jax.shard_map(
        functools.partial(on_device, devices),
        mesh=mesh,
        in_specs=(P("grp", None, "dof"), P("dof", None), P("dof", None, None, None)),
        out_specs=P("grp", None, "dof"),
        check_vma=False,
    )
```

```python
import functools
import math

import jax
import jax.numpy as jnp
import numpy as np
from jax import lax
from jax.experimental import pallas as pl
from jax.experimental.pallas import tpu as pltpu
from jax.sharding import PartitionSpec as P

FREQS = 512
CORES = 2
MIB = 1 << 20


def frequency_order(chips, parity):
    mine = FREQS // (chips * CORES)
    owned = np.arange(FREQS).reshape(chips // 2, 2, CORES, mine // 2, 2)
    return owned[..., parity].transpose(1, 2, 0, 3).reshape(-1)


def forward_tables(steps, chips):
    times = np.arange(steps // 2, dtype=np.int64)
    tables = []
    for parity in range(2):
        ids = frequency_order(chips, parity)
        angle = (ids[:, None] * times[None, :] % steps) * (2.0 * math.pi / steps)
        table = np.stack([np.cos(angle), -np.sin(angle)], axis=1) / math.sqrt(steps)
        tables.append(table.reshape(FREQS, steps // 2))
    return np.stack(tables)


def inverse_tables(steps, chips):
    tables = forward_tables(steps, chips) * 2.0
    for parity in range(2):
        weights = np.where(frequency_order(chips, parity) == 0, 0.5, 1.0)
        tables[parity] *= np.repeat(weights, 2)[:, None]
    return tables.reshape(2, 2, FREQS // 2, steps // 2).transpose(0, 1, 3, 2)


def chunk_list(half):
    unit = half // 8
    sizes = (unit, unit, 2 * unit, 2 * unit, 2 * unit)
    return tuple((sum(sizes[:n]), size) for n, size in enumerate(sizes))


def forward_kernel(
    place_ref, table_ref, forces_ref, shapes_ref, keep_ref, send_ref,
    table_buf, forces_buf, shapes_buf, acc_ref, table_sem, forces_sem, shapes_sem,
):
    _, zs, _, rows, modes = keep_ref.shape
    chunks = chunk_list(forces_ref.shape[1])
    copies = []
    for n, (start, size) in enumerate(chunks):
        part = pl.ds(start, size)
        pair = (
            pltpu.make_async_copy(
                forces_ref.at[:, part], forces_buf.at[:, part], forces_sem.at[n]
            ),
            pltpu.make_async_copy(
                table_ref.at[:, :, part], table_buf.at[:, :, part], table_sem.at[n]
            ),
        )
        for copy in pair:
            copy.start()
        copies.append(pair)
    shapes_copy = pltpu.make_async_copy(shapes_ref, shapes_buf, shapes_sem)
    shapes_copy.start()

    for n, (start, size) in enumerate(chunks):
        for copy in copies[n]:
            copy.wait()
        low = forces_buf[0, start : start + size]
        high = forces_buf[1, start : start + size]
        for parity, folded in enumerate((low + high, low - high)):
            part = jnp.dot(
                table_buf[parity, :, start : start + size],
                folded,
                preferred_element_type=jnp.float32,
            )
            if n == 0:
                acc_ref[parity] = part
            else:
                acc_ref[parity] += part

    shapes_copy.wait()
    first, chip = place_ref[0] == 0, place_ref[1]
    for parity in range(2):
        spec = lax.dot_general(
            acc_ref[parity].astype(jnp.bfloat16),
            shapes_buf[...],
            (((1,), (1,)), ((), ())),
            preferred_element_type=jnp.float32,
        ).reshape(2, CORES, zs, rows, modes)
        for y in range(2):
            keep = jnp.where(first, spec[y, 0], spec[y, 1]).astype(jnp.bfloat16)
            send = jnp.where(first, spec[y, 1], spec[y, 0]).astype(jnp.bfloat16)
            for z in range(zs):
                slot = chip ^ (2 * z + y)
                keep_ref[slot % 2, slot // 2, parity] = keep[z]
                send_ref[slot % 2, slot // 2, parity] = send[z]


def in_hbm(array):
    return pltpu.with_memory_space_constraint(array, pltpu.HBM)


def forward(place, table, forces, shapes_t, chips):
    _, half, dofs = forces.shape
    modes = shapes_t.shape[0]
    rows = FREQS // (chips * CORES)
    out = jax.ShapeDtypeStruct((2, chips // 2, 2, rows, modes), jnp.bfloat16)
    vmem, hbm = pl.BlockSpec(memory_space=pltpu.VMEM), pl.BlockSpec(memory_space=pltpu.HBM)
    count = len(chunk_list(half))
    return pl.pallas_call(
        forward_kernel,
        in_specs=[pl.BlockSpec(memory_space=pltpu.SMEM), hbm, hbm, hbm],
        out_specs=[vmem, vmem],
        out_shape=[out, out],
        scratch_shapes=[
            pltpu.VMEM(table.shape, jnp.bfloat16),
            pltpu.VMEM(forces.shape, jnp.bfloat16),
            pltpu.VMEM(shapes_t.shape, jnp.bfloat16),
            pltpu.VMEM((2, FREQS, dofs), jnp.float32),
            pltpu.SemaphoreType.DMA((count,)),
            pltpu.SemaphoreType.DMA((count,)),
            pltpu.SemaphoreType.DMA,
        ],
        compiler_params=pltpu.CompilerParams(vmem_limit_bytes=24 * MIB),
        cost_estimate=pl.CostEstimate(
            flops=4 * FREQS * dofs * (half + modes), bytes_accessed=12 * MIB, transcendentals=0
        ),
        name="forward",
    )(place, in_hbm(table), in_hbm(forces), in_hbm(shapes_t))


def load_copies(start, frf_ref, held_ref, sem):
    count = sem.shape[0]
    size = held_ref.shape[0] // count
    return [
        pltpu.make_async_copy(
            frf_ref.at[pl.ds(start + n * size, size)],
            held_ref.at[pl.ds(n * size, size)],
            sem.at[n],
        )
        for n in range(count)
    ]


def load_kernel(start, frf_ref, after_ref, held_ref, sem):
    copies = load_copies(start, frf_ref, held_ref, sem)
    for copy in copies:
        copy.start()
    for copy in copies:
        copy.wait()


def load(frf, start, size, after):
    hbm, anywhere = pl.BlockSpec(memory_space=pltpu.HBM), pl.BlockSpec(memory_space=pl.ANY)
    return pl.pallas_call(
        functools.partial(load_kernel, start),
        in_specs=[hbm, anywhere],
        out_specs=pl.BlockSpec(memory_space=pltpu.VMEM),
        out_shape=pltpu.VMEM((size,) + frf.shape[1:], jnp.bfloat16),
        scratch_shapes=[pltpu.SemaphoreType.DMA((math.gcd(size, 4),))],
        compiler_params=pltpu.CompilerParams(vmem_limit_bytes=2 * MIB),
        cost_estimate=pl.CostEstimate(
            flops=0, bytes_accessed=4 * size * math.prod(frf.shape[1:]), transcendentals=0
        ),
        name="load",
    )(in_hbm(frf), after)


def respond_kernel(count, *refs):
    pieces, parts = refs[:count], refs[count:-7]
    frf_ref, out_ref, direct_ref, turned_ref, result_ref, rest_ref, sem = refs[-7:]
    held = sum(part.shape[0] for part in parts)
    copies = load_copies(held, frf_ref, rest_ref, sem)
    for copy in copies:
        copy.start()
    _, rows, modes = out_ref.shape
    total = sum(piece[0].astype(jnp.float32) for piece in pieces).reshape(2 * rows, modes)
    total = total.astype(jnp.bfloat16).astype(jnp.float32)
    row = lax.broadcasted_iota(jnp.int32, total.shape, 0)
    turned = jnp.where(row % 2 == 0, -jnp.roll(total, -1, axis=0), jnp.roll(total, 1, axis=0))

    def place(f):
        return (f % 2) * rows + f // 2 * 2

    direct_ref[...] = jnp.zeros_like(direct_ref)
    turned_ref[...] = jnp.zeros_like(turned_ref)
    for f in range(rows):
        at = place(f)
        direct_ref[f, 0:2] = total[at : at + 2]
        turned_ref[f, 0:2] = turned[at : at + 2]

    def multiply(matrix_ref, step, f):
        products = [
            lax.dot_general(
                ref[f].astype(jnp.bfloat16),
                matrix_ref[step, which],
                (((1,), (1,)), ((), ())),
                preferred_element_type=jnp.float32,
            )
            for which, ref in enumerate((direct_ref, turned_ref))
        ]
        result_ref[f] = products[0] + products[1]

    base = 0
    for part in parts:

        @pl.loop(0, part.shape[0], unroll=part.shape[0])
        def _(step, part=part, base=base):
            multiply(part, step, base + step)

        base += part.shape[0]

    for copy in copies:
        copy.wait()

    @pl.loop(0, rest_ref.shape[0], unroll=rest_ref.shape[0])
    def _(step):
        multiply(rest_ref, step, held + step)

    for f in range(rows):
        at = place(f)
        direct_ref[at // 8, at % 8 : at % 8 + 2] = result_ref[f, 0:2]
    out_ref[...] = (
        direct_ref[: 2 * rows // 8].reshape(2, rows, modes).astype(jnp.bfloat16)
    )


def respond(pieces, parts, frf):
    rows, modes = pieces[0].shape[2:]
    vmem, hbm = pl.BlockSpec(memory_space=pltpu.VMEM), pl.BlockSpec(memory_space=pltpu.HBM)
    rest = frf.shape[0] - sum(part.shape[0] for part in parts)
    return pl.pallas_call(
        functools.partial(respond_kernel, len(pieces)),
        in_specs=[vmem] * (len(pieces) + len(parts)) + [hbm],
        out_specs=vmem,
        out_shape=jax.ShapeDtypeStruct((2, rows, modes), jnp.bfloat16),
        scratch_shapes=[pltpu.VMEM((rows, 8, modes), jnp.float32)] * 3
        + [
            pltpu.VMEM((rest,) + frf.shape[1:], jnp.bfloat16),
            pltpu.SemaphoreType.DMA((rest // math.gcd(rest, 4),)),
        ],
        compiler_params=pltpu.CompilerParams(vmem_limit_bytes=16 * MIB),
        cost_estimate=pl.CostEstimate(
            flops=4 * frf.size, bytes_accessed=2 * frf.size, transcendentals=0
        ),
        name="respond",
    )(*pieces, *parts, in_hbm(frf))


def project(place_ref, slots, shapes_ref, order_ref, moved_ref):
    _, _, zs, rows, modes = order_ref.shape
    core, z = place_ref[0], place_ref[1] // 2
    for shard_ref, n, far, k in slots:
        for parity in range(2):
            order_ref[parity, core ^ far, z ^ k] = shard_ref[n, parity].astype(jnp.float32)
    for parity in range(2):
        moved_ref[parity] = jnp.dot(
            order_ref[parity].reshape(FREQS // 2, modes).astype(jnp.bfloat16),
            shapes_ref[...],
            preferred_element_type=jnp.float32,
        ).astype(jnp.bfloat16)


def named_slots(plan, shards):
    return [(shards[which], n, far, k) for which, n, far, k in plan]


def early_kernel(plan, place_ref, table_ref, shapes_ref, *refs):
    shards, (waves_ref, order_ref, moved_ref) = refs[:-3], refs[-3:]
    project(place_ref, named_slots(plan, shards), shapes_ref, order_ref, moved_ref)
    y = place_ref[1] % 2
    block = waves_ref.shape[1] // 4
    for step in range(4):
        part = slice(step * block, (step + 1) * block)
        for parity in range(2):
            waves_ref[parity, part] = jnp.dot(
                table_ref[parity, y, part], moved_ref[parity], preferred_element_type=jnp.float32
            )


def late_kernel(plan, place_ref, table_ref, shapes_ref, *refs):
    shards, (waves_ref, out_ref, order_ref, moved_ref, out_buf, out_sem) = refs[:-6], refs[-6:]
    project(place_ref, named_slots(plan, shards), shapes_ref, order_ref, moved_ref)
    y = (place_ref[1] % 2) ^ 1
    count = out_sem.shape[0]
    block = out_ref.shape[1] // count

    def copy_out(step):
        part = pl.ds(step * block, block)
        return pltpu.make_async_copy(
            out_buf.at[:, part], out_ref.at[:, part], out_sem.at[step]
        )

    for step in range(count):
        part = slice(step * block, (step + 1) * block)
        even, odd = (
            waves_ref[parity, part]
            + jnp.dot(
                table_ref[parity, y, part], moved_ref[parity], preferred_element_type=jnp.float32
            )
            for parity in range(2)
        )
        out_buf[0, part] = (even + odd).astype(jnp.bfloat16)
        out_buf[1, part] = (even - odd).astype(jnp.bfloat16)
        copy_out(step).start()
    for step in range(count):
        copy_out(step).wait()


def inverse(place, table, shapes_t, shards, plan, waves=None):
    half = table.shape[2]
    modes, dofs = shapes_t.shape
    rows = shards[0].shape[2]
    zs = len(plan) // 2
    vmem = pl.BlockSpec(memory_space=pltpu.VMEM)
    scratch = [
        pltpu.VMEM((2, CORES, zs, rows, modes), jnp.float32),
        pltpu.VMEM((2, FREQS // 2, dofs), jnp.bfloat16),
    ]
    given = (place, table, shapes_t) + shards
    in_specs = [pl.BlockSpec(memory_space=pltpu.SMEM)] + [vmem] * (len(given) - 1)
    params = pltpu.CompilerParams(vmem_limit_bytes=20 * MIB)
    cost = pl.CostEstimate(
        flops=2 * FREQS * dofs * (half + modes), bytes_accessed=8 * MIB, transcendentals=0
    )
    if waves is None:
        return pl.pallas_call(
            functools.partial(early_kernel, plan),
            in_specs=in_specs,
            out_specs=vmem,
            out_shape=pltpu.VMEM((2, half, dofs), jnp.float32),
            scratch_shapes=scratch,
            compiler_params=params,
            cost_estimate=pl.CostEstimate(flops=1000, bytes_accessed=1000, transcendentals=0),
            name="early",
        )(*given)
    return pl.pallas_call(
        functools.partial(late_kernel, plan),
        in_specs=in_specs + [vmem],
        out_specs=pl.BlockSpec(memory_space=pltpu.HBM),
        out_shape=jax.ShapeDtypeStruct((2, half, dofs), jnp.bfloat16),
        scratch_shapes=scratch
        + [pltpu.VMEM((2, half, dofs), jnp.bfloat16), pltpu.SemaphoreType.DMA((8,))],
        compiler_params=params,
        cost_estimate=cost,
        name="late",
    )(*given, waves)


def add_kernel(start, splits, ours_ref, came_ref, after_ref, *out_refs):
    at = 0
    for size, out_ref in zip(splits, out_refs):
        for n in range(size):
            total = ours_ref[start + at + n].astype(jnp.float32) + came_ref[at + n].astype(
                jnp.float32
            )
            out_ref[n] = total.astype(jnp.bfloat16)
        at += size


def add(ours, came, start, splits, after):
    vmem, anywhere = pl.BlockSpec(memory_space=pltpu.VMEM), pl.BlockSpec(memory_space=pl.ANY)
    return pl.pallas_call(
        functools.partial(add_kernel, start, splits),
        in_specs=[vmem, vmem, anywhere],
        out_specs=[vmem] * len(splits),
        out_shape=[
            jax.ShapeDtypeStruct((size,) + ours.shape[1:], jnp.bfloat16) for size in splits
        ],
        compiler_params=pltpu.CompilerParams(vmem_limit_bytes=8 * MIB),
        cost_estimate=pl.CostEstimate(
            flops=came.size, bytes_accessed=6 * came.size, transcendentals=0
        ),
        name="add",
    )(ours, came, after)


def on_device(devices, forces, mode_shapes, frf):
    _, steps, dofs = forces.shape
    half = steps // 2
    chips = devices // CORES
    zs = chips // 2

    def swap(values, distance):
        pairs = [(i, i ^ distance) for i in range(devices)]
        return lax.ppermute(values, "dof", pairs)

    index = lax.axis_index("dof")
    place = jnp.stack([index % CORES, index // CORES]).astype(jnp.int32)
    shapes_t = mode_shapes.T
    fwd = jnp.asarray(forward_tables(steps, chips).astype(jnp.bfloat16))
    inv = jnp.asarray(inverse_tables(steps, chips).astype(jnp.bfloat16))

    unit = frf.shape[0] // 8
    keep, send = forward(place, fwd, forces.reshape(2, half, dofs), shapes_t, chips)
    slots = (2 * zs,) + keep.shape[2:]
    here, there_near, there_far = add(
        keep.reshape(slots), swap(send, 1).reshape(slots), 0, (zs, 1, zs - 1), send
    )
    came_far, came_near = swap(there_far, 2), swap(there_near, 2)
    part0 = load(frf, 0, 3 * unit, there_far)
    pieces = add(here, came_far, 1, (1,) * (zs - 1), part0)
    part1 = load(frf, 3 * unit, 2 * unit, pieces[0])
    came = [swap(piece, 4 * k) for k, piece in enumerate(pieces, 1)]
    response = respond([here[:1], came_near, *came], (part0, part1), frf)

    shards = [response] + [swap(response, 4 * k) for k in range(1, zs)]
    own = jnp.stack(shards)
    over = swap(own, 2)
    cut = zs // 2
    twin = [swap(jnp.stack(half_shards), 1) for half_shards in (shards[:cut], shards[cut:])]
    plan = [(0, k, 0, k) for k in range(zs)]
    plan += [(1 + k // cut, k % cut, 1, k) for k in range(zs)]
    waves = inverse(place, inv, shapes_t, (own, *twin), plan)
    over, waves = lax.optimization_barrier((over, waves))
    plan = [(far, k, far, k) for far in range(CORES) for k in range(zs)]
    out = inverse(place, inv, shapes_t, (over, swap(over, 1)), plan, waves)
    return out.reshape(1, steps, dofs)


def solution(mesh):
    devices = mesh.shape["dof"]
    return jax.shard_map(
        functools.partial(on_device, devices),
        mesh=mesh,
        in_specs=(P("grp", None, "dof"), P("dof", None), P("dof", None, None, None)),
        out_specs=P("grp", None, "dof"),
        check_vma=False,
    )
```

```python
import functools
import math

import jax
import jax.numpy as jnp
import numpy as np
from jax import lax
from jax.experimental import pallas as pl
from jax.experimental.pallas import tpu as pltpu
from jax.sharding import PartitionSpec as P

FREQS = 512
CORES = 2
MIB = 1 << 20


def frequency_order(chips, parity):
    mine = FREQS // (chips * CORES)
    owned = np.arange(FREQS).reshape(chips // 2, 2, CORES, mine // 2, 2)
    return owned[..., parity].transpose(1, 2, 0, 3).reshape(-1)


def forward_tables(steps, chips):
    times = np.arange(steps // 2, dtype=np.int64)
    tables = []
    for parity in range(2):
        ids = frequency_order(chips, parity)
        angle = (ids[:, None] * times[None, :] % steps) * (2.0 * math.pi / steps)
        table = np.stack([np.cos(angle), -np.sin(angle)], axis=1) / math.sqrt(steps)
        tables.append(table.reshape(FREQS, steps // 2))
    return np.stack(tables)


def inverse_tables(steps, chips):
    tables = forward_tables(steps, chips) * 2.0
    for parity in range(2):
        weights = np.where(frequency_order(chips, parity) == 0, 0.5, 1.0)
        tables[parity] *= np.repeat(weights, 2)[:, None]
    return tables.reshape(2, 2, FREQS // 2, steps // 2).transpose(0, 1, 3, 2)


def chunk_list(half):
    unit = half // 8
    sizes = (unit, unit, 2 * unit, 2 * unit, 2 * unit)
    return tuple((sum(sizes[:n]), size) for n, size in enumerate(sizes))


def forward_kernel(
    place_ref, table_ref, forces_ref, shapes_ref, keep_ref, send_ref,
    table_buf, forces_buf, shapes_buf, acc_ref, table_sem, forces_sem, shapes_sem,
):
    _, zs, _, rows, modes = keep_ref.shape
    chunks = chunk_list(forces_ref.shape[1])
    copies = []
    for n, (start, size) in enumerate(chunks):
        part = pl.ds(start, size)
        pair = (
            pltpu.make_async_copy(
                forces_ref.at[:, part], forces_buf.at[:, part], forces_sem.at[n]
            ),
            pltpu.make_async_copy(
                table_ref.at[:, :, part], table_buf.at[:, :, part], table_sem.at[n]
            ),
        )
        for copy in pair:
            copy.start()
        copies.append(pair)
    shapes_copy = pltpu.make_async_copy(shapes_ref, shapes_buf, shapes_sem)
    shapes_copy.start()

    for n, (start, size) in enumerate(chunks):
        for copy in copies[n]:
            copy.wait()
        low = forces_buf[0, start : start + size]
        high = forces_buf[1, start : start + size]
        for parity, folded in enumerate((low + high, low - high)):
            part = jnp.dot(
                table_buf[parity, :, start : start + size],
                folded,
                preferred_element_type=jnp.float32,
            )
            if n == 0:
                acc_ref[parity] = part
            else:
                acc_ref[parity] += part

    shapes_copy.wait()
    first, chip = place_ref[0] == 0, place_ref[1]
    for parity in range(2):
        spec = lax.dot_general(
            acc_ref[parity].astype(jnp.bfloat16),
            shapes_buf[...],
            (((1,), (1,)), ((), ())),
            preferred_element_type=jnp.float32,
        ).reshape(2, CORES, zs, rows, modes)
        for y in range(2):
            keep = jnp.where(first, spec[y, 0], spec[y, 1]).astype(jnp.bfloat16)
            send = jnp.where(first, spec[y, 1], spec[y, 0]).astype(jnp.bfloat16)
            for z in range(zs):
                slot = chip ^ (2 * z + y)
                keep_ref[slot % 2, slot // 2, parity] = keep[z]
                send_ref[slot % 2, slot // 2, parity] = send[z]


def in_hbm(array):
    return pltpu.with_memory_space_constraint(array, pltpu.HBM)


def forward(place, table, forces, shapes_t, chips):
    _, half, dofs = forces.shape
    modes = shapes_t.shape[0]
    rows = FREQS // (chips * CORES)
    out = jax.ShapeDtypeStruct((2, chips // 2, 2, rows, modes), jnp.bfloat16)
    vmem, hbm = pl.BlockSpec(memory_space=pltpu.VMEM), pl.BlockSpec(memory_space=pltpu.HBM)
    count = len(chunk_list(half))
    return pl.pallas_call(
        forward_kernel,
        in_specs=[pl.BlockSpec(memory_space=pltpu.SMEM), hbm, hbm, hbm],
        out_specs=[vmem, vmem],
        out_shape=[out, out],
        scratch_shapes=[
            pltpu.VMEM(table.shape, jnp.bfloat16),
            pltpu.VMEM(forces.shape, jnp.bfloat16),
            pltpu.VMEM(shapes_t.shape, jnp.bfloat16),
            pltpu.VMEM((2, FREQS, dofs), jnp.float32),
            pltpu.SemaphoreType.DMA((count,)),
            pltpu.SemaphoreType.DMA((count,)),
            pltpu.SemaphoreType.DMA,
        ],
        compiler_params=pltpu.CompilerParams(vmem_limit_bytes=24 * MIB),
        cost_estimate=pl.CostEstimate(
            flops=4 * FREQS * dofs * (half + modes), bytes_accessed=12 * MIB, transcendentals=0
        ),
        name="forward",
    )(place, in_hbm(table), in_hbm(forces), in_hbm(shapes_t))


def load_copies(start, frf_ref, held_ref, sem):
    count = sem.shape[0]
    size = held_ref.shape[0] // count
    return [
        pltpu.make_async_copy(
            frf_ref.at[pl.ds(start + n * size, size)],
            held_ref.at[pl.ds(n * size, size)],
            sem.at[n],
        )
        for n in range(count)
    ]


def load_kernel(start, frf_ref, after_ref, held_ref, sem):
    copies = load_copies(start, frf_ref, held_ref, sem)
    for copy in copies:
        copy.start()
    for copy in copies:
        copy.wait()


def load(frf, start, size, after):
    hbm, anywhere = pl.BlockSpec(memory_space=pltpu.HBM), pl.BlockSpec(memory_space=pl.ANY)
    return pl.pallas_call(
        functools.partial(load_kernel, start),
        in_specs=[hbm, anywhere],
        out_specs=pl.BlockSpec(memory_space=pltpu.VMEM),
        out_shape=pltpu.VMEM((size,) + frf.shape[1:], jnp.bfloat16),
        scratch_shapes=[pltpu.SemaphoreType.DMA((math.gcd(size, 4),))],
        compiler_params=pltpu.CompilerParams(vmem_limit_bytes=2 * MIB),
        cost_estimate=pl.CostEstimate(
            flops=0, bytes_accessed=4 * size * math.prod(frf.shape[1:]), transcendentals=0
        ),
        name="load",
    )(in_hbm(frf), after)


def respond_kernel(count, *refs):
    pieces, parts = refs[:count], refs[count:-7]
    frf_ref, out_ref, direct_ref, turned_ref, result_ref, rest_ref, sem = refs[-7:]
    held = sum(part.shape[0] for part in parts)
    copies = load_copies(held, frf_ref, rest_ref, sem)
    for copy in copies:
        copy.start()
    _, rows, modes = out_ref.shape
    total = sum(piece[0].astype(jnp.float32) for piece in pieces).reshape(2 * rows, modes)
    total = total.astype(jnp.bfloat16).astype(jnp.float32)
    row = lax.broadcasted_iota(jnp.int32, total.shape, 0)
    turned = jnp.where(row % 2 == 0, -jnp.roll(total, -1, axis=0), jnp.roll(total, 1, axis=0))

    def place(f):
        return (f % 2) * rows + f // 2 * 2

    direct_ref[...] = jnp.zeros_like(direct_ref)
    turned_ref[...] = jnp.zeros_like(turned_ref)
    for f in range(rows):
        at = place(f)
        direct_ref[f, 0:2] = total[at : at + 2]
        turned_ref[f, 0:2] = turned[at : at + 2]

    def multiply(matrix_ref, step, f):
        products = [
            lax.dot_general(
                ref[f].astype(jnp.bfloat16),
                matrix_ref[step, which],
                (((1,), (1,)), ((), ())),
                preferred_element_type=jnp.float32,
            )
            for which, ref in enumerate((direct_ref, turned_ref))
        ]
        result_ref[f] = products[0] + products[1]

    base = 0
    for part in parts:

        @pl.loop(0, part.shape[0], unroll=math.gcd(4, part.shape[0]))
        def _(step, part=part, base=base):
            multiply(part, step, base + step)

        base += part.shape[0]

    for copy in copies:
        copy.wait()

    @pl.loop(0, rest_ref.shape[0], unroll=math.gcd(4, rest_ref.shape[0]))
    def _(step):
        multiply(rest_ref, step, held + step)

    for f in range(rows):
        at = place(f)
        direct_ref[at // 8, at % 8 : at % 8 + 2] = result_ref[f, 0:2]
    out_ref[...] = (
        direct_ref[: 2 * rows // 8].reshape(2, rows, modes).astype(jnp.bfloat16)
    )


def respond(pieces, parts, frf):
    rows, modes = pieces[0].shape[2:]
    vmem, hbm = pl.BlockSpec(memory_space=pltpu.VMEM), pl.BlockSpec(memory_space=pltpu.HBM)
    rest = frf.shape[0] - sum(part.shape[0] for part in parts)
    return pl.pallas_call(
        functools.partial(respond_kernel, len(pieces)),
        in_specs=[vmem] * (len(pieces) + len(parts)) + [hbm],
        out_specs=vmem,
        out_shape=jax.ShapeDtypeStruct((2, rows, modes), jnp.bfloat16),
        scratch_shapes=[pltpu.VMEM((rows, 8, modes), jnp.float32)] * 3
        + [
            pltpu.VMEM((rest,) + frf.shape[1:], jnp.bfloat16),
            pltpu.SemaphoreType.DMA((rest // math.gcd(rest, 4),)),
        ],
        compiler_params=pltpu.CompilerParams(vmem_limit_bytes=16 * MIB),
        cost_estimate=pl.CostEstimate(
            flops=4 * frf.size, bytes_accessed=2 * frf.size, transcendentals=0
        ),
        name="respond",
    )(*pieces, *parts, in_hbm(frf))


def project(place_ref, slots, shapes_ref, order_ref, moved_ref):
    _, _, zs, rows, modes = order_ref.shape
    core, z = place_ref[0], place_ref[1] // 2
    for shard_ref, n, far, k in slots:
        for parity in range(2):
            order_ref[parity, core ^ far, z ^ k] = shard_ref[n, parity].astype(jnp.float32)
    for parity in range(2):
        moved_ref[parity] = jnp.dot(
            order_ref[parity].reshape(FREQS // 2, modes).astype(jnp.bfloat16),
            shapes_ref[...],
            preferred_element_type=jnp.float32,
        ).astype(jnp.bfloat16)


def named_slots(plan, shards):
    return [(shards[which], n, far, k) for which, n, far, k in plan]


def early_kernel(plan, place_ref, table_ref, shapes_ref, *refs):
    shards, (waves_ref, order_ref, moved_ref) = refs[:-3], refs[-3:]
    project(place_ref, named_slots(plan, shards), shapes_ref, order_ref, moved_ref)
    y = place_ref[1] % 2
    block = waves_ref.shape[1] // 4
    for step in range(4):
        part = slice(step * block, (step + 1) * block)
        for parity in range(2):
            waves_ref[parity, part] = jnp.dot(
                table_ref[parity, y, part], moved_ref[parity], preferred_element_type=jnp.float32
            )


def late_kernel(plan, place_ref, table_ref, shapes_ref, *refs):
    shards, (waves_ref, out_ref, order_ref, moved_ref, out_buf, out_sem) = refs[:-6], refs[-6:]
    project(place_ref, named_slots(plan, shards), shapes_ref, order_ref, moved_ref)
    y = (place_ref[1] % 2) ^ 1
    count = out_sem.shape[0]
    block = out_ref.shape[1] // count

    def copy_out(step):
        part = pl.ds(step * block, block)
        return pltpu.make_async_copy(
            out_buf.at[:, part], out_ref.at[:, part], out_sem.at[step]
        )

    for step in range(count):
        part = slice(step * block, (step + 1) * block)
        even, odd = (
            waves_ref[parity, part]
            + jnp.dot(
                table_ref[parity, y, part], moved_ref[parity], preferred_element_type=jnp.float32
            )
            for parity in range(2)
        )
        out_buf[0, part] = (even + odd).astype(jnp.bfloat16)
        out_buf[1, part] = (even - odd).astype(jnp.bfloat16)
        copy_out(step).start()
    for step in range(count):
        copy_out(step).wait()


def inverse(place, table, shapes_t, shards, plan, waves=None):
    half = table.shape[2]
    modes, dofs = shapes_t.shape
    rows = shards[0].shape[2]
    zs = len(plan) // 2
    vmem = pl.BlockSpec(memory_space=pltpu.VMEM)
    scratch = [
        pltpu.VMEM((2, CORES, zs, rows, modes), jnp.float32),
        pltpu.VMEM((2, FREQS // 2, dofs), jnp.bfloat16),
    ]
    given = (place, table, shapes_t) + shards
    in_specs = [pl.BlockSpec(memory_space=pltpu.SMEM)] + [vmem] * (len(given) - 1)
    params = pltpu.CompilerParams(vmem_limit_bytes=20 * MIB)
    cost = pl.CostEstimate(
        flops=2 * FREQS * dofs * (half + modes), bytes_accessed=8 * MIB, transcendentals=0
    )
    if waves is None:
        return pl.pallas_call(
            functools.partial(early_kernel, plan),
            in_specs=in_specs,
            out_specs=vmem,
            out_shape=pltpu.VMEM((2, half, dofs), jnp.float32),
            scratch_shapes=scratch,
            compiler_params=params,
            cost_estimate=pl.CostEstimate(flops=1000, bytes_accessed=1000, transcendentals=0),
            name="early",
        )(*given)
    return pl.pallas_call(
        functools.partial(late_kernel, plan),
        in_specs=in_specs + [vmem],
        out_specs=pl.BlockSpec(memory_space=pltpu.HBM),
        out_shape=jax.ShapeDtypeStruct((2, half, dofs), jnp.bfloat16),
        scratch_shapes=scratch
        + [pltpu.VMEM((2, half, dofs), jnp.bfloat16), pltpu.SemaphoreType.DMA((8,))],
        compiler_params=params,
        cost_estimate=cost,
        name="late",
    )(*given, waves)


def add_kernel(start, splits, ours_ref, came_ref, after_ref, *out_refs):
    at = 0
    for size, out_ref in zip(splits, out_refs):
        for n in range(size):
            total = ours_ref[start + at + n].astype(jnp.float32) + came_ref[at + n].astype(
                jnp.float32
            )
            out_ref[n] = total.astype(jnp.bfloat16)
        at += size


def add(ours, came, start, splits, after):
    vmem, anywhere = pl.BlockSpec(memory_space=pltpu.VMEM), pl.BlockSpec(memory_space=pl.ANY)
    return pl.pallas_call(
        functools.partial(add_kernel, start, splits),
        in_specs=[vmem, vmem, anywhere],
        out_specs=[vmem] * len(splits),
        out_shape=[
            jax.ShapeDtypeStruct((size,) + ours.shape[1:], jnp.bfloat16) for size in splits
        ],
        compiler_params=pltpu.CompilerParams(vmem_limit_bytes=8 * MIB),
        cost_estimate=pl.CostEstimate(
            flops=came.size, bytes_accessed=6 * came.size, transcendentals=0
        ),
        name="add",
    )(ours, came, after)


def on_device(devices, forces, mode_shapes, frf):
    _, steps, dofs = forces.shape
    half = steps // 2
    chips = devices // CORES
    zs = chips // 2

    def swap(values, distance):
        pairs = [(i, i ^ distance) for i in range(devices)]
        return lax.ppermute(values, "dof", pairs)

    index = lax.axis_index("dof")
    place = jnp.stack([index % CORES, index // CORES]).astype(jnp.int32)
    shapes_t = mode_shapes.T
    fwd = jnp.asarray(forward_tables(steps, chips).astype(jnp.bfloat16))
    inv = jnp.asarray(inverse_tables(steps, chips).astype(jnp.bfloat16))

    unit = frf.shape[0] // 8
    keep, send = forward(place, fwd, forces.reshape(2, half, dofs), shapes_t, chips)
    slots = (2 * zs,) + keep.shape[2:]
    here, there_near, there_far = add(
        keep.reshape(slots), swap(send, 1).reshape(slots), 0, (zs, 1, zs - 1), send
    )
    came_far, came_near = swap(there_far, 2), swap(there_near, 2)
    part0 = load(frf, 0, 3 * unit, there_far)
    pieces = add(here, came_far, 1, (1,) * (zs - 1), part0)
    part1 = load(frf, 3 * unit, 2 * unit, pieces[0])
    came = [swap(piece, 4 * k) for k, piece in enumerate(pieces, 1)]
    response = respond([here[:1], came_near, *came], (part0, part1), frf)

    shards = [response] + [swap(response, 4 * k) for k in range(1, zs)]
    own = jnp.stack(shards)
    over = swap(own, 2)
    cut = zs // 2
    twin = [swap(jnp.stack(half_shards), 1) for half_shards in (shards[:cut], shards[cut:])]
    plan = [(0, k, 0, k) for k in range(zs)]
    plan += [(1 + k // cut, k % cut, 1, k) for k in range(zs)]
    waves = inverse(place, inv, shapes_t, (own, *twin), plan)
    over, waves = lax.optimization_barrier((over, waves))
    plan = [(far, k, far, k) for far in range(CORES) for k in range(zs)]
    out = inverse(place, inv, shapes_t, (over, swap(over, 1)), plan, waves)
    return out.reshape(1, steps, dofs)


def solution(mesh):
    devices = mesh.shape["dof"]
    return jax.shard_map(
        functools.partial(on_device, devices),
        mesh=mesh,
        in_specs=(P("grp", None, "dof"), P("dof", None), P("dof", None, None, None)),
        out_specs=P("grp", None, "dof"),
        check_vma=False,
    )
```

```python
import functools
import math

import jax
import jax.numpy as jnp
import numpy as np
from jax import lax
from jax.experimental import pallas as pl
from jax.experimental.pallas import tpu as pltpu
from jax.sharding import PartitionSpec as P

FREQS = 512
CORES = 2
MIB = 1 << 20


def frequency_order(chips, parity):
    mine = FREQS // (chips * CORES)
    owned = np.arange(FREQS).reshape(chips // 2, 2, CORES, mine // 2, 2)
    return owned[..., parity].transpose(1, 2, 0, 3).reshape(-1)


def forward_tables(steps, chips):
    times = np.arange(steps // 2, dtype=np.int64)
    tables = []
    for parity in range(2):
        ids = frequency_order(chips, parity)
        angle = (ids[:, None] * times[None, :] % steps) * (2.0 * math.pi / steps)
        table = np.stack([np.cos(angle), -np.sin(angle)], axis=1) / math.sqrt(steps)
        tables.append(table.reshape(FREQS, steps // 2))
    return np.stack(tables)


def inverse_tables(steps, chips):
    tables = forward_tables(steps, chips) * 2.0
    for parity in range(2):
        weights = np.where(frequency_order(chips, parity) == 0, 0.5, 1.0)
        tables[parity] *= np.repeat(weights, 2)[:, None]
    return tables.reshape(2, 2, FREQS // 2, steps // 2).transpose(0, 1, 3, 2)


def chunk_list(half):
    unit = half // 8
    sizes = (unit, unit, 2 * unit, 2 * unit, 2 * unit)
    return tuple((sum(sizes[:n]), size) for n, size in enumerate(sizes))


def forward_kernel(
    place_ref, table_ref, forces_ref, shapes_ref, keep_ref, send_ref,
    table_buf, forces_buf, shapes_buf, acc_ref, table_sem, forces_sem, shapes_sem,
):
    _, zs, _, rows, modes = keep_ref.shape
    chunks = chunk_list(forces_ref.shape[1])
    copies = []
    for n, (start, size) in enumerate(chunks):
        part = pl.ds(start, size)
        pair = (
            pltpu.make_async_copy(
                forces_ref.at[:, part], forces_buf.at[:, part], forces_sem.at[n]
            ),
            pltpu.make_async_copy(
                table_ref.at[:, :, part], table_buf.at[:, :, part], table_sem.at[n]
            ),
        )
        for copy in pair:
            copy.start()
        copies.append(pair)
    shapes_copy = pltpu.make_async_copy(shapes_ref, shapes_buf, shapes_sem)
    shapes_copy.start()

    for n, (start, size) in enumerate(chunks):
        for copy in copies[n]:
            copy.wait()
        low = forces_buf[0, start : start + size]
        high = forces_buf[1, start : start + size]
        for parity, folded in enumerate((low + high, low - high)):
            part = jnp.dot(
                table_buf[parity, :, start : start + size],
                folded,
                preferred_element_type=jnp.float32,
            )
            if n == 0:
                acc_ref[parity] = part
            else:
                acc_ref[parity] += part

    shapes_copy.wait()
    first, chip = place_ref[0] == 0, place_ref[1]
    for parity in range(2):
        spec = lax.dot_general(
            acc_ref[parity].astype(jnp.bfloat16),
            shapes_buf[...],
            (((1,), (1,)), ((), ())),
            preferred_element_type=jnp.float32,
        ).reshape(2, CORES, zs, rows, modes)
        for y in range(2):
            keep = jnp.where(first, spec[y, 0], spec[y, 1]).astype(jnp.bfloat16)
            send = jnp.where(first, spec[y, 1], spec[y, 0]).astype(jnp.bfloat16)
            for z in range(zs):
                slot = chip ^ (2 * z + y)
                keep_ref[slot % 2, slot // 2, parity] = keep[z]
                send_ref[slot % 2, slot // 2, parity] = send[z]


def in_hbm(array):
    return pltpu.with_memory_space_constraint(array, pltpu.HBM)


def forward(place, table, forces, shapes_t, chips):
    _, half, dofs = forces.shape
    modes = shapes_t.shape[0]
    rows = FREQS // (chips * CORES)
    out = jax.ShapeDtypeStruct((2, chips // 2, 2, rows, modes), jnp.bfloat16)
    vmem, hbm = pl.BlockSpec(memory_space=pltpu.VMEM), pl.BlockSpec(memory_space=pltpu.HBM)
    count = len(chunk_list(half))
    return pl.pallas_call(
        forward_kernel,
        in_specs=[pl.BlockSpec(memory_space=pltpu.SMEM), hbm, hbm, hbm],
        out_specs=[vmem, vmem],
        out_shape=[out, out],
        scratch_shapes=[
            pltpu.VMEM(table.shape, jnp.bfloat16),
            pltpu.VMEM(forces.shape, jnp.bfloat16),
            pltpu.VMEM(shapes_t.shape, jnp.bfloat16),
            pltpu.VMEM((2, FREQS, dofs), jnp.float32),
            pltpu.SemaphoreType.DMA((count,)),
            pltpu.SemaphoreType.DMA((count,)),
            pltpu.SemaphoreType.DMA,
        ],
        compiler_params=pltpu.CompilerParams(vmem_limit_bytes=24 * MIB),
        cost_estimate=pl.CostEstimate(
            flops=4 * FREQS * dofs * (half + modes), bytes_accessed=12 * MIB, transcendentals=0
        ),
        name="forward",
    )(place, in_hbm(table), in_hbm(forces), in_hbm(shapes_t))


def load_copies(start, frf_ref, held_ref, sem):
    count = sem.shape[0]
    size = held_ref.shape[0] // count
    return [
        pltpu.make_async_copy(
            frf_ref.at[pl.ds(start + n * size, size)],
            held_ref.at[pl.ds(n * size, size)],
            sem.at[n],
        )
        for n in range(count)
    ]


def load_kernel(start, frf_ref, after_ref, held_ref, sem):
    copies = load_copies(start, frf_ref, held_ref, sem)
    for copy in copies:
        copy.start()
    for copy in copies:
        copy.wait()


def load(frf, start, size, after):
    hbm, anywhere = pl.BlockSpec(memory_space=pltpu.HBM), pl.BlockSpec(memory_space=pl.ANY)
    return pl.pallas_call(
        functools.partial(load_kernel, start),
        in_specs=[hbm, anywhere],
        out_specs=pl.BlockSpec(memory_space=pltpu.VMEM),
        out_shape=pltpu.VMEM((size,) + frf.shape[1:], jnp.bfloat16),
        scratch_shapes=[pltpu.SemaphoreType.DMA((math.gcd(size, 4),))],
        compiler_params=pltpu.CompilerParams(vmem_limit_bytes=2 * MIB),
        cost_estimate=pl.CostEstimate(
            flops=0, bytes_accessed=4 * size * math.prod(frf.shape[1:]), transcendentals=0
        ),
        name="load",
    )(in_hbm(frf), after)


def respond_kernel(count, *refs):
    pieces, parts = refs[:count], refs[count:-7]
    frf_ref, out_ref, direct_ref, turned_ref, result_ref, rest_ref, sem = refs[-7:]
    held = sum(part.shape[0] for part in parts)
    copies = load_copies(held, frf_ref, rest_ref, sem)
    for copy in copies:
        copy.start()
    _, rows, modes = out_ref.shape
    total = sum(piece[0].astype(jnp.float32) for piece in pieces).reshape(2 * rows, modes)
    total = total.astype(jnp.bfloat16).astype(jnp.float32)
    row = lax.broadcasted_iota(jnp.int32, total.shape, 0)
    turned = jnp.where(row % 2 == 0, -jnp.roll(total, -1, axis=0), jnp.roll(total, 1, axis=0))

    def place(f):
        return (f % 2) * rows + f // 2 * 2

    direct_ref[...] = jnp.zeros_like(direct_ref)
    turned_ref[...] = jnp.zeros_like(turned_ref)
    for f in range(rows):
        at = place(f)
        direct_ref[f, 0:2] = total[at : at + 2]
        turned_ref[f, 0:2] = turned[at : at + 2]

    def multiply(matrix_ref, step, f):
        products = [
            lax.dot_general(
                ref[f].astype(jnp.bfloat16),
                matrix_ref[step, which],
                (((1,), (1,)), ((), ())),
                preferred_element_type=jnp.float32,
            )
            for which, ref in enumerate((direct_ref, turned_ref))
        ]
        result_ref[f] = products[0] + products[1]

    base = 0
    for part in parts:

        @pl.loop(0, part.shape[0], unroll=math.gcd(2, part.shape[0]))
        def _(step, part=part, base=base):
            multiply(part, step, base + step)

        base += part.shape[0]

    for copy in copies:
        copy.wait()

    @pl.loop(0, rest_ref.shape[0], unroll=math.gcd(2, rest_ref.shape[0]))
    def _(step):
        multiply(rest_ref, step, held + step)

    for f in range(rows):
        at = place(f)
        direct_ref[at // 8, at % 8 : at % 8 + 2] = result_ref[f, 0:2]
    out_ref[...] = (
        direct_ref[: 2 * rows // 8].reshape(2, rows, modes).astype(jnp.bfloat16)
    )


def respond(pieces, parts, frf):
    rows, modes = pieces[0].shape[2:]
    vmem, hbm = pl.BlockSpec(memory_space=pltpu.VMEM), pl.BlockSpec(memory_space=pltpu.HBM)
    rest = frf.shape[0] - sum(part.shape[0] for part in parts)
    return pl.pallas_call(
        functools.partial(respond_kernel, len(pieces)),
        in_specs=[vmem] * (len(pieces) + len(parts)) + [hbm],
        out_specs=vmem,
        out_shape=jax.ShapeDtypeStruct((2, rows, modes), jnp.bfloat16),
        scratch_shapes=[pltpu.VMEM((rows, 8, modes), jnp.float32)] * 3
        + [
            pltpu.VMEM((rest,) + frf.shape[1:], jnp.bfloat16),
            pltpu.SemaphoreType.DMA((rest // math.gcd(rest, 4),)),
        ],
        compiler_params=pltpu.CompilerParams(vmem_limit_bytes=16 * MIB),
        cost_estimate=pl.CostEstimate(
            flops=4 * frf.size, bytes_accessed=2 * frf.size, transcendentals=0
        ),
        name="respond",
    )(*pieces, *parts, in_hbm(frf))


def project(place_ref, slots, shapes_ref, order_ref, moved_ref):
    _, _, zs, rows, modes = order_ref.shape
    core, z = place_ref[0], place_ref[1] // 2
    for shard_ref, n, far, k in slots:
        for parity in range(2):
            order_ref[parity, core ^ far, z ^ k] = shard_ref[n, parity].astype(jnp.float32)
    for parity in range(2):
        moved_ref[parity] = jnp.dot(
            order_ref[parity].reshape(FREQS // 2, modes).astype(jnp.bfloat16),
            shapes_ref[...],
            preferred_element_type=jnp.float32,
        ).astype(jnp.bfloat16)


def named_slots(plan, shards):
    return [(shards[which], n, far, k) for which, n, far, k in plan]


def early_kernel(plan, place_ref, table_ref, shapes_ref, *refs):
    shards, (waves_ref, order_ref, moved_ref) = refs[:-3], refs[-3:]
    project(place_ref, named_slots(plan, shards), shapes_ref, order_ref, moved_ref)
    y = place_ref[1] % 2
    block = waves_ref.shape[1] // 4
    for step in range(4):
        part = slice(step * block, (step + 1) * block)
        for parity in range(2):
            waves_ref[parity, part] = jnp.dot(
                table_ref[parity, y, part], moved_ref[parity], preferred_element_type=jnp.float32
            )


def late_kernel(plan, place_ref, table_ref, shapes_ref, *refs):
    shards, (waves_ref, out_ref, order_ref, moved_ref, out_buf, out_sem) = refs[:-6], refs[-6:]
    project(place_ref, named_slots(plan, shards), shapes_ref, order_ref, moved_ref)
    y = (place_ref[1] % 2) ^ 1
    count = out_sem.shape[0]
    block = out_ref.shape[1] // count

    def copy_out(step):
        part = pl.ds(step * block, block)
        return pltpu.make_async_copy(
            out_buf.at[:, part], out_ref.at[:, part], out_sem.at[step]
        )

    for step in range(count):
        part = slice(step * block, (step + 1) * block)
        even, odd = (
            waves_ref[parity, part]
            + jnp.dot(
                table_ref[parity, y, part], moved_ref[parity], preferred_element_type=jnp.float32
            )
            for parity in range(2)
        )
        out_buf[0, part] = (even + odd).astype(jnp.bfloat16)
        out_buf[1, part] = (even - odd).astype(jnp.bfloat16)
        copy_out(step).start()
    for step in range(count):
        copy_out(step).wait()


def inverse(place, table, shapes_t, shards, plan, waves=None):
    half = table.shape[2]
    modes, dofs = shapes_t.shape
    rows = shards[0].shape[2]
    zs = len(plan) // 2
    vmem = pl.BlockSpec(memory_space=pltpu.VMEM)
    scratch = [
        pltpu.VMEM((2, CORES, zs, rows, modes), jnp.float32),
        pltpu.VMEM((2, FREQS // 2, dofs), jnp.bfloat16),
    ]
    given = (place, table, shapes_t) + shards
    in_specs = [pl.BlockSpec(memory_space=pltpu.SMEM)] + [vmem] * (len(given) - 1)
    params = pltpu.CompilerParams(vmem_limit_bytes=20 * MIB)
    cost = pl.CostEstimate(
        flops=2 * FREQS * dofs * (half + modes), bytes_accessed=8 * MIB, transcendentals=0
    )
    if waves is None:
        return pl.pallas_call(
            functools.partial(early_kernel, plan),
            in_specs=in_specs,
            out_specs=vmem,
            out_shape=pltpu.VMEM((2, half, dofs), jnp.float32),
            scratch_shapes=scratch,
            compiler_params=params,
            cost_estimate=pl.CostEstimate(flops=1000, bytes_accessed=1000, transcendentals=0),
            name="early",
        )(*given)
    return pl.pallas_call(
        functools.partial(late_kernel, plan),
        in_specs=in_specs + [vmem],
        out_specs=pl.BlockSpec(memory_space=pltpu.HBM),
        out_shape=jax.ShapeDtypeStruct((2, half, dofs), jnp.bfloat16),
        scratch_shapes=scratch
        + [pltpu.VMEM((2, half, dofs), jnp.bfloat16), pltpu.SemaphoreType.DMA((8,))],
        compiler_params=params,
        cost_estimate=cost,
        name="late",
    )(*given, waves)


def add_kernel(start, splits, ours_ref, came_ref, after_ref, *out_refs):
    at = 0
    for size, out_ref in zip(splits, out_refs):
        for n in range(size):
            total = ours_ref[start + at + n].astype(jnp.float32) + came_ref[at + n].astype(
                jnp.float32
            )
            out_ref[n] = total.astype(jnp.bfloat16)
        at += size


def add(ours, came, start, splits, after):
    vmem, anywhere = pl.BlockSpec(memory_space=pltpu.VMEM), pl.BlockSpec(memory_space=pl.ANY)
    return pl.pallas_call(
        functools.partial(add_kernel, start, splits),
        in_specs=[vmem, vmem, anywhere],
        out_specs=[vmem] * len(splits),
        out_shape=[
            jax.ShapeDtypeStruct((size,) + ours.shape[1:], jnp.bfloat16) for size in splits
        ],
        compiler_params=pltpu.CompilerParams(vmem_limit_bytes=8 * MIB),
        cost_estimate=pl.CostEstimate(
            flops=came.size, bytes_accessed=6 * came.size, transcendentals=0
        ),
        name="add",
    )(ours, came, after)


def on_device(devices, forces, mode_shapes, frf):
    _, steps, dofs = forces.shape
    half = steps // 2
    chips = devices // CORES
    zs = chips // 2

    def swap(values, distance):
        pairs = [(i, i ^ distance) for i in range(devices)]
        return lax.ppermute(values, "dof", pairs)

    index = lax.axis_index("dof")
    place = jnp.stack([index % CORES, index // CORES]).astype(jnp.int32)
    shapes_t = mode_shapes.T
    fwd = jnp.asarray(forward_tables(steps, chips).astype(jnp.bfloat16))
    inv = jnp.asarray(inverse_tables(steps, chips).astype(jnp.bfloat16))

    unit = frf.shape[0] // 8
    keep, send = forward(place, fwd, forces.reshape(2, half, dofs), shapes_t, chips)
    slots = (2 * zs,) + keep.shape[2:]
    here, there_near, there_far = add(
        keep.reshape(slots), swap(send, 1).reshape(slots), 0, (zs, 1, zs - 1), send
    )
    came_far, came_near = swap(there_far, 2), swap(there_near, 2)
    part0 = load(frf, 0, 3 * unit, there_far)
    pieces = add(here, came_far, 1, (1,) * (zs - 1), part0)
    part1 = load(frf, 3 * unit, 2 * unit, pieces[0])
    came = [swap(piece, 4 * k) for k, piece in enumerate(pieces, 1)]
    response = respond([here[:1], came_near, *came], (part0, part1), frf)

    shards = [response] + [swap(response, 4 * k) for k in range(1, zs)]
    own = jnp.stack(shards)
    over = swap(own, 2)
    cut = zs // 2
    twin = [swap(jnp.stack(half_shards), 1) for half_shards in (shards[:cut], shards[cut:])]
    plan = [(0, k, 0, k) for k in range(zs)]
    plan += [(1 + k // cut, k % cut, 1, k) for k in range(zs)]
    waves = inverse(place, inv, shapes_t, (own, *twin), plan)
    over, waves = lax.optimization_barrier((over, waves))
    plan = [(far, k, far, k) for far in range(CORES) for k in range(zs)]
    out = inverse(place, inv, shapes_t, (over, swap(over, 1)), plan, waves)
    return out.reshape(1, steps, dofs)


def solution(mesh):
    devices = mesh.shape["dof"]
    return jax.shard_map(
        functools.partial(on_device, devices),
        mesh=mesh,
        in_specs=(P("grp", None, "dof"), P("dof", None), P("dof", None, None, None)),
        out_specs=P("grp", None, "dof"),
        check_vma=False,
    )
```
